32 devices in a mesh: dp: 8 (over z, y), mp: 4 (over x, core).
Axes of the slice: x: 2, y: 2, z: 4, core: 2. Of those that a mesh axis runs over, the one named last changes fastest.
Arguments:
- images: bfloat16 [48, 3072], P('dp'), may hold values from -1 to 1
- noises: bfloat16 [3, 16, 3072], P(None, 'dp'), may hold values from -6 to 6
- order: int32 [48], P('dp'), may hold values from 0 to 5, as said below
- time_index: int32 [3, 16], P(None, 'dp'), may hold values from 0 to 999
- io_weight: float32 [6144], P(('mp', 'dp')), may hold values from -0.875 to 0.875
- conv_weight: float32 [4, 9, 256, 256], P(None, None, 'dp', 'mp'), may hold values from -0.125 to 0.125
- time_weight: float32 [2, 256, 256], P(None, 'dp', 'mp'), may hold values from -0.375 to 0.375
- attn_weight: float32 [256, 4, 256], P('dp', None, 'mp'), may hold values from -0.375 to 0.375
- norm_param: float32 [3072], P(('mp', 'dp'))
- io_first: float32 [6144], P(('mp', 'dp')), may hold values from -0.00390625 to 0.00390625
- conv_first: float32 [4, 9, 256, 256], P(None, None, 'dp', 'mp'), may hold values from -0.00390625 to 0.00390625
- time_first: float32 [2, 256, 256], P(None, 'dp', 'mp'), may hold values from -0.00390625 to 0.00390625
- attn_first: float32 [256, 4, 256], P('dp', None, 'mp'), may hold values from -0.00390625 to 0.00390625
- norm_first: float32 [3072], P(('mp', 'dp')), may hold values from -0.015625 to 0.015625
- io_second: float32 [6144], P(('mp', 'dp')), may hold values from 3.6209215e-07 to 1.4483686e-06
- conv_second: float32 [4, 9, 256, 256], P(None, None, 'dp', 'mp'), may hold values from 3.6209215e-07 to 1.4483686e-06
- time_second: float32 [2, 256, 256], P(None, 'dp', 'mp'), may hold values from 3.6209215e-07 to 1.4483686e-06
- attn_second: float32 [256, 4, 256], P('dp', None, 'mp'), may hold values from 3.6209215e-07 to 1.4483686e-06
- norm_second: float32 [3072], P(('mp', 'dp')), may hold values from 5.7934744e-06 to 2.3173898e-05
- io_average: float32 [6144], P(('mp', 'dp')), may hold values from -0.875 to 0.875
- conv_average: float32 [4, 9, 256, 256], P(None, None, 'dp', 'mp'), may hold values from -0.125 to 0.125
- time_average: float32 [2, 256, 256], P(None, 'dp', 'mp'), may hold values from -0.375 to 0.375
- attn_average: float32 [256, 4, 256], P('dp', None, 'mp'), may hold values from -0.375 to 0.375
- norm_average: float32 [3072], P(('mp', 'dp'))
Outputs:
- io_new: float32 [6144], P(('mp', 'dp'))
- conv_new: float32 [4, 9, 256, 256], P(None, None, 'dp', 'mp')
- time_new: float32 [2, 256, 256], P(None, 'dp', 'mp')
- attn_new: float32 [256, 4, 256], P('dp', None, 'mp')
- norm_new: float32 [3072], P(('mp', 'dp'))
- io_first_new: float32 [6144], P(('mp', 'dp'))
- conv_first_new: float32 [4, 9, 256, 256], P(None, None, 'dp', 'mp')
- time_first_new: float32 [2, 256, 256], P(None, 'dp', 'mp')
- attn_first_new: float32 [256, 4, 256], P('dp', None, 'mp')
- norm_first_new: float32 [3072], P(('mp', 'dp'))
- io_second_new: float32 [6144], P(('mp', 'dp'))
- conv_second_new: float32 [4, 9, 256, 256], P(None, None, 'dp', 'mp')
- time_second_new: float32 [2, 256, 256], P(None, 'dp', 'mp')
- attn_second_new: float32 [256, 4, 256], P('dp', None, 'mp')
- norm_second_new: float32 [3072], P(('mp', 'dp'))
- io_average_new: float32 [6144], P(('mp', 'dp'))
- conv_average_new: float32 [4, 9, 256, 256], P(None, None, 'dp', 'mp')
- time_average_new: float32 [2, 256, 256], P(None, 'dp', 'mp')
- attn_average_new: float32 [256, 4, 256], P('dp', None, 'mp')
- norm_average_new: float32 [3072], P(('mp', 'dp'))
- loss_sums: float32 [3], replicated
- transport_cost: float32 [3], replicated
- grad_norm: float32 [], replicated
The draws below stay inside these ranges and needn't reach their ends.
Inputs may be any that keep to these rules, and one draw needn't show every extreme that they name: `order`: each aligned block of 6 entries is a permutation of 0 to 5.
All inputs are finite; a program needn't handle non-finite values.
Results may differ from the reference program's by a relative error of at most 0.0018.
The reference program's roundings to bfloat16 on the way count: a program that leaves them out, or rounds other values in their place, can miss the bound.
Values may be sent and summed in bfloat16 or wider, within the bound.
A program may use at most 128 MiB of HBM per device.

```python
import math
import jax
import jax.numpy as jnp
from jax import lax

CH = 256
GROUPS = 32
HEADS = 4
HD = 64
SUB = 12
POS = 256
IMG_DEV = 2
MB = 3
SINK = 10
NT = 1000
STEP = 5
BATCH = 16
TOTAL = 48


def draw_order(key, part):
    key = jax.random.fold_in(key, 11)
    blocks = TOTAL // (MB * IMG_DEV)
    keys = jax.random.split(key, blocks)

    def one_block(block_key):
        return jax.random.permutation(block_key, MB * IMG_DEV)
    return jax.vmap(one_block)(keys).reshape(-1).astype(jnp.int32)


def norm_values(key, spread):
    rising = 0.5 + jnp.arange(CH, dtype=jnp.float32)[:, None] / CH
    factor = jax.random.uniform(key, (CH, 12), jnp.float32, 1.0 - spread, 1.0 + spread)
    offsets = 0.3 * jax.random.normal(jax.random.fold_in(key, 1), (CH, 12), jnp.float32)
    column = jnp.arange(12) % 2
    table = jnp.where(column[None, :] == 0, rising * factor, offsets)
    return table.reshape(-1)


def draw_norm_param(key, part):
    key = jax.random.fold_in(key, 21)
    return norm_values(key, 0.2)


def draw_norm_average(key, part):
    key = jax.random.fold_in(key, 22)
    return norm_values(key, 0.2)


def set_ends(entries, own_key, least, largest):
    place = [jax.random.randint(jax.random.fold_in(own_key, axis), (), 0, length) for axis, length in enumerate(entries.shape)]
    widest = entries.shape.index(max(entries.shape))
    beside = place[:widest] + [(place[widest] + 1) % entries.shape[widest]] + place[widest + 1:]
    return entries.at[tuple(place)].set(least).at[tuple(beside)].set(largest)


def block_scale(key, extent, shards, smallest, high):
    level, own = 1.0, jax.random.fold_in(key, 6)
    for position, parts in shards:
        heights = jnp.exp(jax.random.uniform(jax.random.fold_in(own, position), (parts,), jnp.float32, smallest / len(shards), high / len(shards)))
        level = level * jnp.repeat(heights, extent[position] // parts).reshape([-1 if axis == position else 1 for axis in range(len(extent))])
    return level


def scatter_about(own_key, shape, scale, reach, cuts=(), kind=jnp.bfloat16):
    array = scale * jax.random.normal(own_key, shape, jnp.float32)
    if cuts:
        array = array * block_scale(own_key, shape, cuts, -0.22, 0.18)
    return jnp.clip(array, -reach, reach).astype(kind)


def setup_inputs(seed: int = 0) -> dict:
    key_list = jax.random.split(jax.random.key(seed), 25)
    images = jnp.clip(jax.random.uniform(key_list[0], (TOTAL, SUB * POS), jnp.float32, -1.0, 1.0) * block_scale(key_list[0], (TOTAL, SUB * POS), ((0, 8),), -0.4, 0.0), -1.0, 1.0).astype(jnp.bfloat16)
    noises = scatter_about(key_list[1], (MB, BATCH, SUB * POS), 1.0, 6.0, ((1, 8),))
    order = draw_order(jax.random.fold_in(key_list[24], 71), 0)
    time_index = set_ends(jax.random.randint(key_list[3], (MB, BATCH), 0, NT), jax.random.fold_in(key_list[3], 1), 0, NT - 1).astype(jnp.int32)
    io_weight = scatter_about(key_list[4], (CH * 2 * SUB,), 48 ** -0.5, 0.875, ((0, 32),), jnp.float32)
    conv_weight = scatter_about(key_list[5], (4, 9, CH, CH), (9 * CH) ** -0.5, 0.125, ((2, 8), (3, 4)), jnp.float32)
    time_weight = scatter_about(key_list[6], (2, CH, CH), CH ** -0.5, 0.375, ((1, 8), (2, 4)), jnp.float32)
    attn_weight = scatter_about(key_list[7], (CH, 4, CH), CH ** -0.5, 0.375, ((0, 8), (2, 4)), jnp.float32)
    norm_param = draw_norm_param(jax.random.fold_in(key_list[24], 71), 0)
    io_first = scatter_about(key_list[9], (CH * 2 * SUB,), ((42 * CH * CH + 36 * CH) ** -0.5), 0.00390625, ((0, 32),), jnp.float32)
    conv_first = scatter_about(key_list[10], (4, 9, CH, CH), ((42 * CH * CH + 36 * CH) ** -0.5), 0.00390625, ((2, 8), (3, 4)), jnp.float32)
    time_first = scatter_about(key_list[11], (2, CH, CH), ((42 * CH * CH + 36 * CH) ** -0.5), 0.00390625, ((1, 8), (2, 4)), jnp.float32)
    attn_first = scatter_about(key_list[12], (CH, 4, CH), ((42 * CH * CH + 36 * CH) ** -0.5), 0.00390625, ((0, 8), (2, 4)), jnp.float32)
    norm_first = scatter_about(key_list[13], (CH * 12,), (4 * (42 * CH * CH + 36 * CH) ** -0.5), 0.015625, ((0, 32),), jnp.float32)
    io_second = jnp.clip(jnp.exp(math.log(1.4483686072708224e-06) - 1.3862944 * jax.random.uniform(key_list[14], (CH * 2 * SUB,), jnp.float32) ** block_scale(key_list[14], (CH * 2 * SUB,), ((0, 32),), -0.2, 0.2)), 3.620921518177056e-07, 1.4483686072708224e-06)
    conv_second = jnp.clip(jnp.exp(math.log(1.4483686072708224e-06) - 1.3862944 * jax.random.uniform(key_list[15], (4, 9, CH, CH), jnp.float32) ** block_scale(key_list[15], (4, 9, CH, CH), ((2, 8), (3, 4)), -0.2, 0.2)), 3.620921518177056e-07, 1.4483686072708224e-06)
    time_second = jnp.clip(jnp.exp(math.log(1.4483686072708224e-06) - 1.3862944 * jax.random.uniform(key_list[16], (2, CH, CH), jnp.float32) ** block_scale(key_list[16], (2, CH, CH), ((1, 8), (2, 4)), -0.2, 0.2)), 3.620921518177056e-07, 1.4483686072708224e-06)
    attn_second = jnp.clip(jnp.exp(math.log(1.4483686072708224e-06) - 1.3862944 * jax.random.uniform(key_list[17], (CH, 4, CH), jnp.float32) ** block_scale(key_list[17], (CH, 4, CH), ((0, 8), (2, 4)), -0.2, 0.2)), 3.620921518177056e-07, 1.4483686072708224e-06)
    norm_second = jnp.clip(jnp.exp(math.log(2.317389771633316e-05) - 1.3862944 * jax.random.uniform(key_list[18], (CH * 12,), jnp.float32) ** block_scale(key_list[18], (CH * 12,), ((0, 32),), -0.2, 0.2)), 5.79347442908329e-06, 2.317389771633316e-05)
    io_average = scatter_about(key_list[19], (CH * 2 * SUB,), 48 ** -0.5, 0.875, ((0, 32),), jnp.float32)
    conv_average = scatter_about(key_list[20], (4, 9, CH, CH), (9 * CH) ** -0.5, 0.125, ((2, 8), (3, 4)), jnp.float32)
    time_average = scatter_about(key_list[21], (2, CH, CH), CH ** -0.5, 0.375, ((1, 8), (2, 4)), jnp.float32)
    attn_average = scatter_about(key_list[22], (CH, 4, CH), CH ** -0.5, 0.375, ((0, 8), (2, 4)), jnp.float32)
    norm_average = draw_norm_average(jax.random.fold_in(key_list[24], 71), 0)
    return dict(images=images, noises=noises, order=order, time_index=time_index, io_weight=io_weight, conv_weight=conv_weight, time_weight=time_weight, attn_weight=attn_weight, norm_param=norm_param, io_first=io_first, conv_first=conv_first, time_first=time_first, attn_first=attn_first, norm_first=norm_first, io_second=io_second, conv_second=conv_second, time_second=time_second, attn_second=attn_second, norm_second=norm_second, io_average=io_average, conv_average=conv_average, time_average=time_average, attn_average=attn_average, norm_average=norm_average)


EPS_NORM = 1e-05
SINK_EPS = 0.01
CLIP_NORM = 1.0
BETA_ONE = 0.5
BETA_TWO = 0.5
ADAM_EPS = 1e-08
WEIGHT_DECAY = 0.01
EMA_DECAY = 0.9
RATES = (0.06, 0.01, 0.03, 0.03, 0.3)
HIGH = lax.Precision.HIGHEST
OFFSETS = [(row_off, col_off) for row_off in (-1, 0, 1) for col_off in (-1, 0, 1)]

@jax.custom_vjp
def low(v):
    return lax.optimization_barrier(v.astype(jnp.bfloat16)).astype(jnp.float32)

@jax.custom_vjp
def low_back(v):
    return v

def low_keep(v):
    return (low(v), None)

def low_pass(kept, grad):
    return (grad,)

def back_keep(v):
    return (v, None)

def back_low(kept, grad):
    return (low(grad),)
low.defvjp(low_keep, low_pass)
low_back.defvjp(back_keep, back_low)

def shifted(field, row_step, col_step):
    side = math.isqrt(field.shape[-1])
    leading = field.shape[:-1]
    grid = field.reshape(leading + (side, side))
    padded = jnp.pad(grid, [(0, 0)] * len(leading) + [(1, 1), (1, 1)])
    moved = padded[..., 1 + row_step:1 + row_step + side, 1 + col_step:1 + col_step + side]
    return moved.reshape(leading + (side * side,))

def conv_apply(inputs, kernel):
    stacked = jnp.stack([shifted(inputs, row_off, col_off) for row_off, col_off in OFFSETS], axis=1)
    return jnp.einsum('nkcp,kco->nop', stacked, kernel, precision=HIGH)

def norm_act(field, gain, bias, active):
    count, channels, spots = field.shape
    grouped = field.reshape(count, channels // (CH // GROUPS), CH // GROUPS, spots)
    center = lax.optimization_barrier(jnp.mean(grouped, axis=(2, 3), keepdims=True))
    centred = grouped - center
    spread = lax.optimization_barrier(jnp.mean(centred * centred, axis=(2, 3), keepdims=True))
    normed = (centred * lax.rsqrt(spread + EPS_NORM)).reshape(field.shape)
    normed = normed * gain[None, :, None] + bias[None, :, None]
    if active:
        return jax.nn.silu(normed)
    return normed

def time_features(time_index):
    times = (time_index.astype(jnp.float32) + 0.5) / NT
    half = CH // 2
    frequency = jnp.exp(-math.log(10000.0) * jnp.arange(half, dtype=jnp.float32) / half)
    angles = 1000.0 * times[:, None] * frequency[None, :]
    return jnp.concatenate([jnp.sin(angles), jnp.cos(angles)], axis=1)

def network(params, inputs, features):
    io_all = low(params[0]).reshape(CH, 2, SUB)
    conv = low(params[1])
    temb = low(params[2])
    attn = low(params[3])
    norms = low(params[4]).reshape(CH, 12)
    feats = low(features)

    def normed(field, slot, active):
        return norm_act(field, norms[:, 2 * slot], norms[:, 2 * slot + 1], active)

    def residual(field, layer, slot):
        first = low(normed(field, slot, True))
        added = jnp.einsum('ni,io->no', feats, temb[layer], precision=HIGH)
        mixed = low_back(conv_apply(first, conv[2 * layer]) + added[:, :, None])
        second = low(normed(mixed, slot + 1, True))
        return field + low_back(conv_apply(second, conv[2 * layer + 1]))

    def attention(field):
        normal = low(normed(field, 2, False))
        proj = attn[:, :3].reshape(CH, 3, HEADS, HD)
        qkv = jnp.einsum('ncp,cjhd->jnhpd', normal, proj, precision=HIGH)
        query = low(low_back(qkv[0]))
        key_part = low(low_back(qkv[1]))
        value = low(low_back(qkv[2]))
        scores = low_back(jnp.einsum('nhpd,nhqd->nhpq', query, key_part, precision=HIGH) * HD ** (-0.5))
        probs = jax.nn.softmax(scores, axis=-1)
        mixed = low(low_back(jnp.einsum('nhpq,nhqd->nhpd', low(probs), value, precision=HIGH)))
        out_proj = attn[:, 3].reshape(CH, HEADS, HD)
        return field + low_back(jnp.einsum('nhpd,chd->ncp', mixed, out_proj, precision=HIGH))
    field = low_back(jnp.einsum('nkp,ck->ncp', low(inputs), io_all[:, 0], precision=HIGH))
    field = residual(field, 0, 0)
    field = attention(field)
    field = residual(field, 1, 3)
    last = low(normed(field, 5, True))
    return low_back(jnp.einsum('ncp,ck->nkp', last, io_all[:, 1], precision=HIGH))

def pairing(pixels_low, noise_low):
    pixels = pixels_low.astype(jnp.float32)
    noise = noise_low.astype(jnp.float32)
    gram = jnp.dot(pixels, noise.T, precision=HIGH)
    cost = (lax.optimization_barrier(jnp.sum(pixels * pixels, axis=1))[:, None] + lax.optimization_barrier(jnp.sum(noise * noise, axis=1))[None, :] - 2.0 * gram) / (SUB * POS)
    affinity = 2.0 * gram / (SUB * POS * SINK_EPS)
    kernel = jnp.exp(affinity - lax.optimization_barrier(jnp.max(affinity, axis=1, keepdims=True)))
    share = 1.0 / BATCH
    left = jnp.ones((BATCH,), jnp.float32)
    right = jnp.ones((BATCH,), jnp.float32)
    for sweep in range(SINK):
        left = share / jnp.dot(kernel, right, precision=HIGH)
        right = share / jnp.dot(left, kernel, precision=HIGH)
    scaled = kernel * right[None, :]
    mixing = (scaled / lax.optimization_barrier(jnp.sum(scaled, axis=1, keepdims=True))).astype(jnp.bfloat16)
    paired = jnp.dot(mixing, noise_low, preferred_element_type=jnp.float32)
    plan_cost = jnp.sum(left[:, None] * scaled * cost)
    return (paired, plan_cost)

def adam_update(weight, first, second, average, gradient, rate):
    first = BETA_ONE * first + (1 - BETA_ONE) * gradient
    second = BETA_TWO * second + (1 - BETA_TWO) * gradient * gradient
    ratio = first / (1 - BETA_ONE ** STEP) / (jnp.sqrt(second / (1 - BETA_TWO ** STEP)) + ADAM_EPS)
    weight = weight - rate * (ratio + WEIGHT_DECAY * weight)
    average = EMA_DECAY * average + (1 - EMA_DECAY) * weight
    return (weight, first, second, average)

def reference(images, noises, order, time_index, io_weight, conv_weight, time_weight, attn_weight, norm_param, io_first, conv_first, time_first, attn_first, norm_first, io_second, conv_second, time_second, attn_second, norm_second, io_average, conv_average, time_average, attn_average, norm_average):
    params = (io_weight, conv_weight, time_weight, attn_weight, norm_param)
    blocks = TOTAL // (MB * IMG_DEV)
    base = (jnp.arange(blocks, dtype=jnp.int32) * (MB * IMG_DEV))[:, None]
    picked = images[(order.reshape(blocks, MB * IMG_DEV) + base).reshape(-1)]
    grouped = picked.reshape(blocks, MB, IMG_DEV, SUB * POS).transpose(1, 0, 2, 3).reshape(MB, BATCH, SUB * POS)
    summed = jax.tree.map(jnp.zeros_like, params)
    loss_list = []
    cost_list = []
    groups_count = BATCH // IMG_DEV
    for micro in range(MB):
        paired, plan_cost = pairing(grouped[micro], noises[micro])
        times = ((time_index[micro].astype(jnp.float32) + 0.5) / NT)[:, None]
        pixels = grouped[micro].astype(jnp.float32)
        inputs = ((1 - times) * paired + times * pixels).reshape(groups_count, IMG_DEV, SUB, POS)
        target = (pixels - paired).reshape(groups_count, IMG_DEV, SUB, POS)
        feats = time_features(time_index[micro]).reshape(groups_count, IMG_DEV, CH)

        def group_step(carry, pieces):
            totals, loss_total = carry
            group_in, group_target, group_feats = pieces

            def objective(weights):
                error = network(weights, group_in, group_feats) - group_target
                return jnp.sum(error * error)
            value, back = jax.vjp(jax.checkpoint(objective), params)
            grads = back(jnp.float32(1.0 / (MB * BATCH)))[0]
            return ((jax.tree.map(jnp.add, totals, grads), loss_total + value), None)
        (summed, loss_value), unused = lax.scan(group_step, (summed, jnp.float32(0.0)), (inputs, target, feats))
        loss_list.append(loss_value)
        cost_list.append(plan_cost)
    squares = sum((jnp.sum(part * part) for part in summed))
    grad_norm = jnp.sqrt(squares)
    scale = CLIP_NORM / jnp.maximum(grad_norm, CLIP_NORM)
    firsts = (io_first, conv_first, time_first, attn_first, norm_first)
    seconds = (io_second, conv_second, time_second, attn_second, norm_second)
    averages = (io_average, conv_average, time_average, attn_average, norm_average)
    results = [adam_update(params[kind], firsts[kind], seconds[kind], averages[kind], summed[kind] * scale, RATES[kind]) for kind in range(5)]
    return (results[0][0], results[1][0], results[2][0], results[3][0], results[4][0], results[0][1], results[1][1], results[2][1], results[3][1], results[4][1], results[0][2], results[1][2], results[2][2], results[3][2], results[4][2], results[0][3], results[1][3], results[2][3], results[3][3], results[4][3], jnp.stack(loss_list), jnp.stack(cost_list), grad_norm)
```

```python
from functools import partial
import math

import jax
import jax.numpy as jnp
from jax import lax
from jax.experimental import pallas as pl
from jax.experimental.pallas import tpu as pltpu
from jax.sharding import PartitionSpec as P

CH = 256
GROUPS = 32
HEADS = 4
HD = 64
SUB = 12
POS = 256
SIDE = 16
SINK = 10
NT = 1000
STEP = 5
MATS = 42
TIME_AT = 36
ATTN_AT = 38


EPS_NORM = 1e-05
SINK_EPS = 0.01
CLIP_NORM = 1.0
BETA_ONE = 0.5
BETA_TWO = 0.5
ADAM_EPS = 1e-08
WEIGHT_DECAY = 0.01
EMA_DECAY = 0.9
RATES = (0.06, 0.01, 0.03, 0.03, 0.3)
F32 = jnp.float32
BF16 = jnp.bfloat16
ROWS = 32
PAD = SIDE
IMGS = 2
SPOTS = IMGS * POS


def dot(a, b, ca=1, cb=0):
    return lax.dot_general(a, b, (((ca,), (cb,)), ((), ())), preferred_element_type=F32)


def split3(v):
    one = v.astype(BF16)
    rest = v - one.astype(F32)
    two = rest.astype(BF16)
    three = (rest - two.astype(F32)).astype(BF16)
    return one, two, three


def group_sum(v):
    per = CH // GROUPS
    rows = lax.broadcasted_iota(jnp.int32, (CH, CH), 0) // per
    cols = lax.broadcasted_iota(jnp.int32, (CH, CH), 1) // per
    ones = jnp.where(rows == cols, 1.0, 0.0).astype(BF16)
    one, two, three = split3(v)
    got = dot(jnp.concatenate([one.astype(F32), two.astype(F32), three.astype(F32)], axis=0).astype(BF16), ones)
    n = v.shape[0]
    return got[:n] + got[n : 2 * n] + got[2 * n :]


def rows8(*rows):
    return jnp.concatenate(list(rows) + [jnp.zeros((8 - len(rows), CH), F32)], axis=0)


def for_blocks(step, init):
    return lax.fori_loop(0, POS // ROWS, lambda i, c: step(pl.multiple_of(i * ROWS, ROWS), c), init, unroll=2)


def norm_stats(field, stats, slot):
    zero = jnp.zeros((8, CH), F32)

    def fold(v):
        return v.reshape(ROWS // 8, 8, CH).sum(axis=0)

    sums = []
    for n in range(IMGS):
        acc = for_blocks(lambda at, c: c + fold(field[pl.ds(n * POS + at, ROWS), :]), zero)
        sums.append(jnp.sum(acc, axis=0, keepdims=True))
    scale = 1.0 / (POS * (CH // GROUPS))
    means = group_sum(rows8(*sums)) * scale
    sums = []
    for n in range(IMGS):
        mean = means[n : n + 1]

        def step(at, c):
            d = field[pl.ds(n * POS + at, ROWS), :] - mean
            return c + fold(d * d)

        sums.append(jnp.sum(for_blocks(step, zero), axis=0, keepdims=True))
    devs = group_sum(rows8(*sums)) * scale
    stats[slot, 0:8] = means
    stats[slot, 8:16] = lax.rsqrt(devs + EPS_NORM)


def put_shifts(pads, n, at, value):
    col = lax.broadcasted_iota(jnp.int32, value.shape, 0) % SIDE
    left = jnp.where(col == 0, 0.0, pltpu.roll(value, 1, 0))
    right = jnp.where(col == SIDE - 1, 0.0, pltpu.roll(value, value.shape[0] - 1, 0))
    rows = pl.ds(PAD + at, value.shape[0])
    pads[0, n, rows, :] = left.astype(BF16)
    pads[1, n, rows, :] = value.astype(BF16)
    pads[2, n, rows, :] = right.astype(BF16)


def tap(pads, r, c):
    return pads[c + 1, :, PAD + SIDE * r : PAD + SIDE * r + POS, :].reshape(SPOTS, CH)


OFFSETS = [(r, c) for r in (-1, 0, 1) for c in (-1, 0, 1)]


def network_kernel(
    x_ref, z_ref, mine_ref, noise_ref, when_ref, feat_ref, flag_ref, mats, ion_ref,
    dmats, dion_ref, scal_ref,
    h, flow, c1s, pads, acts, stats, start, goal, qkv, probs, mixed, tmp, smallf, dqkv,
):
    batch = x_ref.shape[0]
    depth = x_ref.shape[1]
    active = flag_ref[0, 0]
    ion = ion_ref[...].T
    w_in = ion[0:16].astype(BF16)
    w_out = ion[16:32].astype(BF16)

    def gain(s):
        return ion[32 + 2 * s : 33 + 2 * s]

    def bias(s):
        return ion[33 + 2 * s : 34 + 2 * s]

    x = x_ref[...]
    z = z_ref[...]
    gram = dot(x, z, 1, 1)
    xf = x.astype(F32)
    zf = z.astype(F32)
    sq_x = jnp.sum(xf * xf, axis=1, keepdims=True)
    sq_z = jnp.sum(zf * zf, axis=1, keepdims=True)
    eye = lax.broadcasted_iota(jnp.int32, (batch, batch), 0) == lax.broadcasted_iota(jnp.int32, (batch, batch), 1)
    sq_z = jnp.sum(jnp.where(eye, sq_z, 0.0), axis=0, keepdims=True)
    cost = (sq_x + sq_z - 2.0 * gram) / depth
    affinity = 2.0 * gram / (depth * SINK_EPS)
    kern = jnp.exp(affinity - jnp.max(affinity, axis=1, keepdims=True))
    share = 1.0 / batch

    def sweep(i, c):
        left, right = c
        left = share / jnp.sum(kern * right, axis=1, keepdims=True)
        right = share / jnp.sum(left * kern, axis=0, keepdims=True)
        return left, right

    left, right = lax.fori_loop(0, SINK, sweep, (jnp.ones((batch, 1), F32), jnp.ones((1, batch), F32)))
    scaled = kern * right
    plan_cost = jnp.sum(left * scaled * cost)
    mixing = (scaled / jnp.sum(scaled, axis=1, keepdims=True)).astype(BF16)
    d = mine_ref[...].astype(BF16)
    mix = dot(d, mixing).astype(BF16)
    paired = dot(mix, z)[0:IMGS]
    pixels = dot(d, x)[0:IMGS]
    times = when_ref[0:IMGS, 0:1]
    inputs = ((1.0 - times) * paired + times * pixels).astype(BF16).astype(F32)
    target = pixels - paired
    start[...] = jnp.zeros_like(start)
    goal[...] = jnp.zeros_like(goal)
    for n in range(IMGS):
        for k in range(SUB):
            start[16 * n + k : 16 * n + k + 1, :] = inputs[n : n + 1, k * POS : (k + 1) * POS]
            goal[16 * n + k : 16 * n + k + 1, :] = target[n : n + 1, k * POS : (k + 1) * POS]
    begin = start[...].astype(BF16)

    for c in range(3):
        for n in range(IMGS):
            pads[c, n, 0:PAD, :] = jnp.zeros((PAD, CH), BF16)
            pads[c, n, PAD + POS :, :] = jnp.zeros((PAD, CH), BF16)

    def blocks(body):
        for n in range(IMGS):
            for_blocks(lambda at, c: (body(n, at), c)[1], 0)

    def norm_forward(field, slot, shifted, keep):
        norm_stats(field, stats, slot)
        g, b = gain(slot), bias(slot)

        def body(n, at):
            mean = stats[slot, n : n + 1]
            rstd = stats[slot, 8 + n : 9 + n]
            rows = pl.ds(n * POS + at, ROWS)
            y = (field[rows, :] - mean) * rstd * g + b
            if slot != 2:
                y = y * (1.0 / (1.0 + jnp.exp(-y)))
            acts[keep, rows, :] = y.astype(BF16)
            if shifted:
                put_shifts(pads, n, at, y)

        blocks(body)

    def conv(layer):
        acc = None
        for k, (r, c) in enumerate(OFFSETS):
            term = dot(tap(pads, r, c), mats[9 * layer + k])
            acc = term if acc is None else acc + term
        return acc

    feats = feat_ref[...].astype(BF16)

    for n in range(IMGS):
        h[0, n * POS : (n + 1) * POS, :] = dot(begin[16 * n : 16 * n + 16], w_in, 0, 0)

    def residual(layer, slot, src, dst):
        norm_forward(h.at[src], slot, True, slot)
        added = dot(feats, mats[TIME_AT + layer])
        got = conv(2 * layer)
        for n in range(IMGS):
            c1s[layer, n * POS : (n + 1) * POS, :] = got[n * POS : (n + 1) * POS] + added[n : n + 1]
        norm_forward(c1s.at[layer], slot + 1, True, slot + 1)
        h[dst] = h[src] + conv(2 * layer + 1)

    residual(0, 0, 0, 1)
    norm_forward(h.at[1], 2, False, 2)
    normal = acts[2]
    for j in range(3):
        qkv[j] = dot(normal, mats[ATTN_AT + j]).astype(BF16)
    scale = HD ** (-0.5)

    def head_mask(hh):
        return lax.broadcasted_iota(jnp.int32, (POS, CH), 1) // HD == hh

    for n in range(IMGS):
        rows = slice(n * POS, (n + 1) * POS)
        tmp[...] = jnp.zeros_like(tmp)

        def head(hh, c):
            mask = head_mask(hh)
            q = jnp.where(mask, qkv[0, rows, :].astype(F32), 0.0).astype(BF16)
            scores = dot(q, qkv[1, rows, :], 1, 1) * scale
            e = jnp.exp(scores - jnp.max(scores, axis=1, keepdims=True))
            p = e / jnp.sum(e, axis=1, keepdims=True)
            probs[n, hh] = p
            o = dot(p.astype(BF16), qkv[2, rows, :])
            tmp[...] = jnp.where(mask, o, tmp[...])
            return c

        lax.fori_loop(0, HEADS, head, 0)
        mixed[rows, :] = tmp[...].astype(BF16)
    h[2] = h[1] + dot(mixed[...], mats[ATTN_AT + 3], 1, 1)
    residual(1, 3, 2, 3)
    norm_forward(h.at[3], 5, False if False else False, 5)

    dion_ref[...] = jnp.zeros_like(dion_ref)
    loss = jnp.zeros((), F32)
    for n in range(IMGS):
        rows = slice(n * POS, (n + 1) * POS)
        last = acts[5, rows, :]
        pred = dot(w_out, last, 1, 1)
        error = pred - goal[16 * n : 16 * n + 16, :]
        loss = loss + jnp.sum(error * error)
        low = (error * (flag_ref[0, 1] * active)).astype(BF16)
        dion_ref[16:32, :] += dot(low, last)
        flow[rows, :] = dot(low, w_out, 0, 0)
    lane = lax.broadcasted_iota(jnp.int32, (8, 128), 1)
    scal_ref[...] = jnp.where(lane == 0, loss * active, jnp.where(lane == 1, plan_cost, 0.0))

    def norm_backward(field, slot, up, finish):
        g, b = gain(slot), bias(slot)
        zero = jnp.zeros((8, CH), F32)

        def fold(v):
            return v.reshape(ROWS // 8, 8, CH).sum(axis=0)

        dbs, dgs = [], []
        for n in range(IMGS):
            mean = stats[slot, n : n + 1]
            rstd = stats[slot, 8 + n : 9 + n]

            def step(at, c):
                rows = pl.ds(n * POS + at, ROWS)
                hat = (field[rows, :] - mean) * rstd
                dz = up[rows, :]
                if slot != 2:
                    y = hat * g + b
                    s = 1.0 / (1.0 + jnp.exp(-y))
                    dz = dz * (s * (1.0 + y * (1.0 - s)))
                    up[rows, :] = dz
                return (c[0] + fold(dz), c[1] + fold(dz * hat))

            db, dg = for_blocks(step, (zero, zero))
            dbs.append(jnp.sum(db, axis=0, keepdims=True))
            dgs.append(jnp.sum(dg, axis=0, keepdims=True))
        dion_ref[32 + 2 * slot : 33 + 2 * slot, :] = dgs[0] + dgs[1]
        dion_ref[33 + 2 * slot : 34 + 2 * slot, :] = dbs[0] + dbs[1]
        sums = group_sum(rows8(*[v * g for v in dbs + dgs])) * (1.0 / (POS * (CH // GROUPS)))
        for n in range(IMGS):
            mean = stats[slot, n : n + 1]
            rstd = stats[slot, 8 + n : 9 + n]
            m1 = sums[n : n + 1]
            m2 = sums[IMGS + n : IMGS + n + 1]

            def step(at, c):
                rows = pl.ds(n * POS + at, ROWS)
                hat = (field[rows, :] - mean) * rstd
                finish(n, at, rstd * (up[rows, :] * g - m1 - hat * m2))
                return c

            for_blocks(step, 0)

    def conv_backward(layer, keep):
        turned = acts[keep].T
        acc = None
        for k, (r, c) in enumerate(OFFSETS):
            there = tap(pads, -r, -c)
            dmats[9 * layer + k] = dot(turned, there)
            term = dot(there, mats[9 * layer + k], 1, 1)
            acc = term if acc is None else acc + term
        smallf[...] = acc

    def add_flow(shifted):
        def finish(n, at, dx):
            rows = pl.ds(n * POS + at, ROWS)
            total = flow[rows, :] + dx
            flow[rows, :] = total
            if shifted:
                put_shifts(pads, n, at, total)

        return finish

    def set_flow(n, at, dx):
        rows = pl.ds(n * POS + at, ROWS)
        flow[rows, :] = dx
        put_shifts(pads, n, at, dx)

    def only_shifts(n, at, dx):
        put_shifts(pads, n, at, dx)

    def residual_backward(layer, slot, src, last_one):
        conv_backward(2 * layer + 1, slot + 1)
        norm_backward(c1s.at[layer], slot + 1, smallf, only_shifts)
        sums = []
        for n in range(IMGS):
            low = pads[1, n, PAD : PAD + POS, :].astype(F32)
            sums.append(jnp.sum(low, axis=0, keepdims=True))
        one, two, three = split3(rows8(*sums))
        stack = jnp.concatenate([v.astype(F32) for v in (one, two, three)], axis=0).astype(BF16)
        feats3 = jnp.concatenate([feats.astype(F32)] * 3, axis=0).astype(BF16)
        dmats[TIME_AT + layer] = dot(feats3, stack, 0, 0)
        conv_backward(2 * layer, slot)
        norm_backward(h.at[src], slot, smallf, add_flow(False))

    norm_backward(h.at[3], 5, flow, set_flow)
    residual_backward(1, 3, 2, False)

    dy = flow[...].astype(BF16)
    dmats[ATTN_AT + 3] = dot(dy.T, mixed[...])
    dqkv[3] = dot(dy, mats[ATTN_AT + 3]).astype(BF16)
    for n in range(IMGS):
        rows = slice(n * POS, (n + 1) * POS)
        for j in range(3):
            smallf[j % 2 * POS : j % 2 * POS + POS, :] = jnp.zeros((POS, CH), F32)
        tmp[...] = jnp.zeros_like(tmp)

        def head(hh, c):
            mask = head_mask(hh)
            do = jnp.where(mask, dqkv[3, rows, :].astype(F32), 0.0).astype(BF16)
            q = jnp.where(mask, qkv[0, rows, :].astype(F32), 0.0).astype(BF16)
            p = probs[n, hh]
            dp = dot(do, qkv[2, rows, :], 1, 1)
            ds = (p * (dp - jnp.sum(p * dp, axis=1, keepdims=True))).astype(BF16)
            tmp[...] = jnp.where(mask, dot(ds, qkv[1, rows, :]), tmp[...])
            smallf[0:POS, :] += dot(ds, q, 0, 0)
            smallf[POS:, :] += dot(p.astype(BF16), do, 0, 0)
            return c

        lax.fori_loop(0, HEADS, head, 0)
        dqkv[0, rows, :] = (tmp[...] * scale).astype(BF16)
        dqkv[1, rows, :] = (smallf[0:POS, :] * scale).astype(BF16)
        dqkv[2, rows, :] = smallf[POS:, :].astype(BF16)
    turned = acts[2].T
    acc = None
    for j in range(3):
        dmats[ATTN_AT + j] = dot(turned, dqkv[j])
        term = dot(dqkv[j], mats[ATTN_AT + j], 1, 1)
        acc = term if acc is None else acc + term
    smallf[...] = acc
    norm_backward(h.at[1], 2, smallf, add_flow(True))
    residual_backward(0, 0, 0, True)
    for n in range(IMGS):
        rows = slice(n * POS, (n + 1) * POS)
        dion_ref[0:16, :] += dot(begin[16 * n : 16 * n + 16], flow[rows, :].astype(BF16))


def network(x, z, mine, when, feat, flag, mats, ion):
    whole = pl.BlockSpec(memory_space=pltpu.VMEM)
    noise = jnp.zeros((8, 128), F32)
    return pl.pallas_call(
        network_kernel,
        out_shape=(
            jax.ShapeDtypeStruct((MATS, CH, CH), F32),
            jax.ShapeDtypeStruct((48, CH), F32),
            jax.ShapeDtypeStruct((8, 128), F32),
        ),
        in_specs=[whole] * 6 + [pl.BlockSpec(memory_space=pltpu.SMEM)] + [whole] * 2,
        out_specs=(whole, whole, whole),
        scratch_shapes=[
            pltpu.VMEM((4, SPOTS, CH), F32),
            pltpu.VMEM((SPOTS, CH), F32),
            pltpu.VMEM((2, SPOTS, CH), F32),
            pltpu.VMEM((3, IMGS, POS + 2 * PAD, CH), BF16),
            pltpu.VMEM((6, SPOTS, CH), BF16),
            pltpu.VMEM((6, 16, CH), F32),
            pltpu.VMEM((16 * IMGS, POS), F32),
            pltpu.VMEM((16 * IMGS, POS), F32),
            pltpu.VMEM((3, SPOTS, CH), BF16),
            pltpu.VMEM((IMGS, HEADS, POS, POS), F32),
            pltpu.VMEM((SPOTS, CH), BF16),
            pltpu.VMEM((POS, CH), F32),
            pltpu.VMEM((SPOTS, CH), F32),
            pltpu.VMEM((4, SPOTS, CH), BF16),
        ],
        compiler_params=pltpu.CompilerParams(vmem_limit_bytes=56 * 2**20),
    )(x, z, mine, noise, when, feat, flag, mats, ion)


def time_features(time_index):
    times = (time_index.astype(jnp.float32) + 0.5) / NT
    half = CH // 2
    frequency = jnp.exp(-math.log(10000.0) * jnp.arange(half, dtype=jnp.float32) / half)
    angles = 1000.0 * times[:, None] * frequency[None, :]
    return jnp.concatenate([jnp.sin(angles), jnp.cos(angles)], axis=1)


def adam_update(weight, first, second, average, gradient, rate):
    first = BETA_ONE * first + (1 - BETA_ONE) * gradient
    second = BETA_TWO * second + (1 - BETA_TWO) * gradient * gradient
    ratio = first / (1 - BETA_ONE**STEP) / (jnp.sqrt(second / (1 - BETA_TWO**STEP)) + ADAM_EPS)
    weight = weight - rate * (ratio + WEIGHT_DECAY * weight)
    average = EMA_DECAY * average + (1 - EMA_DECAY) * weight
    return (weight, first, second, average)


def pack_mats(conv, time, attn):
    return jnp.concatenate(
        [conv.reshape((TIME_AT,) + conv.shape[2:]), time, attn.transpose(1, 0, 2)], axis=0
    )


def pack_small(io, norm):
    own = norm.shape[0] // SUB
    io = io.reshape(own, 2, SUB)
    norm = norm.reshape(own, SUB)
    gap = jnp.zeros((own, 16 - SUB), io.dtype)
    return jnp.concatenate(
        [io[:, 0], gap, io[:, 1], gap, norm, gap, jnp.zeros((own, 80), io.dtype)], axis=1
    )


def body(
    images, noises, order, time_index, io_weight, conv_weight, time_weight, attn_weight, norm_param,
    io_first, conv_first, time_first, attn_first, norm_first,
    io_second, conv_second, time_second, attn_second, norm_second,
    io_average, conv_average, time_average, attn_average, norm_average,
):
    rank = lax.axis_index("mp")
    place = lax.axis_index("dp")
    micro, count, depth = noises.shape
    turn = jnp.minimum(rank, micro - 1)
    mats = pack_mats(conv_weight, time_weight, attn_weight).astype(BF16)
    mats = lax.all_gather(lax.all_gather(mats, "dp", axis=1, tiled=True), "mp", axis=2, tiled=True)
    ion = pack_small(io_weight, norm_param).astype(BF16)
    ion = lax.all_gather(ion, ("mp", "dp"), axis=0, tiled=True).astype(F32)
    chosen = lax.dynamic_slice_in_dim(order, turn * count, count, 0)
    own = jnp.stack(
        [jnp.take(images, chosen, axis=0), lax.dynamic_index_in_dim(noises, turn, 0, keepdims=False)]
    )
    both = lax.all_gather(own, "dp", axis=1, tiled=True)
    batch = both.shape[1]
    when = lax.dynamic_index_in_dim(time_index, turn, 0, keepdims=False)
    feat = jnp.pad(time_features(when).astype(BF16).astype(F32), ((0, 8 - count), (0, 0)))
    times = (when.astype(F32) + 0.5) / NT
    times = jnp.pad(jnp.broadcast_to(times[:, None], (count, 128)), ((0, 8 - count), (0, 0)))
    spot = jnp.arange(8)[:, None]
    mine = ((jnp.arange(batch)[None, :] == place * count + spot) & (spot < count)).astype(F32)
    active = (rank < micro).astype(F32)
    flag = jnp.stack([active, jnp.float32(2.0 / (micro * batch))]).reshape(1, 2)
    dmats, dion, scal = network(both[0], both[1], mine, times, feat, flag, mats, ion)
    dmats = lax.psum_scatter(dmats, "dp", scatter_dimension=1, tiled=True)
    dmats = lax.psum_scatter(dmats, "mp", scatter_dimension=2, tiled=True)
    dion = lax.psum_scatter(dion.T, ("mp", "dp"), scatter_dimension=0, tiled=True)
    hot = (jnp.arange(micro) == rank).astype(F32)
    squares = jnp.sum(dmats * dmats) + jnp.sum(dion * dion)
    total_sq, loss_sum, cost_sum = lax.psum(
        (squares, hot * scal[0, 0], jnp.where(place == 0, hot * scal[0, 1], 0.0)), ("dp", "mp")
    )
    grad_norm = jnp.sqrt(total_sq)
    scale = CLIP_NORM / jnp.maximum(grad_norm, CLIP_NORM)
    grads = (
        jnp.concatenate([dion[:, None, 0:SUB], dion[:, None, 16 : 16 + SUB]], axis=1).reshape(-1),
        dmats[:TIME_AT].reshape(conv_weight.shape),
        dmats[TIME_AT:ATTN_AT],
        dmats[ATTN_AT:].transpose(1, 0, 2),
        dion[:, 32 : 32 + SUB].reshape(-1),
    )
    weights = (io_weight, conv_weight, time_weight, attn_weight, norm_param)
    firsts = (io_first, conv_first, time_first, attn_first, norm_first)
    seconds = (io_second, conv_second, time_second, attn_second, norm_second)
    averages = (io_average, conv_average, time_average, attn_average, norm_average)
    results = [
        adam_update(weights[kind], firsts[kind], seconds[kind], averages[kind], grads[kind] * scale, RATES[kind])
        for kind in range(5)
    ]
    return tuple(results[kind][part] for part in range(4) for kind in range(5)) + (loss_sum, cost_sum, grad_norm)


def solution(mesh):
    flat = P(("mp", "dp"))
    state = (flat, P(None, None, "dp", "mp"), P(None, "dp", "mp"), P("dp", None, "mp"), flat)
    return jax.shard_map(
        body,
        mesh=mesh,
        in_specs=(P("dp", None), P(None, "dp", None), P("dp"), P(None, "dp")) + state * 4,
        out_specs=state * 4 + (P(), P(), P()),
        check_vma=False,
    )
```

```python
import functools
import math

import jax
import jax.numpy as jnp
from jax import lax
from jax.experimental import pallas as pl
from jax.experimental.pallas import tpu as pltpu
from jax.sharding import PartitionSpec as P

CH = 256
GROUPS = 32
HEADS = 4
HD = 64
SUB = 12
POS = 256
SIDE = 16
SINK = 10
NT = 1000
STEP = 5
MATS = 42
CONV_AT = (1, 10, 24, 33)
TIME_AT = (0, 23)
ATTN_AT = 19
CHUNKS = ((0, 10), (10, 9), (19, 4), (23, 10), (33, 9))
LEVELS = 32000.0
MESH = pl.DeviceIdType.MESH


EPS_NORM = 1e-05
SINK_EPS = 0.01
CLIP_NORM = 1.0
BETA_ONE = 0.5
BETA_TWO = 0.5
ADAM_EPS = 1e-08
WEIGHT_DECAY = 0.01
EMA_DECAY = 0.9
RATES = (0.06, 0.01, 0.03, 0.03, 0.3)
F32 = jnp.float32
BF16 = jnp.bfloat16
ROWS = 32
PAD = SIDE
IMGS = 2
SPOTS = IMGS * POS


def dot(a, b, ca=1, cb=0):
    return lax.dot_general(a, b, (((ca,), (cb,)), ((), ())), preferred_element_type=F32)


def split3(v):
    one = v.astype(BF16)
    rest = v - one.astype(F32)
    two = rest.astype(BF16)
    three = (rest - two.astype(F32)).astype(BF16)
    return one, two, three


def group_sum(v):
    per = CH // GROUPS
    rows = lax.broadcasted_iota(jnp.int32, (CH, CH), 0) // per
    cols = lax.broadcasted_iota(jnp.int32, (CH, CH), 1) // per
    ones = jnp.where(rows == cols, 1.0, 0.0).astype(BF16)
    one, two, three = split3(v)
    got = dot(jnp.concatenate([one.astype(F32), two.astype(F32), three.astype(F32)], axis=0).astype(BF16), ones)
    n = v.shape[0]
    return got[:n] + got[n : 2 * n] + got[2 * n :]


def rows8(*rows):
    return jnp.concatenate(list(rows) + [jnp.zeros((8 - len(rows), CH), F32)], axis=0)


def for_blocks(step, init):
    return lax.fori_loop(0, POS // ROWS, lambda i, c: step(pl.multiple_of(i * ROWS, ROWS), c), init, unroll=2)


def norm_stats(field, stats, slot):
    zero = jnp.zeros((8, CH), F32)

    def fold(v):
        return v.reshape(ROWS // 8, 8, CH).sum(axis=0)

    sums = []
    for n in range(IMGS):
        acc = for_blocks(lambda at, c: c + fold(field[pl.ds(n * POS + at, ROWS), :]), zero)
        sums.append(jnp.sum(acc, axis=0, keepdims=True))
    scale = 1.0 / (POS * (CH // GROUPS))
    means = group_sum(rows8(*sums)) * scale
    sums = []
    for n in range(IMGS):
        mean = means[n : n + 1]

        def step(at, c):
            d = field[pl.ds(n * POS + at, ROWS), :] - mean
            return c + fold(d * d)

        sums.append(jnp.sum(for_blocks(step, zero), axis=0, keepdims=True))
    devs = group_sum(rows8(*sums)) * scale
    stats[slot, 0:8] = means
    stats[slot, 8:16] = lax.rsqrt(devs + EPS_NORM)


def put_shifts(pads, n, at, value):
    col = lax.broadcasted_iota(jnp.int32, value.shape, 0) % SIDE
    left = jnp.where(col == 0, 0.0, pltpu.roll(value, 1, 0))
    right = jnp.where(col == SIDE - 1, 0.0, pltpu.roll(value, value.shape[0] - 1, 0))
    rows = pl.ds(PAD + at, value.shape[0])
    pads[0, n, rows, :] = left.astype(BF16)
    pads[1, n, rows, :] = value.astype(BF16)
    pads[2, n, rows, :] = right.astype(BF16)


def tap(pads, r, c):
    return pads[c + 1, :, PAD + SIDE * r : PAD + SIDE * r + POS, :].reshape(SPOTS, CH)


OFFSETS = [(r, c) for r in (-1, 0, 1) for c in (-1, 0, 1)]


def train(
    x, z, mine, when_ref, feat_ref, active, step_scale, ion, mat, put, ready, done,
    dion_ref, scal_ref,
    h, flow, c1s, pads, acts, stats, start, goal, qkv, probs, mixed, tmp, smallf, dqkv,
):
    batch, depth = x.shape
    w_in = ion[0:16].astype(BF16)
    w_out = ion[16:32].astype(BF16)

    def gain(s):
        return ion[32 + 2 * s : 33 + 2 * s]

    def bias(s):
        return ion[33 + 2 * s : 34 + 2 * s]

    gram = dot(x, z, 1, 1)
    xf = x.astype(F32)
    zf = z.astype(F32)
    sq_x = jnp.sum(xf * xf, axis=1, keepdims=True)
    sq_z = jnp.sum(zf * zf, axis=1, keepdims=True)
    eye = lax.broadcasted_iota(jnp.int32, (batch, batch), 0) == lax.broadcasted_iota(jnp.int32, (batch, batch), 1)
    sq_z = jnp.sum(jnp.where(eye, sq_z, 0.0), axis=0, keepdims=True)
    cost = (sq_x + sq_z - 2.0 * gram) / depth
    affinity = 2.0 * gram / (depth * SINK_EPS)
    kern = jnp.exp(affinity - jnp.max(affinity, axis=1, keepdims=True))
    share = 1.0 / batch

    def sweep(i, c):
        left, right = c
        left = share / jnp.sum(kern * right, axis=1, keepdims=True)
        right = share / jnp.sum(left * kern, axis=0, keepdims=True)
        return left, right

    left, right = lax.fori_loop(0, SINK, sweep, (jnp.ones((batch, 1), F32), jnp.ones((1, batch), F32)))
    scaled = kern * right
    plan_cost = jnp.sum(left * scaled * cost)
    mixing = (scaled / jnp.sum(scaled, axis=1, keepdims=True)).astype(BF16)
    d = mine.astype(BF16)
    mix = dot(d, mixing).astype(BF16)
    paired = dot(mix, z)[0:IMGS]
    pixels = dot(d, x)[0:IMGS]
    times = when_ref[0:IMGS, 0:1]
    inputs = ((1.0 - times) * paired + times * pixels).astype(BF16).astype(F32)
    target = pixels - paired
    start[...] = jnp.zeros_like(start)
    goal[...] = jnp.zeros_like(goal)
    for n in range(IMGS):
        for k in range(SUB):
            start[16 * n + k : 16 * n + k + 1, :] = inputs[n : n + 1, k * POS : (k + 1) * POS]
            goal[16 * n + k : 16 * n + k + 1, :] = target[n : n + 1, k * POS : (k + 1) * POS]
    begin = start[...].astype(BF16)

    for c in range(3):
        for n in range(IMGS):
            pads[c, n, 0:PAD, :] = jnp.zeros((PAD, CH), BF16)
            pads[c, n, PAD + POS :, :] = jnp.zeros((PAD, CH), BF16)

    def blocks(body):
        for n in range(IMGS):
            for_blocks(lambda at, c: (body(n, at), c)[1], 0)

    def norm_forward(field, slot, shifted, keep):
        norm_stats(field, stats, slot)
        g, b = gain(slot), bias(slot)

        def body(n, at):
            mean = stats[slot, n : n + 1]
            rstd = stats[slot, 8 + n : 9 + n]
            rows = pl.ds(n * POS + at, ROWS)
            y = (field[rows, :] - mean) * rstd * g + b
            if slot != 2:
                y = y * (1.0 / (1.0 + jnp.exp(-y)))
            acts[keep, rows, :] = y.astype(BF16)
            if shifted:
                put_shifts(pads, n, at, y)

        blocks(body)

    def conv(layer):
        acc = None
        for k, (r, c) in enumerate(OFFSETS):
            term = dot(tap(pads, r, c), mat(CONV_AT[layer] + k))
            acc = term if acc is None else acc + term
        return acc

    feats = feat_ref[...].astype(BF16)

    for n in range(IMGS):
        h[0, n * POS : (n + 1) * POS, :] = dot(begin[16 * n : 16 * n + 16], w_in, 0, 0)

    def residual(layer, slot, src, dst):
        norm_forward(h.at[src], slot, True, slot)
        ready(0 if layer == 0 else 3)
        added = dot(feats, mat(TIME_AT[layer]))
        got = conv(2 * layer)
        for n in range(IMGS):
            c1s[layer, n * POS : (n + 1) * POS, :] = got[n * POS : (n + 1) * POS] + added[n : n + 1]
        norm_forward(c1s.at[layer], slot + 1, True, slot + 1)
        ready(1 if layer == 0 else 4)
        h[dst] = h[src] + conv(2 * layer + 1)

    residual(0, 0, 0, 1)
    norm_forward(h.at[1], 2, False, 2)
    ready(2)
    normal = acts[2]
    for j in range(3):
        qkv[j] = dot(normal, mat(ATTN_AT + j)).astype(BF16)
    scale = HD ** (-0.5)

    def head_mask(hh):
        return lax.broadcasted_iota(jnp.int32, (POS, CH), 1) // HD == hh

    for n in range(IMGS):
        rows = slice(n * POS, (n + 1) * POS)
        tmp[...] = jnp.zeros_like(tmp)

        def head(hh, c):
            mask = head_mask(hh)
            q = jnp.where(mask, qkv[0, rows, :].astype(F32), 0.0).astype(BF16)
            scores = dot(q, qkv[1, rows, :], 1, 1) * scale
            e = jnp.exp(scores - jnp.max(scores, axis=1, keepdims=True))
            p = e / jnp.sum(e, axis=1, keepdims=True)
            probs[n, hh] = p
            o = dot(p.astype(BF16), qkv[2, rows, :])
            tmp[...] = jnp.where(mask, o, tmp[...])
            return c

        lax.fori_loop(0, HEADS, head, 0)
        mixed[rows, :] = tmp[...].astype(BF16)
    h[2] = h[1] + dot(mixed[...], mat(ATTN_AT + 3), 1, 1)
    residual(1, 3, 2, 3)
    norm_forward(h.at[3], 5, False, 5)

    dion_ref[...] = jnp.zeros_like(dion_ref)
    loss = jnp.zeros((), F32)
    for n in range(IMGS):
        rows = slice(n * POS, (n + 1) * POS)
        last = acts[5, rows, :]
        pred = dot(w_out, last, 1, 1)
        error = pred - goal[16 * n : 16 * n + 16, :]
        loss = loss + jnp.sum(error * error)
        low = (error * (step_scale * active)).astype(BF16)
        dion_ref[16:32, :] += dot(low, last)
        flow[rows, :] = dot(low, w_out, 0, 0)
    lane = lax.broadcasted_iota(jnp.int32, (8, 128), 1)
    scal_ref[...] = jnp.where(lane == 0, loss * active, jnp.where(lane == 1, plan_cost, 0.0))

    def norm_backward(field, slot, up, finish):
        g, b = gain(slot), bias(slot)
        zero = jnp.zeros((8, CH), F32)

        def fold(v):
            return v.reshape(ROWS // 8, 8, CH).sum(axis=0)

        dbs, dgs = [], []
        for n in range(IMGS):
            mean = stats[slot, n : n + 1]
            rstd = stats[slot, 8 + n : 9 + n]

            def step(at, c):
                rows = pl.ds(n * POS + at, ROWS)
                hat = (field[rows, :] - mean) * rstd
                dz = up[rows, :]
                if slot != 2:
                    y = hat * g + b
                    s = 1.0 / (1.0 + jnp.exp(-y))
                    dz = dz * (s * (1.0 + y * (1.0 - s)))
                    up[rows, :] = dz
                return (c[0] + fold(dz), c[1] + fold(dz * hat))

            db, dg = for_blocks(step, (zero, zero))
            dbs.append(jnp.sum(db, axis=0, keepdims=True))
            dgs.append(jnp.sum(dg, axis=0, keepdims=True))
        dion_ref[32 + 2 * slot : 33 + 2 * slot, :] = dgs[0] + dgs[1]
        dion_ref[33 + 2 * slot : 34 + 2 * slot, :] = dbs[0] + dbs[1]
        sums = group_sum(rows8(*[v * g for v in dbs + dgs])) * (1.0 / (POS * (CH // GROUPS)))
        for n in range(IMGS):
            mean = stats[slot, n : n + 1]
            rstd = stats[slot, 8 + n : 9 + n]
            m1 = sums[n : n + 1]
            m2 = sums[IMGS + n : IMGS + n + 1]

            def step(at, c):
                rows = pl.ds(n * POS + at, ROWS)
                hat = (field[rows, :] - mean) * rstd
                finish(n, at, rstd * (up[rows, :] * g - m1 - hat * m2))
                return c

            for_blocks(step, 0)

    def conv_backward(layer, keep):
        turned = acts[keep].T
        acc = None
        for k, (r, c) in enumerate(OFFSETS):
            there = tap(pads, -r, -c)
            put(CONV_AT[layer] + k, dot(turned, there))
            term = dot(there, mat(CONV_AT[layer] + k), 1, 1)
            acc = term if acc is None else acc + term
        smallf[...] = acc

    def add_flow(shifted):
        def finish(n, at, dx):
            rows = pl.ds(n * POS + at, ROWS)
            total = flow[rows, :] + dx
            flow[rows, :] = total
            if shifted:
                put_shifts(pads, n, at, total)

        return finish

    def set_flow(n, at, dx):
        rows = pl.ds(n * POS + at, ROWS)
        flow[rows, :] = dx
        put_shifts(pads, n, at, dx)

    def only_shifts(n, at, dx):
        put_shifts(pads, n, at, dx)

    def residual_backward(layer, slot, src, last_one):
        conv_backward(2 * layer + 1, slot + 1)
        done(4 if layer == 1 else 1)
        norm_backward(c1s.at[layer], slot + 1, smallf, only_shifts)
        sums = []
        for n in range(IMGS):
            low = pads[1, n, PAD : PAD + POS, :].astype(F32)
            sums.append(jnp.sum(low, axis=0, keepdims=True))
        one, two, three = split3(rows8(*sums))
        stack = jnp.concatenate([v.astype(F32) for v in (one, two, three)], axis=0).astype(BF16)
        feats3 = jnp.concatenate([feats.astype(F32)] * 3, axis=0).astype(BF16)
        put(TIME_AT[layer], dot(feats3, stack, 0, 0))
        conv_backward(2 * layer, slot)
        done(3 if layer == 1 else 0)
        norm_backward(h.at[src], slot, smallf, add_flow(False))

    norm_backward(h.at[3], 5, flow, set_flow)
    residual_backward(1, 3, 2, False)

    dy = flow[...].astype(BF16)
    put(ATTN_AT + 3, dot(dy.T, mixed[...]))
    dqkv[3] = dot(dy, mat(ATTN_AT + 3)).astype(BF16)
    for n in range(IMGS):
        rows = slice(n * POS, (n + 1) * POS)
        for j in range(3):
            smallf[j % 2 * POS : j % 2 * POS + POS, :] = jnp.zeros((POS, CH), F32)
        tmp[...] = jnp.zeros_like(tmp)

        def head(hh, c):
            mask = head_mask(hh)
            do = jnp.where(mask, dqkv[3, rows, :].astype(F32), 0.0).astype(BF16)
            q = jnp.where(mask, qkv[0, rows, :].astype(F32), 0.0).astype(BF16)
            p = probs[n, hh]
            dp = dot(do, qkv[2, rows, :], 1, 1)
            ds = (p * (dp - jnp.sum(p * dp, axis=1, keepdims=True))).astype(BF16)
            tmp[...] = jnp.where(mask, dot(ds, qkv[1, rows, :]), tmp[...])
            smallf[0:POS, :] += dot(ds, q, 0, 0)
            smallf[POS:, :] += dot(p.astype(BF16), do, 0, 0)
            return c

        lax.fori_loop(0, HEADS, head, 0)
        dqkv[0, rows, :] = (tmp[...] * scale).astype(BF16)
        dqkv[1, rows, :] = (smallf[0:POS, :] * scale).astype(BF16)
        dqkv[2, rows, :] = smallf[POS:, :].astype(BF16)
    turned = acts[2].T
    acc = None
    for j in range(3):
        put(ATTN_AT + j, dot(turned, dqkv[j]))
        term = dot(dqkv[j], mat(ATTN_AT + j), 1, 1)
        acc = term if acc is None else acc + term
    smallf[...] = acc
    done(2)
    norm_backward(h.at[1], 2, smallf, add_flow(True))
    residual_backward(0, 0, 0, True)
    for n in range(IMGS):
        rows = slice(n * POS, (n + 1) * POS)
        dion_ref[0:16, :] += dot(begin[16 * n : 16 * n + 16], flow[rows, :].astype(BF16))


def work_space():
    return [
        pltpu.VMEM((4, SPOTS, CH), F32),
        pltpu.VMEM((SPOTS, CH), F32),
        pltpu.VMEM((2, SPOTS, CH), F32),
        pltpu.VMEM((3, IMGS, POS + 2 * PAD, CH), BF16),
        pltpu.VMEM((6, SPOTS, CH), BF16),
        pltpu.VMEM((6, 16, CH), F32),
        pltpu.VMEM((16 * IMGS, POS), F32),
        pltpu.VMEM((16 * IMGS, POS), F32),
        pltpu.VMEM((3, SPOTS, CH), BF16),
        pltpu.VMEM((IMGS, HEADS, POS, POS), F32),
        pltpu.VMEM((SPOTS, CH), BF16),
        pltpu.VMEM((POS, CH), F32),
        pltpu.VMEM((SPOTS, CH), F32),
        pltpu.VMEM((4, SPOTS, CH), BF16),
    ]


def local_kernel(x_ref, z_ref, mine_ref, when_ref, feat_ref, flag_ref, mats, ion_ref, dmats, dion_ref, scal_ref, *work):
    def put(m, value):
        dmats[m] = value

    train(
        x_ref[...], z_ref[...], mine_ref[...], when_ref, feat_ref, flag_ref[0, 0], flag_ref[0, 1],
        ion_ref[...].T, lambda m: mats[m], put, lambda chunk: None, lambda chunk: None,
        dion_ref, scal_ref, *work,
    )


def local_network(x, z, mine, when, feat, flag, mats, ion):
    whole = pl.BlockSpec(memory_space=pltpu.VMEM)
    return pl.pallas_call(
        local_kernel,
        out_shape=(
            jax.ShapeDtypeStruct((MATS, CH, CH), F32),
            jax.ShapeDtypeStruct((48, CH), F32),
            jax.ShapeDtypeStruct((8, 128), F32),
        ),
        in_specs=[whole] * 5 + [pl.BlockSpec(memory_space=pltpu.SMEM)] + [whole] * 2,
        out_specs=(whole, whole, whole),
        scratch_shapes=work_space(),
        compiler_params=pltpu.CompilerParams(vmem_limit_bytes=56 * 2**20),
    )(x, z, mine, when, feat, flag, mats, ion)


Z, Y, X, C = 4, 2, 2, 2
DEVICES = Z * Y * X * C


def fused_kernel(
    micro, batch,
    ot_ref, when_ref, feat_ref, own_ref, ownion_ref,
    grads_ref, gion_ref, total_ref,
    mats, dmats, other, land, otbuf, otwide, xz, ionbuf, dion, diont, ionr, scal, scalr,
    s1q, s1r, s2q, s2r, zq, zr, expo, kept, gother,
    ot_s, ot_r, ion_s, ion_r, g_s, g_r, r_s, r_r, d_s, d_r, n_s, n_r,
    *work,
):
    dp = lax.axis_index("dp")
    mp = lax.axis_index("mp")
    z, y, x, c = dp // Y, dp % Y, mp // C, mp % C
    flat = mp * (Z * Y) + dp

    def place(z_, y_, x_, c_):
        return (z_ * Y + y_, x_ * C + c_)

    def from_flat(f):
        return (f % (Z * Y), f // (Z * Y))

    sibling = place(z, y, x, 1 - c)
    first = place(z, y * c + (1 - y) * (1 - c), x * (1 - c) + (1 - x) * c, c)
    second = place(z, (1 - y) * c + y * (1 - c), (1 - x) * (1 - c) + x * c, c)

    def remote(src, dst, send, recv, where):
        return pltpu.make_async_remote_copy(
            src_ref=src, dst_ref=dst, send_sem=send, recv_sem=recv, device_id=where, device_id_type=MESH
        )

    barrier = pltpu.get_barrier_semaphore()

    def greet(j, carry):
        pl.semaphore_signal(
            barrier, inc=1, device_id=from_flat((flat + j) % DEVICES), device_id_type=MESH
        )
        return carry

    lax.fori_loop(1, DEVICES, greet, 0)
    pl.semaphore_wait(barrier, DEVICES - 1)

    zero_copy = remote(own_ref.at[:, pl.ds((1 - c) * 16, 16)], land, g_s.at[0, 0], g_r.at[0, 0], sibling)
    zero_copy.start()

    def ot_copy(j):
        there = (dp + j) % (Z * Y)
        return remote(ot_ref, otbuf.at[dp], ot_s.at[j], ot_r.at[j], (there, mp))

    for j in range(1, Z * Y):
        ot_copy(j).start()
    otbuf[dp] = ot_ref[...]

    def ion_copy(j):
        return remote(ownion_ref, ionbuf.at[flat], ion_s.at[j], ion_r.at[j], from_flat((flat + j) % DEVICES))

    def ion_start(j, carry):
        ion_copy(j).start()
        return carry

    lax.fori_loop(1, DEVICES, ion_start, 0)
    ionbuf[flat] = ownion_ref[...]

    zero_copy.wait()

    def merge(m, carry):
        mats[m, x, z, y, c] = own_ref[m, pl.ds(pl.multiple_of(c * 16, 16), 16), :] + land[m]
        return carry

    lax.fori_loop(0, MATS, merge, 0)

    def span(i):
        return pl.ds(CHUNKS[i][0], CHUNKS[i][1])

    def z_copy(i, j):
        part = mats.at[span(i), x, z, y, c]
        return remote(part, part, g_s.at[i + 1, j], g_r.at[i + 1, j], place((z + j) % Z, y, x, c))

    def u_copy(i):
        part = mats.at[span(i), x, :, y, c]
        return remote(part, part, g_s.at[i + 1, 4], g_r.at[i + 1, 4], first)

    def v_copy(i, core):
        part = mats.at[span(i), x, :, :, 0] if core == 0 else mats.at[span(i), :, :, y, 1]
        return remote(part, part, g_s.at[i + 1, 5], g_r.at[i + 1, 5], second)

    def c_copy(i):
        part = mats.at[span(i), :, :, :, c]
        return remote(part, part, g_s.at[i + 1, 6], g_r.at[i + 1, 6], sibling)

    def on_core(act):
        for core in range(C):
            pl.when(c == core)(functools.partial(act, core))

    def gather_step(stage, i):
        if i < 0 or i >= len(CHUNKS):
            return
        if stage == 0:
            for j in range(1, Z):
                z_copy(i, j).start()
        elif stage == 1:
            for j in range(1, Z):
                z_copy(i, j).wait()
            u_copy(i).start()
        elif stage == 2:
            u_copy(i).wait()
            on_core(lambda core: v_copy(i, core).start())
        elif stage == 3:
            on_core(lambda core: v_copy(i, core).wait())
            c_copy(i).start()
        else:
            c_copy(i).wait()

    for i in range(len(CHUNKS)):
        gather_step(0, i)
    gather_step(1, 0)

    for j in range(1, Z * Y):
        ot_copy(j).wait()
    rows = ot_ref.shape[0]
    for j in range(Z * Y):
        otwide[pl.ds(j * rows, rows), :] = otbuf[j].astype(F32)
    lines = rows // (2 * IMGS)
    for r in range(2 * IMGS):
        for k in range(lines):
            xz[r // IMGS, (r % IMGS) * Z * Y : (r % IMGS + 1) * Z * Y, k * 128 : (k + 1) * 128] = otwide[
                pl.ds(r * lines + k, Z * Y, stride=rows), :
            ]
    gather_step(2, 0)
    gather_step(1, 1)

    def ion_wait(j, carry):
        ion_copy(j).wait()
        return carry

    lax.fori_loop(1, DEVICES, ion_wait, 0)
    ion = ionbuf[...].reshape(CH, 128).T
    spot = lax.broadcasted_iota(jnp.int32, (8, batch), 0)
    column = lax.broadcasted_iota(jnp.int32, (8, batch), 1)
    mine = jnp.where((column == spot * (Z * Y) + dp) & (spot < IMGS), 1.0, 0.0)
    active = jnp.where(mp < micro, 1.0, 0.0)

    def mat(m):
        return jnp.concatenate([mats[m, k].reshape(CH, 128) for k in range(X)], axis=1)

    def put(m, value):
        for k in range(X):
            dmats[m, k] = value[:, 128 * k : 128 * k + 128].reshape(Z, Y, C, 16, 128)

    def ready(i):
        gather_step(3, i)
        gather_step(2, i + 1)
        gather_step(1, i + 2)
        gather_step(4, i)

    mine_a = x * (1 - c) + y * c
    mine_b = y * (1 - c) + x * c

    def xy(a, b):
        return a * (1 - c) + b * c, b * (1 - c) + a * c

    def r_copy(i):
        return remote(
            dmats.at[span(i), :, :, :, 1 - c], other.at[span(i)], r_s.at[i, 0], r_r.at[i, 0], sibling
        )

    def base(i, per):
        return CHUNKS[i][0] * per + i

    def one_copy(i):
        part = pl.ds(base(i, 8), CHUNKS[i][1] * 8 + 1)
        return remote(s1q.at[part], s1r.at[part], r_s.at[i, 1], r_r.at[i, 1], second)

    def two_copy(i):
        part = pl.ds(base(i, 4), CHUNKS[i][1] * 4 + 1)
        return remote(s2q.at[part], s2r.at[part], r_s.at[i, 2], r_r.at[i, 2], first)

    def three_copy(i, j):
        part = pl.ds(base(i, 1), CHUNKS[i][1] + 1)
        return remote(
            zq.at[j - 1, part], zr.at[j - 1, part], r_s.at[i, 2 + j], r_r.at[i, 2 + j], place((z + j) % Z, y, x, c)
        )

    def four_copy(i):
        return remote(kept.at[span(i)], gother.at[span(i)], r_s.at[i, 6], r_r.at[i, 6], sibling)

    def exponent(tiles):
        top = jnp.max(jnp.abs(tiles[0]), axis=0, keepdims=True)
        for t in tiles[1:]:
            top = jnp.maximum(top, jnp.max(jnp.abs(t), axis=0, keepdims=True))
        return jnp.floor(jnp.log2(jnp.maximum(top, 1e-30))) + 1.0

    def coded(tile, power):
        return jnp.round(tile * (LEVELS * jnp.exp2(-power))).astype(jnp.int32).astype(jnp.int16)

    def decoded(tile, unit):
        return tile.astype(jnp.int32).astype(F32) * unit

    def units(ref, at, slot):
        expo[slot] = jnp.exp2(ref[at].astype(jnp.int32).astype(F32)) * (1.0 / LEVELS)

    def powers(ref, at):
        ref[at] = expo[0].astype(jnp.int32).astype(jnp.int16)

    def stage_one(i):
        r_copy(i).wait()
        first_m, count = CHUNKS[i]
        start = base(i, 8)

        def step(k, carry):
            m = first_m + k
            tiles = []
            for b in range(2):
                x_, y_ = xy(1 - mine_a, b)
                for zz in range(Z):
                    tiles.append(dmats[m, x_, zz, y_, c] + other[m, x_, zz, y_])
            power = exponent(tiles)
            expo[0, pl.ds(k, 1), :] = power
            for t, tile in enumerate(tiles):
                s1q[start + k * 8 + t] = coded(tile, power)
            return carry

        lax.fori_loop(0, count, step, 0)
        powers(s1q, start + count * 8)
        one_copy(i).start()

    def stage_two(i):
        one_copy(i).wait()
        first_m, count = CHUNKS[i]
        start, start_one = base(i, 4), base(i, 8)
        units(s1r, start_one + count * 8, 1)

        def step(k, carry):
            m = first_m + k
            unit = expo[1, pl.ds(k, 1), :]
            x_, y_ = xy(mine_a, 1 - mine_b)
            tiles = []
            for zz in range(Z):
                got = decoded(s1r[start_one + k * 8 + (1 - mine_b) * 4 + zz], unit)
                tiles.append(dmats[m, x_, zz, y_, c] + other[m, x_, zz, y_] + got)
            power = exponent(tiles)
            expo[0, pl.ds(k, 1), :] = power
            for t, tile in enumerate(tiles):
                s2q[start + k * 4 + t] = coded(tile, power)
            return carry

        lax.fori_loop(0, count, step, 0)
        powers(s2q, start + count * 4)
        two_copy(i).start()

    def stage_three(i):
        two_copy(i).wait()
        first_m, count = CHUNKS[i]
        start, start_one, start_two = base(i, 1), base(i, 8), base(i, 4)
        units(s1r, start_one + count * 8, 1)
        units(s2r, start_two + count * 4, 2)

        def step(k, carry):
            m = first_m + k
            unit_one = expo[1, pl.ds(k, 1), :]
            unit_two = expo[2, pl.ds(k, 1), :]

            def tile(zz):
                return (
                    dmats[m, x, zz, y, c]
                    + other[m, x, zz, y]
                    + decoded(s1r[start_one + k * 8 + mine_b * 4 + zz], unit_one)
                    + decoded(s2r[start_two + k * 4 + zz], unit_two)
                )

            tiles = [tile((z + j) % Z) for j in range(1, Z)]
            power = exponent(tiles)
            expo[0, pl.ds(k, 1), :] = power
            for j in range(1, Z):
                zq[j - 1, start + k] = coded(tiles[j - 1], power)
            kept[m] = tile(z)
            return carry

        lax.fori_loop(0, count, step, 0)
        for j in range(1, Z):
            powers(zq.at[j - 1], start + count)
        for j in range(1, Z):
            three_copy(i, j).start()

    def stage_four(i):
        for j in range(1, Z):
            three_copy(i, j).wait()
        first_m, count = CHUNKS[i]
        start = base(i, 1)
        for j in range(1, Z):
            units(zr.at[j - 1], start + count, j)

        def step(k, carry):
            m = first_m + k
            total = kept[m]
            for j in range(1, Z):
                total = total + decoded(zr[j - 1, start + k], expo[j, pl.ds(k, 1), :])
            kept[m] = total
            return carry + total * total

        square = lax.fori_loop(0, count, step, jnp.zeros((16, 128), F32))
        four_copy(i).start()
        return square

    squares = []
    order = (4, 3, 2, 1, 0)

    def reduce_step(stage, turn):
        if turn < 0 or turn >= len(order):
            return
        i = order[turn]
        if stage == 0:
            r_copy(i).start()
        elif stage == 1:
            stage_one(i)
        elif stage == 2:
            stage_two(i)
        elif stage == 3:
            stage_three(i)
        else:
            squares.append(stage_four(i))

    def done(i):
        turn = order.index(i)
        for stage in range(5):
            reduce_step(stage, turn - stage)

    train(
        xz[0].astype(BF16), xz[1].astype(BF16), mine, when_ref, feat_ref, active, 2.0 / (micro * batch),
        ion, mat, put, ready, done, dion, scal, *work,
    )

    diont[...] = jnp.concatenate([dion[...], jnp.zeros((128 - 48, CH), F32)], axis=0).T.reshape(DEVICES, 8, 128)

    def dion_copy(j):
        there = (flat + j) % DEVICES
        return remote(diont.at[there], ionr.at[flat], d_s.at[j], d_r.at[j], from_flat(there))

    def dion_start(j, carry):
        dion_copy(j).start()
        return carry

    lax.fori_loop(1, DEVICES, dion_start, 0)
    ionr[flat] = diont[flat]
    for turn in range(len(order), len(order) + 4):
        for stage in range(5):
            reduce_step(stage, turn - stage)

    def dion_wait(j, carry):
        dion_copy(j).wait()
        return carry

    lax.fori_loop(1, DEVICES, dion_wait, 0)
    small = jnp.sum(ionr[...], axis=0)
    gion_ref[...] = small
    square = jnp.sum(small * small)
    for part in squares:
        square = square + jnp.sum(part)

    loss, plan_cost = scal[0:1, 0:1], scal[0:1, 1:2]
    lane = lax.broadcasted_iota(jnp.int32, (8, 128), 1)
    tile = jnp.where(lane == 0, square, 0.0)
    tile = jnp.where(lane == 1 + mp, loss, tile)
    tile = jnp.where((lane == 1 + micro + mp) & (mp < micro) & (dp == 0), plan_cost, tile)
    tile = jnp.where((mp >= micro) & (lane > 0), 0.0, tile)
    scal[...] = tile
    scalr[flat] = tile

    def n_copy(j):
        return remote(scal, scalr.at[flat], n_s.at[j], n_r.at[j], from_flat((flat + j) % DEVICES))

    def n_start(j, carry):
        n_copy(j).start()
        return carry

    def n_wait(j, carry):
        n_copy(j).wait()
        return carry

    lax.fori_loop(1, DEVICES, n_start, 0)
    for i in order:
        four_copy(i).wait()

    def finish(m, carry):
        for half in range(C):
            tile = jnp.where(c == half, kept[m], gother[m])
            grads_ref[m, half * 16 : half * 16 + 16, :] = jnp.where(c == 0, tile[:, 0:64], tile[:, 64:128])
        return carry

    lax.fori_loop(0, MATS, finish, 0)
    lax.fori_loop(1, DEVICES, n_wait, 0)
    total_ref[...] = jnp.sum(scalr[...], axis=0)


def fused_network(micro, batch, ot, when, feat, own, ownion):
    whole = pl.BlockSpec(memory_space=pltpu.VMEM)
    blocks = (X, Z, Y)
    dma = pltpu.SemaphoreType.DMA
    count = len(CHUNKS)
    return pl.pallas_call(
        functools.partial(fused_kernel, micro, batch),
        out_shape=(
            jax.ShapeDtypeStruct((MATS, 32, 64), F32),
            jax.ShapeDtypeStruct((8, 128), F32),
            jax.ShapeDtypeStruct((8, 128), F32),
        ),
        in_specs=[whole] * 5,
        out_specs=(whole, whole, whole),
        scratch_shapes=[
            pltpu.VMEM((MATS,) + blocks + (C, 16, 128), BF16),
            pltpu.VMEM((MATS,) + blocks + (C, 16, 128), F32),
            pltpu.VMEM((MATS,) + blocks + (16, 128), F32),
            pltpu.VMEM((MATS, 16, 128), BF16),
            pltpu.VMEM((Z * Y,) + ot.shape, BF16),
            pltpu.VMEM((Z * Y * ot.shape[0], 128), F32),
            pltpu.VMEM((2, batch, SUB * POS), F32),
            pltpu.VMEM((DEVICES, 8, 128), F32),
            pltpu.VMEM((48, CH), F32),
            pltpu.VMEM((DEVICES, 8, 128), F32),
            pltpu.VMEM((DEVICES, 8, 128), F32),
            pltpu.VMEM((8, 128), F32),
            pltpu.VMEM((DEVICES, 8, 128), F32),
            pltpu.VMEM((MATS * 8 + count, 16, 128), jnp.int16),
            pltpu.VMEM((MATS * 8 + count, 16, 128), jnp.int16),
            pltpu.VMEM((MATS * 4 + count, 16, 128), jnp.int16),
            pltpu.VMEM((MATS * 4 + count, 16, 128), jnp.int16),
            pltpu.VMEM((Z - 1, MATS + count, 16, 128), jnp.int16),
            pltpu.VMEM((Z - 1, MATS + count, 16, 128), jnp.int16),
            pltpu.VMEM((Z, 16, 128), F32),
            pltpu.VMEM((MATS, 16, 128), F32),
            pltpu.VMEM((MATS, 16, 128), F32),
            dma((Z * Y,)), dma((Z * Y,)),
            dma((DEVICES,)), dma((DEVICES,)),
            dma((count + 1, 7)), dma((count + 1, 7)),
            dma((count, 7)), dma((count, 7)),
            dma((DEVICES,)), dma((DEVICES,)),
            dma((DEVICES,)), dma((DEVICES,)),
        ] + work_space(),
        compiler_params=pltpu.CompilerParams(
            vmem_limit_bytes=60 * 2**20, collective_id=0, has_side_effects=True
        ),
    )(ot, when, feat, own, ownion)


def time_features(time_index):
    times = (time_index.astype(jnp.float32) + 0.5) / NT
    half = CH // 2
    frequency = jnp.exp(-math.log(10000.0) * jnp.arange(half, dtype=jnp.float32) / half)
    angles = 1000.0 * times[:, None] * frequency[None, :]
    return jnp.concatenate([jnp.sin(angles), jnp.cos(angles)], axis=1)


def adam_update(weight, first, second, average, gradient, rate):
    first = BETA_ONE * first + (1 - BETA_ONE) * gradient
    second = BETA_TWO * second + (1 - BETA_TWO) * gradient * gradient
    ratio = first / (1 - BETA_ONE**STEP) / (jnp.sqrt(second / (1 - BETA_TWO**STEP)) + ADAM_EPS)
    weight = weight - rate * (ratio + WEIGHT_DECAY * weight)
    average = EMA_DECAY * average + (1 - EMA_DECAY) * weight
    return (weight, first, second, average)


def pack_mats(conv, time, attn):
    kinds = 9
    return jnp.concatenate(
        [time[0:1], conv[0], conv[1], attn.transpose(1, 0, 2), time[1:2], conv[2], conv[3]], axis=0
    )


def unpack_mats(mats):
    conv = jnp.stack([mats[at : at + 9] for at in CONV_AT])
    time = jnp.stack([mats[at] for at in TIME_AT])
    return conv, time, mats[ATTN_AT : ATTN_AT + 4].transpose(1, 0, 2)


def pack_small(io, norm):
    own = norm.shape[0] // SUB
    io = io.reshape(own, 2, SUB)
    norm = norm.reshape(own, SUB)
    gap = jnp.zeros((own, 16 - SUB), io.dtype)
    return jnp.concatenate(
        [io[:, 0], gap, io[:, 1], gap, norm, gap, jnp.zeros((own, 80), io.dtype)], axis=1
    )


def body(
    fused,
    images, noises, order, time_index, io_weight, conv_weight, time_weight, attn_weight, norm_param,
    io_first, conv_first, time_first, attn_first, norm_first,
    io_second, conv_second, time_second, attn_second, norm_second,
    io_average, conv_average, time_average, attn_average, norm_average,
):
    rank = lax.axis_index("mp")
    place = lax.axis_index("dp")
    micro, count, depth = noises.shape
    batch = count * lax.axis_size("dp")
    turn = jnp.minimum(rank, micro - 1)
    mats = pack_mats(conv_weight, time_weight, attn_weight).astype(BF16)
    ion = pack_small(io_weight, norm_param).astype(BF16)
    chosen = lax.dynamic_slice_in_dim(order, turn * count, count, 0)
    own_x = jnp.take(images, chosen, axis=0)
    own_z = lax.dynamic_index_in_dim(noises, turn, 0, keepdims=False)
    when = lax.dynamic_index_in_dim(time_index, turn, 0, keepdims=False)
    feat = jnp.pad(time_features(when).astype(BF16).astype(F32), ((0, 8 - count), (0, 0)))
    times = (when.astype(F32) + 0.5) / NT
    times = jnp.pad(jnp.broadcast_to(times[:, None], (count, 128)), ((0, 8 - count), (0, 0)))
    if fused:
        ot = jnp.concatenate([own_x, own_z]).reshape(-1, 128)
        none = jnp.zeros_like(mats)
        low = rank % 2 == 0
        own = jnp.concatenate([jnp.where(low, mats, none), jnp.where(low, none, mats)], axis=2)
        dmats, dion, total = fused_network(micro, batch, ot, times, feat, own, ion.astype(F32))
        total_sq = total[0, 0]
        loss_sum = total[0, 1 : 1 + micro]
        cost_sum = total[0, 1 + micro : 1 + 2 * micro]
    else:
        mats = lax.all_gather(lax.all_gather(mats, "dp", axis=1, tiled=True), "mp", axis=2, tiled=True)
        ion = lax.all_gather(ion, ("mp", "dp"), axis=0, tiled=True).astype(F32)
        both = lax.all_gather(jnp.stack([own_x, own_z]), "dp", axis=1, tiled=True)
        spot = jnp.arange(8)[:, None]
        mine = ((jnp.arange(batch)[None, :] == place * count + spot) & (spot < count)).astype(F32)
        active = (rank < micro).astype(F32)
        flag = jnp.stack([active, jnp.float32(2.0 / (micro * batch))]).reshape(1, 2)
        dmats, dion, scal = local_network(both[0], both[1], mine, times, feat, flag, mats, ion)
        dmats = lax.psum_scatter(dmats, "dp", scatter_dimension=1, tiled=True)
        dmats = lax.psum_scatter(dmats, "mp", scatter_dimension=2, tiled=True)
        dion = lax.psum_scatter(dion.T, ("mp", "dp"), scatter_dimension=0, tiled=True)
        hot = (jnp.arange(micro) == rank).astype(F32)
        squares = jnp.sum(dmats * dmats) + jnp.sum(dion * dion)
        total_sq, loss_sum, cost_sum = lax.psum(
            (squares, hot * scal[0, 0], jnp.where(place == 0, hot * scal[0, 1], 0.0)), ("dp", "mp")
        )
    grad_norm = jnp.sqrt(total_sq)
    scale = CLIP_NORM / jnp.maximum(grad_norm, CLIP_NORM)
    conv_grad, time_grad, attn_grad = unpack_mats(dmats)
    grads = (
        jnp.concatenate([dion[:, None, 0:SUB], dion[:, None, 16 : 16 + SUB]], axis=1).reshape(-1),
        conv_grad,
        time_grad,
        attn_grad,
        dion[:, 32 : 32 + SUB].reshape(-1),
    )
    weights = (io_weight, conv_weight, time_weight, attn_weight, norm_param)
    firsts = (io_first, conv_first, time_first, attn_first, norm_first)
    seconds = (io_second, conv_second, time_second, attn_second, norm_second)
    averages = (io_average, conv_average, time_average, attn_average, norm_average)
    results = [
        adam_update(weights[kind], firsts[kind], seconds[kind], averages[kind], grads[kind] * scale, RATES[kind])
        for kind in range(5)
    ]
    return tuple(results[kind][part] for part in range(4) for kind in range(5)) + (loss_sum, cost_sum, grad_norm)


def solution(mesh):
    flat = P(("mp", "dp"))
    state = (flat, P(None, None, "dp", "mp"), P(None, "dp", "mp"), P("dp", None, "mp"), flat)
    fused = mesh.shape["dp"] == Z * Y and mesh.shape["mp"] == X * C
    return jax.shard_map(
        functools.partial(body, fused),
        mesh=mesh,
        in_specs=(P("dp", None), P(None, "dp", None), P("dp"), P(None, "dp")) + state * 4,
        out_specs=state * 4 + (P(), P(), P()),
        check_vma=False,
    )
```

```python
import functools
import math

import jax
import numpy as np
import jax.numpy as jnp
from jax import lax
from jax.experimental import pallas as pl
from jax.experimental.pallas import tpu as pltpu
from jax.sharding import PartitionSpec as P

CH = 256
GROUPS = 32
HEADS = 4
HD = 64
SUB = 12
POS = 256
SIDE = 16
SINK = 10
NT = 1000
STEP = 5
MATS = 42
CONV_AT = (1, 10, 24, 33)
TIME_AT = (0, 23)
ATTN_AT = 19
CHUNKS = ((0, 5), (5, 5), (10, 5), (15, 4), (19, 4), (23, 5), (28, 5), (33, 5), (38, 4))
SPLITS = (5, 15, 28, 38)
EARLY = (4, 8)
PLAN = {
    "start": ("zero", "ot", "merge", "iz", "A4", "A8", "Z0", "Z1", "Z2", "Z3", "Z5", "Z6", "B4", "B8", "Z7", "iu",
        "otw"),
    "sink": ("E4", "iv", "E8", "U0"),
    "h0": ("ic", "U1", "U2", "iw"),
    "n0": ("V0", "U3"),
    "c0": ("U5", "V1", "V2", "U6", "C0", "U7", "V3", "V5", "C1", "W0", "W1"),
    "n1": ("C4", "C2", "V6"),
    "c1": ("V7", "C3", "W2", "W3"),
    "n2": ("C8", "C5"),
    "qkv": ("C6", "W4"),
    "at1": ("C7",),
    "c2": ("W5", "W6"),
    "c3": ("W7", "W8"),
    "w3b": ("R7",),
    "d3": ("R8",),
    "w2a": ("S7",),
    "w2b": ("R5", "S8"),
    "d2": ("R6",),
    "b3": ("S5",),
    "do": ("T7", "S6"),
    "bt1": ("T8", "T5"),
    "proj": ("Y7",),
    "b2": ("R4", "Y8", "T6", "Y5"),
    "w1a": ("S4",),
    "w1b": ("R2",),
    "d1": ("R3", "Y6", "X7"),
    "b1": ("S2", "T4", "S3", "F7", "X8", "X5"),
    "w0a": ("F8", "F5"),
    "w0b": ("R0", "X6"),
    "d0": ("R1", "T2"),
    "b0": ("Y4", "S0", "T3", "S1", "F6"),
    "win": ("Y2",),
    "tail": ("T0", "X4", "Y3", "F4", "T1", "X2", "Y0", "F2", "X3", "Y1", "F3", "X0", "F0", "X1"),
    "end": ("F1",),
}
LEVELS = 32000.0
MESH = pl.DeviceIdType.MESH


EPS_NORM = 1e-05
SINK_EPS = 0.01
CLIP_NORM = 1.0
BETA_ONE = 0.5
BETA_TWO = 0.5
ADAM_EPS = 1e-08
WEIGHT_DECAY = 0.01
EMA_DECAY = 0.9
RATES = (0.06, 0.01, 0.03, 0.03, 0.3)
F32 = jnp.float32
BF16 = jnp.bfloat16
ROWS = 32
PAD = SIDE
IMGS = 2
SPOTS = IMGS * POS


def dot(a, b, ca=1, cb=0):
    return lax.dot_general(a, b, (((ca,), (cb,)), ((), ())), preferred_element_type=F32)


def split3(v):
    one = v.astype(BF16)
    rest = v - one.astype(F32)
    two = rest.astype(BF16)
    three = (rest - two.astype(F32)).astype(BF16)
    return one, two, three


def group_sum(v):
    per = CH // GROUPS
    rows = lax.broadcasted_iota(jnp.int32, (CH, CH), 0) // per
    cols = lax.broadcasted_iota(jnp.int32, (CH, CH), 1) // per
    ones = jnp.where(rows == cols, 1.0, 0.0).astype(BF16)
    one, two, three = split3(v)
    got = dot(jnp.concatenate([one.astype(F32), two.astype(F32), three.astype(F32)], axis=0).astype(BF16), ones)
    n = v.shape[0]
    return got[:n] + got[n : 2 * n] + got[2 * n :]


def rows8(*rows):
    return jnp.concatenate(list(rows) + [jnp.zeros((8 - len(rows), CH), F32)], axis=0)


def for_blocks(step, init):
    return lax.fori_loop(0, POS // ROWS, lambda i, c: step(pl.multiple_of(i * ROWS, ROWS), c), init, unroll=True)


def norm_stats(field, stats, slot):
    zero = jnp.zeros((8, CH), F32)

    def fold(v):
        return v.reshape(ROWS // 8, 8, CH).sum(axis=0)

    sums = []
    for n in range(IMGS):
        acc = for_blocks(lambda at, c: c + fold(field[pl.ds(n * POS + at, ROWS), :]), zero)
        sums.append(jnp.sum(acc, axis=0, keepdims=True))
    scale = 1.0 / (POS * (CH // GROUPS))
    means = group_sum(rows8(*sums)) * scale
    sums = []
    for n in range(IMGS):
        mean = means[n : n + 1]

        def step(at, c):
            d = field[pl.ds(n * POS + at, ROWS), :] - mean
            return c + fold(d * d)

        sums.append(jnp.sum(for_blocks(step, zero), axis=0, keepdims=True))
    devs = group_sum(rows8(*sums)) * scale
    stats[slot, 0:8] = means
    stats[slot, 8:16] = lax.rsqrt(devs + EPS_NORM)


def put_shifts(pads, n, at, value):
    col = lax.broadcasted_iota(jnp.int32, value.shape, 0) % SIDE
    left = jnp.where(col == 0, 0.0, pltpu.roll(value, 1, 0))
    right = jnp.where(col == SIDE - 1, 0.0, pltpu.roll(value, value.shape[0] - 1, 0))
    rows = pl.ds(PAD + at, value.shape[0])
    pads[0, n, rows, :] = left.astype(BF16)
    pads[1, n, rows, :] = value.astype(BF16)
    pads[2, n, rows, :] = right.astype(BF16)


def tap(pads, r, c):
    return pads[c + 1, :, PAD + SIDE * r : PAD + SIDE * r + POS, :].reshape(SPOTS, CH)


OFFSETS = [(r, c) for r in (-1, 0, 1) for c in (-1, 0, 1)]


def train(
    x, z, mine, times, feats, active, step_scale, weights_small, mat, put, pump,
    dion_ref, scal_ref,
    h, flow, c1s, pads, acts, stats, start, goal, qkv, probs, mixed, tmp, smallf, dqkv,
):
    batch, depth = x.shape
    def gain(s):
        return ion[32 + 2 * s : 33 + 2 * s]

    def bias(s):
        return ion[33 + 2 * s : 34 + 2 * s]

    pump("pair")
    gram = dot(x, z, 1, 1)
    xf = x.astype(F32)
    zf = z.astype(F32)
    sq_x = jnp.sum(xf * xf, axis=1, keepdims=True)
    sq_z = jnp.sum(zf * zf, axis=1, keepdims=True)
    eye = lax.broadcasted_iota(jnp.int32, (batch, batch), 0) == lax.broadcasted_iota(jnp.int32, (batch, batch), 1)
    sq_z = jnp.sum(jnp.where(eye, sq_z, 0.0), axis=0, keepdims=True)
    cost = (sq_x + sq_z - 2.0 * gram) / depth
    affinity = 2.0 * gram / (depth * SINK_EPS)
    kern = jnp.exp(affinity - jnp.max(affinity, axis=1, keepdims=True))
    share = 1.0 / batch
    pump("sink")

    def sweep(i, c):
        left, right = c
        left = share / jnp.sum(kern * right, axis=1, keepdims=True)
        right = share / jnp.sum(left * kern, axis=0, keepdims=True)
        return left, right

    left, right = lax.fori_loop(0, SINK, sweep, (jnp.ones((batch, 1), F32), jnp.ones((1, batch), F32)))
    scaled = kern * right
    plan_cost = jnp.sum(left * scaled * cost)
    mixing = (scaled / jnp.sum(scaled, axis=1, keepdims=True)).astype(BF16)
    d = mine.astype(BF16)
    mix = dot(d, mixing).astype(BF16)
    paired = dot(mix, z)[0:IMGS]
    pixels = dot(d, x)[0:IMGS]
    inputs = ((1.0 - times) * paired + times * pixels).astype(BF16).astype(F32)
    target = pixels - paired
    start[...] = jnp.zeros_like(start)
    goal[...] = jnp.zeros_like(goal)
    for n in range(IMGS):
        for k in range(SUB):
            start[16 * n + k : 16 * n + k + 1, :] = inputs[n : n + 1, k * POS : (k + 1) * POS]
            goal[16 * n + k : 16 * n + k + 1, :] = target[n : n + 1, k * POS : (k + 1) * POS]
    begin = start[...].astype(BF16)

    for c in range(3):
        for n in range(IMGS):
            pads[c, n, 0:PAD, :] = jnp.zeros((PAD, CH), BF16)
            pads[c, n, PAD + POS :, :] = jnp.zeros((PAD, CH), BF16)

    def blocks(body):
        for n in range(IMGS):
            for_blocks(lambda at, c: (body(n, at), c)[1], 0)

    def norm_forward(field, slot, shifted, keep):
        norm_stats(field, stats, slot)
        g, b = gain(slot), bias(slot)

        def body(n, at):
            mean = stats[slot, n : n + 1]
            rstd = stats[slot, 8 + n : 9 + n]
            rows = pl.ds(n * POS + at, ROWS)
            y = (field[rows, :] - mean) * rstd * g + b
            if slot != 2:
                y = y * (1.0 / (1.0 + jnp.exp(-y)))
            acts[keep, rows, :] = y.astype(BF16)
            if shifted:
                put_shifts(pads, n, at, y)

        blocks(body)

    def conv(layer):
        acc = None
        for k, (r, c) in enumerate(OFFSETS):
            term = dot(tap(pads, r, c), mat(CONV_AT[layer] + k))
            acc = term if acc is None else acc + term
        return acc


    pump("h0")
    ion = weights_small()
    w_in = ion[0:16].astype(BF16)
    w_out = ion[16:32].astype(BF16)
    for n in range(IMGS):
        h[0, n * POS : (n + 1) * POS, :] = dot(begin[16 * n : 16 * n + 16], w_in, 0, 0)

    def residual(layer, slot, src, dst):
        pump(f"n{slot}")
        norm_forward(h.at[src], slot, True, slot)
        pump(f"c{2 * layer}")
        added = dot(feats, mat(TIME_AT[layer]))
        got = conv(2 * layer)
        for n in range(IMGS):
            c1s[layer, n * POS : (n + 1) * POS, :] = got[n * POS : (n + 1) * POS] + added[n : n + 1]
        pump(f"n{slot + 1}")
        norm_forward(c1s.at[layer], slot + 1, True, slot + 1)
        pump(f"c{2 * layer + 1}")
        h[dst] = h[src] + conv(2 * layer + 1)

    residual(0, 0, 0, 1)
    pump("n2")
    norm_forward(h.at[1], 2, False, 2)
    pump("qkv")
    normal = acts[2]
    for j in range(3):
        qkv[j] = dot(normal, mat(ATTN_AT + j)).astype(BF16)
    scale = HD ** (-0.5)

    def head_mask(hh):
        return lax.broadcasted_iota(jnp.int32, (POS, CH), 1) // HD == hh

    for n in range(IMGS):
        rows = slice(n * POS, (n + 1) * POS)
        pump(f"at{n}")
        tmp[...] = jnp.zeros_like(tmp)

        def head(hh, c):
            mask = head_mask(hh)
            q = jnp.where(mask, qkv[0, rows, :].astype(F32), 0.0).astype(BF16)
            scores = dot(q, qkv[1, rows, :], 1, 1) * scale
            e = jnp.exp(scores - jnp.max(scores, axis=1, keepdims=True))
            p = e / jnp.sum(e, axis=1, keepdims=True)
            probs[n, hh] = p
            o = dot(p.astype(BF16), qkv[2, rows, :])
            tmp[...] = jnp.where(mask, o, tmp[...])
            return c

        lax.fori_loop(0, HEADS, head, 0, unroll=HEADS)
        mixed[rows, :] = tmp[...].astype(BF16)
    pump("ao")
    h[2] = h[1] + dot(mixed[...], mat(ATTN_AT + 3), 1, 1)
    residual(1, 3, 2, 3)
    pump("n5")
    norm_forward(h.at[3], 5, False, 5)
    pump("head")

    dion_ref[...] = jnp.zeros_like(dion_ref)
    loss = jnp.zeros((), F32)
    for n in range(IMGS):
        rows = slice(n * POS, (n + 1) * POS)
        last = acts[5, rows, :]
        pred = dot(w_out, last, 1, 1)
        error = pred - goal[16 * n : 16 * n + 16, :]
        loss = loss + jnp.sum(error * error)
        low = (error * (step_scale * active)).astype(BF16)
        dion_ref[16:32, :] += dot(low, last)
        flow[rows, :] = dot(low, w_out, 0, 0)
    lane = lax.broadcasted_iota(jnp.int32, (8, 128), 1)
    scal_ref[...] = jnp.where(lane == 0, loss * active, jnp.where(lane == 1, plan_cost, 0.0))

    def norm_backward(field, slot, up, finish):
        g, b = gain(slot), bias(slot)
        zero = jnp.zeros((8, CH), F32)

        def fold(v):
            return v.reshape(ROWS // 8, 8, CH).sum(axis=0)

        dbs, dgs = [], []
        for n in range(IMGS):
            mean = stats[slot, n : n + 1]
            rstd = stats[slot, 8 + n : 9 + n]

            def step(at, c):
                rows = pl.ds(n * POS + at, ROWS)
                hat = (field[rows, :] - mean) * rstd
                dz = up[rows, :]
                if slot != 2:
                    y = hat * g + b
                    s = 1.0 / (1.0 + jnp.exp(-y))
                    dz = dz * (s * (1.0 + y * (1.0 - s)))
                    up[rows, :] = dz
                return (c[0] + fold(dz), c[1] + fold(dz * hat))

            db, dg = for_blocks(step, (zero, zero))
            dbs.append(jnp.sum(db, axis=0, keepdims=True))
            dgs.append(jnp.sum(dg, axis=0, keepdims=True))
        dion_ref[32 + 2 * slot : 33 + 2 * slot, :] = dgs[0] + dgs[1]
        dion_ref[33 + 2 * slot : 34 + 2 * slot, :] = dbs[0] + dbs[1]
        sums = group_sum(rows8(*[v * g for v in dbs + dgs])) * (1.0 / (POS * (CH // GROUPS)))
        for n in range(IMGS):
            mean = stats[slot, n : n + 1]
            rstd = stats[slot, 8 + n : 9 + n]
            m1 = sums[n : n + 1]
            m2 = sums[IMGS + n : IMGS + n + 1]

            def step(at, c):
                rows = pl.ds(n * POS + at, ROWS)
                hat = (field[rows, :] - mean) * rstd
                finish(n, at, rstd * (up[rows, :] * g - m1 - hat * m2))
                return c

            for_blocks(step, 0)

    def conv_backward(layer, keep):
        turned = acts[keep].T
        pump(f"w{layer}a")
        for k, (r, c) in enumerate(OFFSETS):
            put(CONV_AT[layer] + k, dot(turned, tap(pads, -r, -c)))
            if CONV_AT[layer] + k + 1 in SPLITS:
                pump(f"w{layer}b")
        pump(f"d{layer}")
        acc = None
        for k, (r, c) in enumerate(OFFSETS):
            term = dot(tap(pads, -r, -c), mat(CONV_AT[layer] + k), 1, 1)
            acc = term if acc is None else acc + term
        smallf[...] = acc

    def add_flow(shifted):
        def finish(n, at, dx):
            rows = pl.ds(n * POS + at, ROWS)
            total = flow[rows, :] + dx
            flow[rows, :] = total
            if shifted:
                put_shifts(pads, n, at, total)

        return finish

    def set_flow(n, at, dx):
        rows = pl.ds(n * POS + at, ROWS)
        flow[rows, :] = dx
        put_shifts(pads, n, at, dx)

    def only_shifts(n, at, dx):
        put_shifts(pads, n, at, dx)

    def residual_backward(layer, slot, src, last_one):
        conv_backward(2 * layer + 1, slot + 1)
        pump(f"b{slot + 1}")
        norm_backward(c1s.at[layer], slot + 1, smallf, only_shifts)
        sums = []
        for n in range(IMGS):
            low = pads[1, n, PAD : PAD + POS, :].astype(F32)
            sums.append(jnp.sum(low, axis=0, keepdims=True))
        one, two, three = split3(rows8(*sums))
        stack = jnp.concatenate([v.astype(F32) for v in (one, two, three)], axis=0).astype(BF16)
        feats3 = jnp.concatenate([feats.astype(F32)] * 3, axis=0).astype(BF16)
        put(TIME_AT[layer], dot(feats3, stack, 0, 0))
        conv_backward(2 * layer, slot)
        pump(f"b{slot}")
        norm_backward(h.at[src], slot, smallf, add_flow(False))

    pump("b5")
    norm_backward(h.at[3], 5, flow, set_flow)
    residual_backward(1, 3, 2, False)

    pump("do")
    dy = flow[...].astype(BF16)
    put(ATTN_AT + 3, dot(dy.T, mixed[...]))
    dqkv[3] = dot(dy, mat(ATTN_AT + 3)).astype(BF16)
    for n in range(IMGS):
        rows = slice(n * POS, (n + 1) * POS)
        pump(f"bt{n}")
        for j in range(3):
            smallf[j % 2 * POS : j % 2 * POS + POS, :] = jnp.zeros((POS, CH), F32)
        tmp[...] = jnp.zeros_like(tmp)

        def head(hh, c):
            mask = head_mask(hh)
            do = jnp.where(mask, dqkv[3, rows, :].astype(F32), 0.0).astype(BF16)
            q = jnp.where(mask, qkv[0, rows, :].astype(F32), 0.0).astype(BF16)
            p = probs[n, hh]
            dp = dot(do, qkv[2, rows, :], 1, 1)
            ds = (p * (dp - jnp.sum(p * dp, axis=1, keepdims=True))).astype(BF16)
            tmp[...] = jnp.where(mask, dot(ds, qkv[1, rows, :]), tmp[...])
            smallf[0:POS, :] += dot(ds, q, 0, 0)
            smallf[POS:, :] += dot(p.astype(BF16), do, 0, 0)
            return c

        lax.fori_loop(0, HEADS, head, 0, unroll=HEADS)
        dqkv[0, rows, :] = (tmp[...] * scale).astype(BF16)
        dqkv[1, rows, :] = (smallf[0:POS, :] * scale).astype(BF16)
        dqkv[2, rows, :] = smallf[POS:, :].astype(BF16)
    pump("proj")
    turned = acts[2].T
    acc = None
    for j in range(3):
        put(ATTN_AT + j, dot(turned, dqkv[j]))
        term = dot(dqkv[j], mat(ATTN_AT + j), 1, 1)
        acc = term if acc is None else acc + term
    smallf[...] = acc
    pump("b2")
    norm_backward(h.at[1], 2, smallf, add_flow(True))
    residual_backward(0, 0, 0, True)
    pump("win")
    for n in range(IMGS):
        rows = slice(n * POS, (n + 1) * POS)
        dion_ref[0:16, :] += dot(begin[16 * n : 16 * n + 16], flow[rows, :].astype(BF16))


def work_space():
    return [
        pltpu.VMEM((4, SPOTS, CH), F32),
        pltpu.VMEM((SPOTS, CH), F32),
        pltpu.VMEM((2, SPOTS, CH), F32),
        pltpu.VMEM((3, IMGS, POS + 2 * PAD, CH), BF16),
        pltpu.VMEM((6, SPOTS, CH), BF16),
        pltpu.VMEM((6, 16, CH), F32),
        pltpu.VMEM((16 * IMGS, POS), F32),
        pltpu.VMEM((16 * IMGS, POS), F32),
        pltpu.VMEM((3, SPOTS, CH), BF16),
        pltpu.VMEM((IMGS, HEADS, POS, POS), F32),
        pltpu.VMEM((SPOTS, CH), BF16),
        pltpu.VMEM((POS, CH), F32),
        pltpu.VMEM((SPOTS, CH), F32),
        pltpu.VMEM((4, SPOTS, CH), BF16),
    ]


def local_kernel(x_ref, z_ref, mine_ref, when_ref, feat_ref, flag_ref, mats, ion_ref, dmats, dion_ref, scal_ref, *work):
    def put(m, value):
        dmats[m] = value

    train(
        x_ref[...], z_ref[...], mine_ref[...], when_ref[0:IMGS, 0:1], feat_ref[...].astype(BF16),
        flag_ref[0, 0], flag_ref[0, 1],
        lambda: ion_ref[...].T, lambda m: mats[m], put, lambda name: None,
        dion_ref, scal_ref, *work,
    )


def local_network(x, z, mine, when, feat, flag, mats, ion):
    whole = pl.BlockSpec(memory_space=pltpu.VMEM)
    return pl.pallas_call(
        local_kernel,
        out_shape=(
            jax.ShapeDtypeStruct((MATS, CH, CH), F32),
            jax.ShapeDtypeStruct((48, CH), F32),
            jax.ShapeDtypeStruct((8, 128), F32),
        ),
        in_specs=[whole] * 5 + [pl.BlockSpec(memory_space=pltpu.SMEM)] + [whole] * 2,
        out_specs=(whole, whole, whole),
        scratch_shapes=work_space(),
        compiler_params=pltpu.CompilerParams(vmem_limit_bytes=56 * 2**20),
    )(x, z, mine, when, feat, flag, mats, ion)


Z, Y, X, C = 4, 2, 2, 2
DEVICES = Z * Y * X * C


def fused_kernel(
    micro, batch,
    order_ref, when_ref, images_ref, noises_ref, freq_ref, conv_ref, time_ref, attn_ref, io_ref, norm_ref,
    grads_ref, gion_ref, total_ref,
    mats, dmats, other, give, land, ottmp, ot_ref, otbuf, otwide, xz, ionbuf, dion, diont, ionr, scal, scalr,
    s1q, s1r, s2q, s2r, zq, zr, expo, kept, gother,
    ot_s, ot_r, ion_s, ion_r, g_s, g_r, r_s, r_r, d_s, d_r, n_s, n_r,
    *work,
):
    dp = lax.axis_index("dp")
    mp = lax.axis_index("mp")
    z, y, x, c = dp // Y, dp % Y, mp // C, mp % C
    flat = mp * (Z * Y) + dp

    def place(z_, y_, x_, c_):
        return (z_ * Y + y_, x_ * C + c_)

    def from_flat(f):
        return (f % (Z * Y), f // (Z * Y))

    sibling = place(z, y, x, 1 - c)
    first = place(z, y * c + (1 - y) * (1 - c), x * (1 - c) + (1 - x) * c, c)
    second = place(z, (1 - y) * c + y * (1 - c), (1 - x) * (1 - c) + x * c, c)

    def remote(src, dst, send, recv, where):
        return pltpu.make_async_remote_copy(
            src_ref=src, dst_ref=dst, send_sem=send, recv_sem=recv, device_id=where, device_id_type=MESH
        )

    barrier = pltpu.get_barrier_semaphore()

    def greet(j, carry):
        pl.semaphore_signal(
            barrier, inc=1, device_id=from_flat((flat + j) % DEVICES), device_id_type=MESH
        )
        return carry

    lax.fori_loop(1, DEVICES, greet, 0)

    def wide(v):
        v = v.astype(BF16).astype(F32)
        none = jnp.zeros_like(v)
        return jnp.where(c == 0, jnp.concatenate([v, none], axis=1), jnp.concatenate([none, v], axis=1)).astype(BF16)

    def pack(m, whole):
        mats[m, x, z, y, c] = wide(jnp.where(c == 0, whole[0:16], whole[16:32]))
        give[m] = wide(jnp.where(c == 0, whole[16:32], whole[0:16]))

    for layer, at in enumerate(CONV_AT):

        def pack_step(k, carry):
            pack(at + k, conv_ref[layer, k])
            return carry

        lax.fori_loop(0, 9, pack_step, 0)
    for layer, at in enumerate(TIME_AT):
        pack(at, time_ref[layer])
    for j in range(4):
        pack(ATTN_AT + j, attn_ref[:, j, :])

    turn = mp - (mp // micro) * (mp - micro + 1)
    row = lax.broadcasted_iota(jnp.int32, (8, images_ref.shape[0]), 0)
    column = lax.broadcasted_iota(jnp.int32, (8, images_ref.shape[0]), 1)
    pick = jnp.zeros(row.shape, F32)
    for n in range(IMGS):
        pick = jnp.where((row == n) & (column == order_ref[turn * IMGS + n]), 1.0, pick)
    own_x = dot(pick.astype(BF16), images_ref[...])
    own_z = noises_ref[turn].astype(F32)
    lines = SUB * POS // 128
    for k in range(lines):
        ottmp[2 * IMGS * k : 2 * IMGS * k + IMGS, :] = own_x[0:IMGS, 128 * k : 128 * k + 128]
        ottmp[2 * IMGS * k + IMGS : 2 * IMGS * (k + 1), :] = own_z[:, 128 * k : 128 * k + 128]
    ot_ref[...] = ottmp[...].astype(BF16)
    io = io_ref[...].reshape(1, io_ref.shape[0])
    norm = norm_ref[...].reshape(1, norm_ref.shape[0])
    zero_row = jnp.zeros((1, 128), F32)
    packed = []
    for r in range(8):
        gap = zero_row[:, 0 : 16 - SUB]
        at = 2 * SUB * r
        packed.append(
            jnp.concatenate(
                [io[:, at : at + SUB], gap, io[:, at + SUB : at + 2 * SUB], gap,
                 norm[:, SUB * r : SUB * r + SUB], zero_row[:, 0 : 128 - 32 - SUB]], axis=1
            )
        )
    ionbuf[x, c, z, y] = jnp.concatenate(packed, axis=0).astype(BF16).astype(F32)
    pl.semaphore_wait(barrier, DEVICES - 1)

    zero_copy = remote(give, land, g_s.at[0, 0], g_r.at[0, 0], sibling)
    def ot_copy(j):
        there = (dp + j) % (Z * Y)
        return remote(ot_ref, otbuf.at[dp], ot_s.at[j], ot_r.at[j], (there, mp))

    def ion_z(j):
        part = ionbuf.at[x, c, z, y]
        return remote(part, part, ion_s.at[j], ion_r.at[j], place((z + j) % Z, y, x, c))

    def ion_u(core):
        part = ionbuf.at[x, c, :, y]
        return remote(part, part, ion_s.at[4], ion_r.at[4], first)

    def ion_v(core):
        part = ionbuf.at[x, 0] if core == 0 else ionbuf.at[:, 1, :, y]
        return remote(part, part, ion_s.at[5], ion_r.at[5], second)

    def ion_c(core):
        part = ionbuf.at[:, c]
        return remote(part, part, ion_s.at[6], ion_r.at[6], sibling)

    def merge(m, carry):
        mats[m, x, z, y, c] = mats[m, x, z, y, c] + land[m]
        return carry

    def span(i):
        return pl.ds(CHUNKS[i][0], CHUNKS[i][1])

    def z_copy(i, j):
        part = mats.at[span(i), x, z, y, c]
        return remote(part, part, g_s.at[i + 1, j], g_r.at[i + 1, j], place((z + j) % Z, y, x, c))

    def u_copy(i):
        part = mats.at[span(i), x, :, y, c]
        return remote(part, part, g_s.at[i + 1, 4], g_r.at[i + 1, 4], first)

    def v_copy(i, core):
        part = mats.at[span(i), x, :, :, 0] if core == 0 else mats.at[span(i), :, :, y, 1]
        return remote(part, part, g_s.at[i + 1, 5], g_r.at[i + 1, 5], second)

    def e_copy(i, j):
        part = mats.at[span(i), :, z, :, c]
        return remote(part, part, g_s.at[i + 1, j], g_r.at[i + 1, j], place((z + j) % Z, y, x, c))

    def a_copy(i):
        part = mats.at[span(i), x, z, y, c]
        return remote(part, part, g_s.at[i + 1, 4], g_r.at[i + 1, 4], first)

    def b_copy(i, core):
        part = mats.at[span(i), x, z, :, 0] if core == 0 else mats.at[span(i), :, z, y, 1]
        return remote(part, part, g_s.at[i + 1, 5], g_r.at[i + 1, 5], second)

    def c_copy(i):
        part = mats.at[span(i), :, :, :, c]
        return remote(part, part, g_s.at[i + 1, 6], g_r.at[i + 1, 6], sibling)

    def on_core(act):
        for core in range(C):
            pl.when(c == core)(functools.partial(act, core))

    def start_all(copies):
        for copy in copies:
            copy.start()

    def wait_all(copies):
        for copy in copies:
            copy.wait()

    peers = range(1, Z)

    def gather_step(kind, i):
        if kind == "A":
            a_copy(i).start()
        elif kind == "B":
            a_copy(i).wait()
            on_core(lambda core: b_copy(i, core).start())
        elif kind == "E":
            on_core(lambda core: b_copy(i, core).wait())
            start_all(e_copy(i, j) for j in peers)
        elif kind == "Z":
            start_all(z_copy(i, j) for j in peers)
        elif kind == "U":
            wait_all(z_copy(i, j) for j in peers)
            u_copy(i).start()
        elif kind == "V":
            u_copy(i).wait()
            on_core(lambda core: v_copy(i, core).start())
        elif kind == "C":
            if i in EARLY:
                wait_all(e_copy(i, j) for j in peers)
            else:
                on_core(lambda core: v_copy(i, core).wait())
            c_copy(i).start()
        elif kind == "W":
            c_copy(i).wait()

    def other_step(kind):
        if kind == "zero":
            zero_copy.start()
        elif kind == "merge":
            zero_copy.wait()
            lax.fori_loop(0, MATS, merge, 0, unroll=6)
        elif kind == "ot":
            start_all(ot_copy(j) for j in range(1, Z * Y))
            otbuf[dp] = ot_ref[...]
        elif kind == "otw":
            wait_all(ot_copy(j) for j in range(1, Z * Y))
        elif kind == "iz":
            start_all(ion_z(j) for j in peers)
        elif kind == "iu":
            wait_all(ion_z(j) for j in peers)
            ion_u(0).start()
        elif kind == "iv":
            ion_u(0).wait()
            on_core(lambda core: ion_v(core).start())
        elif kind == "ic":
            on_core(lambda core: ion_v(core).wait())
            ion_c(0).start()
        elif kind == "iw":
            ion_c(0).wait()

    def do(steps):
        for kind in steps:
            if kind[1:].isdigit():
                i = int(kind[1:])
                if kind[0] in "RSTYXF":
                    reduce_step(kind[0], i)
                else:
                    gather_step(kind[0], i)
            else:
                other_step(kind)

    def pump(name):
        do(PLAN.get(name, ()))

    pump("start")
    rows = ot_ref.shape[0]
    for j in range(Z * Y):
        otwide[pl.ds(j * rows, rows), :] = otbuf[j].astype(F32)
    for r in range(2 * IMGS):
        for k in range(lines):
            xz[r // IMGS, (r % IMGS) * Z * Y : (r % IMGS + 1) * Z * Y, k * 128 : (k + 1) * 128] = otwide[
                pl.ds(k * 2 * IMGS + r, Z * Y, stride=rows), :
            ]
    spot = lax.broadcasted_iota(jnp.int32, (8, batch), 0)
    column = lax.broadcasted_iota(jnp.int32, (8, batch), 1)
    mine = jnp.where((column == spot * (Z * Y) + dp) & (spot < IMGS), 1.0, 0.0)
    active = jnp.where(mp < micro, 1.0, 0.0)

    def mat(m):
        return jnp.concatenate([mats[m, k].reshape(CH, 128) for k in range(X)], axis=1)

    def put(m, value):
        for k in range(X):
            dmats[m, k] = value[:, 128 * k : 128 * k + 128].reshape(Z, Y, C, 16, 128)

    mine_a = x * (1 - c) + y * c
    mine_b = y * (1 - c) + x * c

    def xy(a, b):
        return a * (1 - c) + b * c, b * (1 - c) + a * c

    def r_copy(i):
        return remote(
            dmats.at[span(i), :, :, :, 1 - c], other.at[span(i)], r_s.at[i, 0], r_r.at[i, 0], sibling
        )

    def base(i, per):
        return CHUNKS[i][0] * per + i

    def one_copy(i):
        part = pl.ds(base(i, 8), CHUNKS[i][1] * 8 + 1)
        return remote(s1q.at[part], s1r.at[part], r_s.at[i, 1], r_r.at[i, 1], second)

    def two_copy(i):
        part = pl.ds(base(i, 4), CHUNKS[i][1] * 4 + 1)
        return remote(s2q.at[part], s2r.at[part], r_s.at[i, 2], r_r.at[i, 2], first)

    def three_copy(i, j):
        part = pl.ds(base(i, 1), CHUNKS[i][1] + 1)
        return remote(
            zq.at[j - 1, part], zr.at[j - 1, part], r_s.at[i, 2 + j], r_r.at[i, 2 + j], place((z + j) % Z, y, x, c)
        )

    def four_copy(i):
        return remote(kept.at[span(i)], gother.at[span(i)], r_s.at[i, 6], r_r.at[i, 6], sibling)

    def exponent(tiles):
        top = jnp.max(jnp.abs(tiles[0]), axis=0, keepdims=True)
        for t in tiles[1:]:
            top = jnp.maximum(top, jnp.max(jnp.abs(t), axis=0, keepdims=True))
        return jnp.floor(jnp.log2(jnp.maximum(top, 1e-30))) + 1.0

    def coded(tile, power):
        return jnp.round(tile * (LEVELS * jnp.exp2(-power))).astype(jnp.int32).astype(jnp.int16)

    def decoded(tile, unit):
        return tile.astype(jnp.int32).astype(F32) * unit

    def units(ref, at, slot):
        expo[slot] = jnp.exp2(ref[at].astype(jnp.int32).astype(F32)) * (1.0 / LEVELS)

    def powers(ref, at):
        ref[at] = expo[0].astype(jnp.int32).astype(jnp.int16)

    def stage_one(i):
        r_copy(i).wait()
        first_m, count = CHUNKS[i]
        start = base(i, 8)

        def step(k, carry):
            m = first_m + k
            tiles = []
            for b in range(2):
                x_, y_ = xy(1 - mine_a, b)
                for zz in range(Z):
                    tiles.append(dmats[m, x_, zz, y_, c] + other[m, x_, zz, y_])
            power = exponent(tiles)
            expo[0, pl.ds(k, 1), :] = power
            for t, tile in enumerate(tiles):
                s1q[start + k * 8 + t] = coded(tile, power)
            return carry

        lax.fori_loop(0, count, step, 0, unroll=True)
        powers(s1q, start + count * 8)
        one_copy(i).start()

    def stage_two(i):
        one_copy(i).wait()
        first_m, count = CHUNKS[i]
        start, start_one = base(i, 4), base(i, 8)
        units(s1r, start_one + count * 8, 1)

        def step(k, carry):
            m = first_m + k
            unit = expo[1, pl.ds(k, 1), :]
            x_, y_ = xy(mine_a, 1 - mine_b)
            tiles = []
            for zz in range(Z):
                got = decoded(s1r[start_one + k * 8 + (1 - mine_b) * 4 + zz], unit)
                tiles.append(dmats[m, x_, zz, y_, c] + other[m, x_, zz, y_] + got)
            power = exponent(tiles)
            expo[0, pl.ds(k, 1), :] = power
            for t, tile in enumerate(tiles):
                s2q[start + k * 4 + t] = coded(tile, power)
            return carry

        lax.fori_loop(0, count, step, 0, unroll=True)
        powers(s2q, start + count * 4)
        two_copy(i).start()

    def stage_three(i):
        two_copy(i).wait()
        first_m, count = CHUNKS[i]
        start, start_one, start_two = base(i, 1), base(i, 8), base(i, 4)
        units(s1r, start_one + count * 8, 1)
        units(s2r, start_two + count * 4, 2)

        def step(k, carry):
            m = first_m + k
            unit_one = expo[1, pl.ds(k, 1), :]
            unit_two = expo[2, pl.ds(k, 1), :]

            def tile(zz):
                return (
                    dmats[m, x, zz, y, c]
                    + other[m, x, zz, y]
                    + decoded(s1r[start_one + k * 8 + mine_b * 4 + zz], unit_one)
                    + decoded(s2r[start_two + k * 4 + zz], unit_two)
                )

            tiles = [tile((z + j) % Z) for j in range(1, Z)]
            power = exponent(tiles)
            expo[0, pl.ds(k, 1), :] = power
            for j in range(1, Z):
                zq[j - 1, start + k] = coded(tiles[j - 1], power)
            kept[m] = tile(z)
            return carry

        lax.fori_loop(0, count, step, 0, unroll=True)
        for j in range(1, Z):
            powers(zq.at[j - 1], start + count)
        for j in range(1, Z):
            three_copy(i, j).start()

    def stage_four(i):
        for j in range(1, Z):
            three_copy(i, j).wait()
        first_m, count = CHUNKS[i]
        start = base(i, 1)
        for j in range(1, Z):
            units(zr.at[j - 1], start + count, j)

        def step(k, carry):
            m = first_m + k
            total = kept[m]
            for j in range(1, Z):
                total = total + decoded(zr[j - 1, start + k], expo[j, pl.ds(k, 1), :])
            kept[m] = total
            return carry + total * total

        square = lax.fori_loop(0, count, step, jnp.zeros((16, 128), F32), unroll=True)
        four_copy(i).start()
        return square

    squares = []

    def reduce_step(kind, i):
        if kind == "R":
            r_copy(i).start()
        elif kind == "S":
            stage_one(i)
        elif kind == "T":
            stage_two(i)
        elif kind == "Y":
            stage_three(i)
        elif kind == "X":
            squares.append(stage_four(i))
        else:
            finish(i)

    def finish(i):
        four_copy(i).wait()

        def step(k, carry):
            m = CHUNKS[i][0] + k
            for half in range(C):
                tile = jnp.where(c == half, kept[m], gother[m])
                grads_ref[m, half * 16 : half * 16 + 16, :] = jnp.where(c == 0, tile[:, 0:64], tile[:, 64:128])
            return carry

        lax.fori_loop(0, CHUNKS[i][1], step, 0, unroll=True)

    seat = lax.broadcasted_iota(jnp.int32, (8, 1), 0)
    times = jnp.zeros((8, 1), F32)
    for n in range(IMGS):
        index = when_ref[pl.ds(turn, 1), n : n + 1].astype(F32)
        times = jnp.where(seat == n, (index + 0.5) / NT, times)
    angles = 1000.0 * times * freq_ref[...]
    feats = jnp.where(seat < IMGS, jnp.concatenate([jnp.sin(angles), jnp.cos(angles)], axis=1), 0.0).astype(BF16)
    train(
        xz[0].astype(BF16), xz[1].astype(BF16), mine, times[0:IMGS], feats, active, 2.0 / (micro * batch),
        lambda: ionbuf[...].reshape(CH, 128).T, mat, put, pump, dion, scal, *work,
    )

    diont[...] = jnp.concatenate([dion[...], jnp.zeros((128 - 48, CH), F32)], axis=0).T.reshape(DEVICES, 8, 128)

    def dion_copy(j):
        there = (flat + j) % DEVICES
        return remote(diont.at[there], ionr.at[flat], d_s.at[j], d_r.at[j], from_flat(there))

    def dion_start(j, carry):
        dion_copy(j).start()
        return carry

    lax.fori_loop(1, DEVICES, dion_start, 0)
    ionr[flat] = diont[flat]
    pump("tail")

    def dion_wait(j, carry):
        dion_copy(j).wait()
        return carry

    lax.fori_loop(1, DEVICES, dion_wait, 0)
    small = jnp.sum(ionr[...], axis=0)
    gion_ref[...] = small
    square = jnp.sum(small * small)
    for part in squares:
        square = square + jnp.sum(part)

    loss, plan_cost = scal[0:1, 0:1], scal[0:1, 1:2]
    lane = lax.broadcasted_iota(jnp.int32, (8, 128), 1)
    tile = jnp.where(lane == 0, square, 0.0)
    tile = jnp.where(lane == 1 + mp, loss, tile)
    tile = jnp.where((lane == 1 + micro + mp) & (mp < micro) & (dp == 0), plan_cost, tile)
    tile = jnp.where((mp >= micro) & (lane > 0), 0.0, tile)
    scal[...] = tile
    scalr[flat] = tile

    def n_copy(j):
        return remote(scal, scalr.at[flat], n_s.at[j], n_r.at[j], from_flat((flat + j) % DEVICES))

    def n_start(j, carry):
        n_copy(j).start()
        return carry

    def n_wait(j, carry):
        n_copy(j).wait()
        return carry

    lax.fori_loop(1, DEVICES, n_start, 0)
    pump("end")
    lax.fori_loop(1, DEVICES, n_wait, 0)
    total_ref[...] = jnp.sum(scalr[...], axis=0)


def fused_network(micro, batch, order, when, images, noises, conv, time, attn, io, norm):
    whole = pl.BlockSpec(memory_space=pltpu.VMEM)
    scalar = pl.BlockSpec(memory_space=pltpu.SMEM)
    blocks = (X, Z, Y)
    rows = 2 * IMGS * SUB * POS // 128
    dma = pltpu.SemaphoreType.DMA
    count = len(CHUNKS)
    half = CH // 2
    freq = np.exp(np.float32(-math.log(10000.0)) * np.arange(half, dtype=np.float32) / np.float32(half))
    freq = jnp.asarray(freq.reshape(1, half))
    return pl.pallas_call(
        functools.partial(fused_kernel, micro, batch),
        out_shape=(
            jax.ShapeDtypeStruct((MATS, 32, 64), F32),
            jax.ShapeDtypeStruct((8, 128), F32),
            jax.ShapeDtypeStruct((8, 128), F32),
        ),
        in_specs=[scalar] + [whole] * 9,
        out_specs=(whole, whole, whole),
        scratch_shapes=[
            pltpu.VMEM((MATS,) + blocks + (C, 16, 128), BF16),
            pltpu.VMEM((MATS,) + blocks + (C, 16, 128), F32),
            pltpu.VMEM((MATS,) + blocks + (16, 128), F32),
            pltpu.VMEM((MATS, 16, 128), BF16),
            pltpu.VMEM((MATS, 16, 128), BF16),
            pltpu.VMEM((rows, 128), F32),
            pltpu.VMEM((rows, 128), BF16),
            pltpu.VMEM((Z * Y, rows, 128), BF16),
            pltpu.VMEM((Z * Y * rows, 128), F32),
            pltpu.VMEM((2, batch, SUB * POS), F32),
            pltpu.VMEM((X, C, Z, Y, 8, 128), F32),
            pltpu.VMEM((48, CH), F32),
            pltpu.VMEM((DEVICES, 8, 128), F32),
            pltpu.VMEM((DEVICES, 8, 128), F32),
            pltpu.VMEM((8, 128), F32),
            pltpu.VMEM((DEVICES, 8, 128), F32),
            pltpu.VMEM((MATS * 8 + count, 16, 128), jnp.int16),
            pltpu.VMEM((MATS * 8 + count, 16, 128), jnp.int16),
            pltpu.VMEM((MATS * 4 + count, 16, 128), jnp.int16),
            pltpu.VMEM((MATS * 4 + count, 16, 128), jnp.int16),
            pltpu.VMEM((Z - 1, MATS + count, 16, 128), jnp.int16),
            pltpu.VMEM((Z - 1, MATS + count, 16, 128), jnp.int16),
            pltpu.VMEM((Z, 16, 128), F32),
            pltpu.VMEM((MATS, 16, 128), F32),
            pltpu.VMEM((MATS, 16, 128), F32),
            dma((Z * Y,)), dma((Z * Y,)),
            dma((7,)), dma((7,)),
            dma((count + 1, 7)), dma((count + 1, 7)),
            dma((count, 7)), dma((count, 7)),
            dma((DEVICES,)), dma((DEVICES,)),
            dma((DEVICES,)), dma((DEVICES,)),
        ] + work_space(),
        compiler_params=pltpu.CompilerParams(
            vmem_limit_bytes=60 * 2**20, collective_id=0, has_side_effects=True
        ),
    )(order, when, images, noises, freq, conv, time, attn, io, norm)


def time_features(time_index):
    times = (time_index.astype(jnp.float32) + 0.5) / NT
    half = CH // 2
    frequency = jnp.exp(-math.log(10000.0) * jnp.arange(half, dtype=jnp.float32) / half)
    angles = 1000.0 * times[:, None] * frequency[None, :]
    return jnp.concatenate([jnp.sin(angles), jnp.cos(angles)], axis=1)


def adam_update(weight, first, second, average, gradient, rate):
    first = BETA_ONE * first + (1 - BETA_ONE) * gradient
    second = BETA_TWO * second + (1 - BETA_TWO) * gradient * gradient
    ratio = first / (1 - BETA_ONE**STEP) / (jnp.sqrt(second / (1 - BETA_TWO**STEP)) + ADAM_EPS)
    weight = weight - rate * (ratio + WEIGHT_DECAY * weight)
    average = EMA_DECAY * average + (1 - EMA_DECAY) * weight
    return (weight, first, second, average)


def adam_kernel(grads_ref, gion_ref, total_ref, *refs):
    step = pl.program_id(0)
    old, new = refs[:20], refs[20:40]
    loss_ref, cost_ref, norm_ref = refs[40:]
    norm = jnp.sqrt(total_ref[0:1, 0:1])
    scale = CLIP_NORM / jnp.maximum(norm, CLIP_NORM)

    def update(kind, at, gradient):
        got = adam_update(*[old[5 * part + kind][at] for part in range(4)], gradient * scale, RATES[kind])
        for part in range(4):
            new[5 * part + kind][at] = got[part]

    for layer, start in enumerate(CONV_AT):

        @pl.when(step == layer)
        def conv_step():
            update(1, (0,), grads_ref[start : start + 9])

    @pl.when(step == 0)
    def others():
        for layer, start in enumerate(TIME_AT):
            update(2, (layer,), grads_ref[start])
        for j in range(4):
            update(3, (slice(None), j), grads_ref[ATTN_AT + j])
        tile = gion_ref[...]
        own = old[0].shape[0] // (2 * SUB)
        for kind, pieces in ((0, (0, 16)), (4, (32,))):
            flat = [tile[r : r + 1, at : at + SUB] for r in range(own) for at in pieces]
            flat = jnp.concatenate(flat, axis=1)
            got = adam_update(
                *[old[5 * part + kind][...].reshape(flat.shape) for part in range(4)], flat * scale, RATES[kind]
            )
            for part in range(4):
                new[5 * part + kind][...] = got[part].reshape(old[kind].shape)
        micro = loss_ref.shape[0]
        for m in range(micro):
            loss_ref[m] = total_ref[0, 1 + m]
            cost_ref[m] = total_ref[0, 1 + micro + m]
        norm_ref[0] = norm[0, 0]


def adam(micro, grads, gion, total, state):
    whole = pl.BlockSpec(memory_space=pltpu.VMEM)
    scalar = pl.BlockSpec(memory_space=pltpu.SMEM)

    def spec(v):
        if v.ndim == 4:
            return pl.BlockSpec((1,) + v.shape[1:], lambda i: (i, 0, 0, 0))
        return pl.BlockSpec(v.shape, lambda i: (0,) * v.ndim)

    return pl.pallas_call(
        adam_kernel,
        grid=(len(CONV_AT),),
        out_shape=tuple(jax.ShapeDtypeStruct(v.shape, F32) for v in state)
        + (jax.ShapeDtypeStruct((micro,), F32),) * 2
        + (jax.ShapeDtypeStruct((1,), F32),),
        in_specs=[spec(v) for v in (grads, gion, total)] + [spec(v) for v in state],
        out_specs=tuple(spec(v) for v in state) + (scalar,) * 3,
        compiler_params=pltpu.CompilerParams(vmem_limit_bytes=60 * 2**20),
    )(grads, gion, total, *state)


def pack_mats(conv, time, attn):
    return jnp.concatenate(
        [time[0:1], conv[0], conv[1], attn.transpose(1, 0, 2), time[1:2], conv[2], conv[3]], axis=0
    )


def unpack_mats(mats):
    conv = jnp.stack([mats[at : at + 9] for at in CONV_AT])
    time = jnp.stack([mats[at] for at in TIME_AT])
    return conv, time, mats[ATTN_AT : ATTN_AT + 4].transpose(1, 0, 2)


def pack_small(io, norm):
    own = norm.shape[0] // SUB
    io = io.reshape(own, 2, SUB)
    norm = norm.reshape(own, SUB)
    gap = jnp.zeros((own, 16 - SUB), io.dtype)
    return jnp.concatenate(
        [io[:, 0], gap, io[:, 1], gap, norm, gap, jnp.zeros((own, 80), io.dtype)], axis=1
    )


def body(
    fused,
    images, noises, order, time_index, io_weight, conv_weight, time_weight, attn_weight, norm_param,
    io_first, conv_first, time_first, attn_first, norm_first,
    io_second, conv_second, time_second, attn_second, norm_second,
    io_average, conv_average, time_average, attn_average, norm_average,
):
    rank = lax.axis_index("mp")
    place = lax.axis_index("dp")
    micro, count, depth = noises.shape
    batch = count * lax.axis_size("dp")
    turn = jnp.minimum(rank, micro - 1)
    weights = (io_weight, conv_weight, time_weight, attn_weight, norm_param)
    firsts = (io_first, conv_first, time_first, attn_first, norm_first)
    seconds = (io_second, conv_second, time_second, attn_second, norm_second)
    averages = (io_average, conv_average, time_average, attn_average, norm_average)
    if fused:
        grads, gion, total = fused_network(
            micro, batch, order, time_index, images, noises, conv_weight, time_weight, attn_weight, io_weight, norm_param
        )
        out = adam(micro, grads, gion, total, weights + firsts + seconds + averages)
        return out[:22] + (out[22].reshape(()),)
    chosen = lax.dynamic_slice_in_dim(order, turn * count, count, 0)
    own_x = jnp.take(images, chosen, axis=0)
    own_z = lax.dynamic_index_in_dim(noises, turn, 0, keepdims=False)
    when = lax.dynamic_index_in_dim(time_index, turn, 0, keepdims=False)
    feat = jnp.pad(time_features(when).astype(BF16).astype(F32), ((0, 8 - count), (0, 0)))
    times = (when.astype(F32) + 0.5) / NT
    times = jnp.pad(jnp.broadcast_to(times[:, None], (count, 128)), ((0, 8 - count), (0, 0)))
    mats = pack_mats(conv_weight, time_weight, attn_weight).astype(BF16)
    mats = lax.all_gather(lax.all_gather(mats, "dp", axis=1, tiled=True), "mp", axis=2, tiled=True)
    ion = pack_small(io_weight, norm_param).astype(BF16)
    ion = lax.all_gather(ion, ("mp", "dp"), axis=0, tiled=True).astype(F32)
    both = lax.all_gather(jnp.stack([own_x, own_z]), "dp", axis=1, tiled=True)
    spot = jnp.arange(8)[:, None]
    mine = ((jnp.arange(batch)[None, :] == place * count + spot) & (spot < count)).astype(F32)
    active = (rank < micro).astype(F32)
    flag = jnp.stack([active, jnp.float32(2.0 / (micro * batch))]).reshape(1, 2)
    dmats, dion, scal = local_network(both[0], both[1], mine, times, feat, flag, mats, ion)
    dmats = lax.psum_scatter(dmats, "dp", scatter_dimension=1, tiled=True)
    dmats = lax.psum_scatter(dmats, "mp", scatter_dimension=2, tiled=True)
    dion = lax.psum_scatter(dion.T, ("mp", "dp"), scatter_dimension=0, tiled=True)
    hot = (jnp.arange(micro) == rank).astype(F32)
    squares = jnp.sum(dmats * dmats) + jnp.sum(dion * dion)
    total_sq, loss_sum, cost_sum = lax.psum(
        (squares, hot * scal[0, 0], jnp.where(place == 0, hot * scal[0, 1], 0.0)), ("dp", "mp")
    )
    grad_norm = jnp.sqrt(total_sq)
    scale = CLIP_NORM / jnp.maximum(grad_norm, CLIP_NORM)
    conv_grad, time_grad, attn_grad = unpack_mats(dmats)
    grads = (
        jnp.concatenate([dion[:, None, 0:SUB], dion[:, None, 16 : 16 + SUB]], axis=1).reshape(-1),
        conv_grad,
        time_grad,
        attn_grad,
        dion[:, 32 : 32 + SUB].reshape(-1),
    )
    results = [
        adam_update(weights[kind], firsts[kind], seconds[kind], averages[kind], grads[kind] * scale, RATES[kind])
        for kind in range(5)
    ]
    return tuple(results[kind][part] for part in range(4) for kind in range(5)) + (loss_sum, cost_sum, grad_norm)


def solution(mesh):
    flat = P(("mp", "dp"))
    state = (flat, P(None, None, "dp", "mp"), P(None, "dp", "mp"), P("dp", None, "mp"), flat)
    fused = mesh.shape["dp"] == Z * Y and mesh.shape["mp"] == X * C
    return jax.shard_map(
        functools.partial(body, fused),
        mesh=mesh,
        in_specs=(P("dp", None), P(None, "dp", None), P("dp"), P(None, "dp")) + state * 4,
        out_specs=state * 4 + (P(), P(), P()),
        check_vma=False,
    )
```

```python
import functools
import math

import jax
import numpy as np
import jax.numpy as jnp
from jax import lax
from jax.experimental import pallas as pl
from jax.experimental.pallas import tpu as pltpu
from jax.sharding import PartitionSpec as P

CH = 256
GROUPS = 32
HEADS = 4
HD = 64
SUB = 12
POS = 256
SIDE = 16
SINK = 10
NT = 1000
STEP = 5
MATS = 42
CONV_AT = (1, 10, 24, 33)
TIME_AT = (0, 23)
ATTN_AT = 19
CHUNKS = ((0, 5), (5, 5), (10, 5), (15, 4), (19, 4), (23, 5), (28, 5), (33, 5), (38, 4))
SPLITS = (5, 15, 28, 38)
EARLY = (3, 8)
PLAN = {
    "start": ("zero", "merge", "Z1", "Z7", "A3", "ot", "A8", "Z0", "Z2", "iz", "U1", "B8", "U7", "iu", "B3", "Z5",
        "Z4", "U0", "Z6", "otw", "V1"),
    "sink": ("U2", "iv", "U5", "E3", "V0", "U4", "V2", "U6", "ic", "iw", "C1", "V4"),
    "h0": ("E8", "V5", "C0"),
    "n0": ("V6", "C3", "W1", "C2", "V7"),
    "c0": ("W0",),
    "n1": ("C4",),
    "c1": ("W3", "W2"),
    "n2": ("C5",),
    "qkv": ("W4",),
    "at0": ("C6",),
    "ao": ("C8", "W5"),
    "n3": ("C7",),
    "c2": ("W6",),
    "c3": ("W7", "W8"),
    "w3b": ("R7",),
    "d3": ("R8",),
    "w2b": ("R5", "S7"),
    "d2": ("R6", "S8"),
    "do": ("S5",),
    "bt1": ("S6",),
    "b2": ("R4", "T8", "T7"),
    "w1b": ("T5", "R2"),
    "b1": ("S4", "R3", "T6"),
    "w0a": ("S2",),
    "w0b": ("R0", "Y5", "Y7"),
    "d0": ("S3", "R1", "S0", "Y6"),
    "b0": ("T4", "T2", "Y8", "S1"),
    "win": ("T0", "Y4"),
    "tail": ("X8", "T3", "Y2", "T1", "da", "X6", "X5", "Y0", "Y3", "Y1", "X2", "X7", "F8", "X0", "X3", "F5",
        "X4", "F6", "db", "X1"),
    "end": ("F0", "F2", "F3", "F4", "F7", "F1"),
}
LEVELS = 32000.0
MESH = pl.DeviceIdType.MESH


EPS_NORM = 1e-05
SINK_EPS = 0.01
CLIP_NORM = 1.0
BETA_ONE = 0.5
BETA_TWO = 0.5
ADAM_EPS = 1e-08
WEIGHT_DECAY = 0.01
EMA_DECAY = 0.9
RATES = (0.06, 0.01, 0.03, 0.03, 0.3)
F32 = jnp.float32
BF16 = jnp.bfloat16
ROWS = 32
PAD = SIDE
IMGS = 2
SPOTS = IMGS * POS


def dot(a, b, ca=1, cb=0):
    return lax.dot_general(a, b, (((ca,), (cb,)), ((), ())), preferred_element_type=F32)


def split3(v):
    one = v.astype(BF16)
    rest = v - one.astype(F32)
    two = rest.astype(BF16)
    three = (rest - two.astype(F32)).astype(BF16)
    return one, two, three


def group_sum(v):
    per = CH // GROUPS
    rows = lax.broadcasted_iota(jnp.int32, (CH, CH), 0) // per
    cols = lax.broadcasted_iota(jnp.int32, (CH, CH), 1) // per
    ones = jnp.where(rows == cols, 1.0, 0.0).astype(BF16)
    one, two, three = split3(v)
    got = dot(jnp.concatenate([one.astype(F32), two.astype(F32), three.astype(F32)], axis=0).astype(BF16), ones)
    n = v.shape[0]
    return got[:n] + got[n : 2 * n] + got[2 * n :]


def rows8(*rows):
    return jnp.concatenate(list(rows) + [jnp.zeros((8 - len(rows), CH), F32)], axis=0)


def for_blocks(step, init):
    return lax.fori_loop(0, POS // ROWS, lambda i, c: step(pl.multiple_of(i * ROWS, ROWS), c), init, unroll=True)


def norm_stats(field, stats, slot):
    zero = jnp.zeros((8, CH), F32)

    def fold(v):
        return v.reshape(ROWS // 8, 8, CH).sum(axis=0)

    sums = []
    for n in range(IMGS):
        acc = for_blocks(lambda at, c: c + fold(field[pl.ds(n * POS + at, ROWS), :]), zero)
        sums.append(jnp.sum(acc, axis=0, keepdims=True))
    scale = 1.0 / (POS * (CH // GROUPS))
    means = group_sum(rows8(*sums)) * scale
    sums = []
    for n in range(IMGS):
        mean = means[n : n + 1]

        def step(at, c):
            d = field[pl.ds(n * POS + at, ROWS), :] - mean
            return c + fold(d * d)

        sums.append(jnp.sum(for_blocks(step, zero), axis=0, keepdims=True))
    devs = group_sum(rows8(*sums)) * scale
    stats[slot, 0:8] = means
    stats[slot, 8:16] = lax.rsqrt(devs + EPS_NORM)


def put_shifts(pads, n, at, value):
    col = lax.broadcasted_iota(jnp.int32, value.shape, 0) % SIDE
    left = jnp.where(col == 0, 0.0, pltpu.roll(value, 1, 0))
    right = jnp.where(col == SIDE - 1, 0.0, pltpu.roll(value, value.shape[0] - 1, 0))
    rows = pl.ds(PAD + at, value.shape[0])
    pads[0, n, rows, :] = left.astype(BF16)
    pads[1, n, rows, :] = value.astype(BF16)
    pads[2, n, rows, :] = right.astype(BF16)


def tap(pads, r, c):
    return pads[c + 1, :, PAD + SIDE * r : PAD + SIDE * r + POS, :].reshape(SPOTS, CH)


OFFSETS = [(r, c) for r in (-1, 0, 1) for c in (-1, 0, 1)]


def train(
    x, z, mine, times, feats, active, step_scale, weights_small, mat, put, pump,
    dion_ref, scal_ref,
    h, flow, c1s, pads, acts, stats, start, goal, qkv, probs, mixed, tmp, smallf, dqkv,
):
    batch, depth = x.shape
    def gain(s):
        return ion[32 + 2 * s : 33 + 2 * s]

    def bias(s):
        return ion[33 + 2 * s : 34 + 2 * s]

    pump("pair")
    gram = dot(x, z, 1, 1)
    xf = x.astype(F32)
    zf = z.astype(F32)
    sq_x = jnp.sum(xf * xf, axis=1, keepdims=True)
    sq_z = jnp.sum(zf * zf, axis=1, keepdims=True)
    eye = lax.broadcasted_iota(jnp.int32, (batch, batch), 0) == lax.broadcasted_iota(jnp.int32, (batch, batch), 1)
    sq_z = jnp.sum(jnp.where(eye, sq_z, 0.0), axis=0, keepdims=True)
    cost = (sq_x + sq_z - 2.0 * gram) / depth
    affinity = 2.0 * gram / (depth * SINK_EPS)
    kern = jnp.exp(affinity - jnp.max(affinity, axis=1, keepdims=True))
    share = 1.0 / batch
    pump("sink")

    def sweep(i, c):
        left, right = c
        left = share / jnp.sum(kern * right, axis=1, keepdims=True)
        right = share / jnp.sum(left * kern, axis=0, keepdims=True)
        return left, right

    left, right = lax.fori_loop(0, SINK, sweep, (jnp.ones((batch, 1), F32), jnp.ones((1, batch), F32)))
    scaled = kern * right
    plan_cost = jnp.sum(left * scaled * cost)
    mixing = (scaled / jnp.sum(scaled, axis=1, keepdims=True)).astype(BF16)
    d = mine.astype(BF16)
    mix = dot(d, mixing).astype(BF16)
    paired = dot(mix, z)[0:IMGS]
    pixels = dot(d, x)[0:IMGS]
    inputs = ((1.0 - times) * paired + times * pixels).astype(BF16).astype(F32)
    target = pixels - paired
    start[...] = jnp.zeros_like(start)
    goal[...] = jnp.zeros_like(goal)
    for n in range(IMGS):
        for k in range(SUB):
            start[16 * n + k : 16 * n + k + 1, :] = inputs[n : n + 1, k * POS : (k + 1) * POS]
            goal[16 * n + k : 16 * n + k + 1, :] = target[n : n + 1, k * POS : (k + 1) * POS]
    begin = start[...].astype(BF16)

    for c in range(3):
        for n in range(IMGS):
            pads[c, n, 0:PAD, :] = jnp.zeros((PAD, CH), BF16)
            pads[c, n, PAD + POS :, :] = jnp.zeros((PAD, CH), BF16)

    def blocks(body):
        for n in range(IMGS):
            for_blocks(lambda at, c: (body(n, at), c)[1], 0)

    def norm_forward(field, slot, shifted, keep):
        norm_stats(field, stats, slot)
        g, b = gain(slot), bias(slot)

        def body(n, at):
            mean = stats[slot, n : n + 1]
            rstd = stats[slot, 8 + n : 9 + n]
            rows = pl.ds(n * POS + at, ROWS)
            y = (field[rows, :] - mean) * rstd * g + b
            if slot != 2:
                y = y * (1.0 / (1.0 + jnp.exp(-y)))
            acts[keep, rows, :] = y.astype(BF16)
            if shifted:
                put_shifts(pads, n, at, y)

        blocks(body)

    def conv(layer):
        acc = None
        for k, (r, c) in enumerate(OFFSETS):
            term = dot(tap(pads, r, c), mat(CONV_AT[layer] + k))
            acc = term if acc is None else acc + term
        return acc


    pump("h0")
    ion = weights_small()
    w_in = ion[0:16].astype(BF16)
    w_out = ion[16:32].astype(BF16)
    for n in range(IMGS):
        h[0, n * POS : (n + 1) * POS, :] = dot(begin[16 * n : 16 * n + 16], w_in, 0, 0)

    def residual(layer, slot, src, dst):
        pump(f"n{slot}")
        norm_forward(h.at[src], slot, True, slot)
        pump(f"c{2 * layer}")
        added = dot(feats, mat(TIME_AT[layer]))
        got = conv(2 * layer)
        for n in range(IMGS):
            c1s[layer, n * POS : (n + 1) * POS, :] = got[n * POS : (n + 1) * POS] + added[n : n + 1]
        pump(f"n{slot + 1}")
        norm_forward(c1s.at[layer], slot + 1, True, slot + 1)
        pump(f"c{2 * layer + 1}")
        h[dst] = h[src] + conv(2 * layer + 1)

    residual(0, 0, 0, 1)
    pump("n2")
    norm_forward(h.at[1], 2, False, 2)
    pump("qkv")
    normal = acts[2]
    for j in range(3):
        qkv[j] = dot(normal, mat(ATTN_AT + j)).astype(BF16)
    scale = HD ** (-0.5)

    def head_mask(hh):
        return lax.broadcasted_iota(jnp.int32, (POS, CH), 1) // HD == hh

    for n in range(IMGS):
        rows = slice(n * POS, (n + 1) * POS)
        pump(f"at{n}")
        tmp[...] = jnp.zeros_like(tmp)

        def head(hh, c):
            mask = head_mask(hh)
            q = jnp.where(mask, qkv[0, rows, :].astype(F32), 0.0).astype(BF16)
            scores = dot(q, qkv[1, rows, :], 1, 1) * scale
            e = jnp.exp(scores - jnp.max(scores, axis=1, keepdims=True))
            p = e / jnp.sum(e, axis=1, keepdims=True)
            probs[n, hh] = p
            o = dot(p.astype(BF16), qkv[2, rows, :])
            tmp[...] = jnp.where(mask, o, tmp[...])
            return c

        lax.fori_loop(0, HEADS, head, 0, unroll=HEADS)
        mixed[rows, :] = tmp[...].astype(BF16)
    pump("ao")
    h[2] = h[1] + dot(mixed[...], mat(ATTN_AT + 3), 1, 1)
    residual(1, 3, 2, 3)
    pump("n5")
    norm_forward(h.at[3], 5, False, 5)
    pump("head")

    dion_ref[...] = jnp.zeros_like(dion_ref)
    loss = jnp.zeros((), F32)
    for n in range(IMGS):
        rows = slice(n * POS, (n + 1) * POS)
        last = acts[5, rows, :]
        pred = dot(w_out, last, 1, 1)
        error = pred - goal[16 * n : 16 * n + 16, :]
        loss = loss + jnp.sum(error * error)
        low = (error * (step_scale * active)).astype(BF16)
        dion_ref[16:32, :] += dot(low, last)
        flow[rows, :] = dot(low, w_out, 0, 0)
    lane = lax.broadcasted_iota(jnp.int32, (8, 128), 1)
    scal_ref[...] = jnp.where(lane == 0, loss * active, jnp.where(lane == 1, plan_cost, 0.0))

    def norm_backward(field, slot, up, finish):
        g, b = gain(slot), bias(slot)
        zero = jnp.zeros((8, CH), F32)

        def fold(v):
            return v.reshape(ROWS // 8, 8, CH).sum(axis=0)

        dbs, dgs = [], []
        for n in range(IMGS):
            mean = stats[slot, n : n + 1]
            rstd = stats[slot, 8 + n : 9 + n]

            def step(at, c):
                rows = pl.ds(n * POS + at, ROWS)
                hat = (field[rows, :] - mean) * rstd
                dz = up[rows, :]
                if slot != 2:
                    y = hat * g + b
                    s = 1.0 / (1.0 + jnp.exp(-y))
                    dz = dz * (s * (1.0 + y * (1.0 - s)))
                    up[rows, :] = dz
                return (c[0] + fold(dz), c[1] + fold(dz * hat))

            db, dg = for_blocks(step, (zero, zero))
            dbs.append(jnp.sum(db, axis=0, keepdims=True))
            dgs.append(jnp.sum(dg, axis=0, keepdims=True))
        dion_ref[32 + 2 * slot : 33 + 2 * slot, :] = dgs[0] + dgs[1]
        dion_ref[33 + 2 * slot : 34 + 2 * slot, :] = dbs[0] + dbs[1]
        sums = group_sum(rows8(*[v * g for v in dbs + dgs])) * (1.0 / (POS * (CH // GROUPS)))
        for n in range(IMGS):
            mean = stats[slot, n : n + 1]
            rstd = stats[slot, 8 + n : 9 + n]
            m1 = sums[n : n + 1]
            m2 = sums[IMGS + n : IMGS + n + 1]

            def step(at, c):
                rows = pl.ds(n * POS + at, ROWS)
                hat = (field[rows, :] - mean) * rstd
                finish(n, at, rstd * (up[rows, :] * g - m1 - hat * m2))
                return c

            for_blocks(step, 0)

    def conv_backward(layer, keep):
        turned = acts[keep].T
        pump(f"w{layer}a")
        for k, (r, c) in enumerate(OFFSETS):
            put(CONV_AT[layer] + k, dot(turned, tap(pads, -r, -c)))
            if CONV_AT[layer] + k + 1 in SPLITS:
                pump(f"w{layer}b")
        pump(f"d{layer}")
        acc = None
        for k, (r, c) in enumerate(OFFSETS):
            term = dot(tap(pads, -r, -c), mat(CONV_AT[layer] + k), 1, 1)
            acc = term if acc is None else acc + term
        smallf[...] = acc

    def add_flow(shifted):
        def finish(n, at, dx):
            rows = pl.ds(n * POS + at, ROWS)
            total = flow[rows, :] + dx
            flow[rows, :] = total
            if shifted:
                put_shifts(pads, n, at, total)

        return finish

    def set_flow(n, at, dx):
        rows = pl.ds(n * POS + at, ROWS)
        flow[rows, :] = dx
        put_shifts(pads, n, at, dx)

    def only_shifts(n, at, dx):
        put_shifts(pads, n, at, dx)

    def residual_backward(layer, slot, src, last_one):
        conv_backward(2 * layer + 1, slot + 1)
        pump(f"b{slot + 1}")
        norm_backward(c1s.at[layer], slot + 1, smallf, only_shifts)
        sums = []
        for n in range(IMGS):
            low = pads[1, n, PAD : PAD + POS, :].astype(F32)
            sums.append(jnp.sum(low, axis=0, keepdims=True))
        one, two, three = split3(rows8(*sums))
        stack = jnp.concatenate([v.astype(F32) for v in (one, two, three)], axis=0).astype(BF16)
        feats3 = jnp.concatenate([feats.astype(F32)] * 3, axis=0).astype(BF16)
        put(TIME_AT[layer], dot(feats3, stack, 0, 0))
        conv_backward(2 * layer, slot)
        pump(f"b{slot}")
        norm_backward(h.at[src], slot, smallf, add_flow(False))

    pump("b5")
    norm_backward(h.at[3], 5, flow, set_flow)
    residual_backward(1, 3, 2, False)

    pump("do")
    dy = flow[...].astype(BF16)
    put(ATTN_AT + 3, dot(dy.T, mixed[...]))
    dqkv[3] = dot(dy, mat(ATTN_AT + 3)).astype(BF16)
    for n in range(IMGS):
        rows = slice(n * POS, (n + 1) * POS)
        pump(f"bt{n}")
        for j in range(3):
            smallf[j % 2 * POS : j % 2 * POS + POS, :] = jnp.zeros((POS, CH), F32)
        tmp[...] = jnp.zeros_like(tmp)

        def head(hh, c):
            mask = head_mask(hh)
            do = jnp.where(mask, dqkv[3, rows, :].astype(F32), 0.0).astype(BF16)
            q = jnp.where(mask, qkv[0, rows, :].astype(F32), 0.0).astype(BF16)
            p = probs[n, hh]
            dp = dot(do, qkv[2, rows, :], 1, 1)
            ds = (p * (dp - jnp.sum(p * dp, axis=1, keepdims=True))).astype(BF16)
            tmp[...] = jnp.where(mask, dot(ds, qkv[1, rows, :]), tmp[...])
            smallf[0:POS, :] += dot(ds, q, 0, 0)
            smallf[POS:, :] += dot(p.astype(BF16), do, 0, 0)
            return c

        lax.fori_loop(0, HEADS, head, 0, unroll=HEADS)
        dqkv[0, rows, :] = (tmp[...] * scale).astype(BF16)
        dqkv[1, rows, :] = (smallf[0:POS, :] * scale).astype(BF16)
        dqkv[2, rows, :] = smallf[POS:, :].astype(BF16)
    pump("proj")
    turned = acts[2].T
    acc = None
    for j in range(3):
        put(ATTN_AT + j, dot(turned, dqkv[j]))
        term = dot(dqkv[j], mat(ATTN_AT + j), 1, 1)
        acc = term if acc is None else acc + term
    smallf[...] = acc
    pump("b2")
    norm_backward(h.at[1], 2, smallf, add_flow(True))
    residual_backward(0, 0, 0, True)
    pump("win")
    for n in range(IMGS):
        rows = slice(n * POS, (n + 1) * POS)
        dion_ref[0:16, :] += dot(begin[16 * n : 16 * n + 16], flow[rows, :].astype(BF16))


def work_space():
    return [
        pltpu.VMEM((4, SPOTS, CH), F32),
        pltpu.VMEM((SPOTS, CH), F32),
        pltpu.VMEM((2, SPOTS, CH), F32),
        pltpu.VMEM((3, IMGS, POS + 2 * PAD, CH), BF16),
        pltpu.VMEM((6, SPOTS, CH), BF16),
        pltpu.VMEM((6, 16, CH), F32),
        pltpu.VMEM((16 * IMGS, POS), F32),
        pltpu.VMEM((16 * IMGS, POS), F32),
        pltpu.VMEM((3, SPOTS, CH), BF16),
        pltpu.VMEM((IMGS, HEADS, POS, POS), F32),
        pltpu.VMEM((SPOTS, CH), BF16),
        pltpu.VMEM((POS, CH), F32),
        pltpu.VMEM((SPOTS, CH), F32),
        pltpu.VMEM((4, SPOTS, CH), BF16),
    ]


def local_kernel(x_ref, z_ref, mine_ref, when_ref, feat_ref, flag_ref, mats, ion_ref, dmats, dion_ref, scal_ref, *work):
    def put(m, value):
        dmats[m] = value

    train(
        x_ref[...], z_ref[...], mine_ref[...], when_ref[0:IMGS, 0:1], feat_ref[...].astype(BF16),
        flag_ref[0, 0], flag_ref[0, 1],
        lambda: ion_ref[...].T, lambda m: mats[m], put, lambda name: None,
        dion_ref, scal_ref, *work,
    )


def local_network(x, z, mine, when, feat, flag, mats, ion):
    whole = pl.BlockSpec(memory_space=pltpu.VMEM)
    return pl.pallas_call(
        local_kernel,
        out_shape=(
            jax.ShapeDtypeStruct((MATS, CH, CH), F32),
            jax.ShapeDtypeStruct((48, CH), F32),
            jax.ShapeDtypeStruct((8, 128), F32),
        ),
        in_specs=[whole] * 5 + [pl.BlockSpec(memory_space=pltpu.SMEM)] + [whole] * 2,
        out_specs=(whole, whole, whole),
        scratch_shapes=work_space(),
        compiler_params=pltpu.CompilerParams(vmem_limit_bytes=56 * 2**20),
    )(x, z, mine, when, feat, flag, mats, ion)


Z, Y, X, C = 4, 2, 2, 2
DEVICES = Z * Y * X * C


def fused_kernel(
    micro, batch,
    order_ref, when_ref, images_ref, noises_ref, freq_ref, conv_ref, time_ref, attn_ref, io_ref, norm_ref,
    grads_ref, gion_ref, total_ref,
    mats, dmats, other, give, land, ottmp, ot_ref, otbuf, otwide, xz, ionbuf, dion, diont, ionr, ions, ionq, scal, scalr,
    s1q, s1r, s2q, s2r, zq, zr, expo, kept, gother,
    ot_s, ot_r, ion_s, ion_r, g_s, g_r, r_s, r_r, d_s, d_r, n_s, n_r,
    *work,
):
    dp = lax.axis_index("dp")
    mp = lax.axis_index("mp")
    z, y, x, c = dp // Y, dp % Y, mp // C, mp % C
    flat = mp * (Z * Y) + dp

    def place(z_, y_, x_, c_):
        return (z_ * Y + y_, x_ * C + c_)

    def from_flat(f):
        return (f % (Z * Y), f // (Z * Y))

    sibling = place(z, y, x, 1 - c)
    first = place(z, y * c + (1 - y) * (1 - c), x * (1 - c) + (1 - x) * c, c)
    second = place(z, (1 - y) * c + y * (1 - c), (1 - x) * (1 - c) + x * c, c)

    def remote(src, dst, send, recv, where):
        return pltpu.make_async_remote_copy(
            src_ref=src, dst_ref=dst, send_sem=send, recv_sem=recv, device_id=where, device_id_type=MESH
        )

    barrier = pltpu.get_barrier_semaphore()

    def greet(j, carry):
        pl.semaphore_signal(
            barrier, inc=1, device_id=from_flat((flat + j) % DEVICES), device_id_type=MESH
        )
        return carry

    lax.fori_loop(1, DEVICES, greet, 0)

    def wide(v):
        v = v.astype(BF16).astype(F32)
        none = jnp.zeros_like(v)
        return jnp.where(c == 0, jnp.concatenate([v, none], axis=1), jnp.concatenate([none, v], axis=1)).astype(BF16)

    def pack(m, whole):
        mats[m, x, z, y, c] = wide(jnp.where(c == 0, whole[0:16], whole[16:32]))
        give[m] = wide(jnp.where(c == 0, whole[16:32], whole[0:16]))

    for layer, at in enumerate(CONV_AT):

        def pack_step(k, carry):
            pack(at + k, conv_ref[layer, k])
            return carry

        lax.fori_loop(0, 9, pack_step, 0)
    for layer, at in enumerate(TIME_AT):
        pack(at, time_ref[layer])
    for j in range(4):
        pack(ATTN_AT + j, attn_ref[:, j, :])

    turn = mp - (mp // micro) * (mp - micro + 1)
    row = lax.broadcasted_iota(jnp.int32, (8, images_ref.shape[0]), 0)
    column = lax.broadcasted_iota(jnp.int32, (8, images_ref.shape[0]), 1)
    pick = jnp.zeros(row.shape, F32)
    for n in range(IMGS):
        pick = jnp.where((row == n) & (column == order_ref[turn * IMGS + n]), 1.0, pick)
    own_x = dot(pick.astype(BF16), images_ref[...])
    own_z = noises_ref[turn].astype(F32)
    lines = SUB * POS // 128
    for k in range(lines):
        ottmp[2 * IMGS * k : 2 * IMGS * k + IMGS, :] = own_x[0:IMGS, 128 * k : 128 * k + 128]
        ottmp[2 * IMGS * k + IMGS : 2 * IMGS * (k + 1), :] = own_z[:, 128 * k : 128 * k + 128]
    ot_ref[...] = ottmp[...].astype(BF16)
    io = io_ref[...].reshape(1, io_ref.shape[0])
    norm = norm_ref[...].reshape(1, norm_ref.shape[0])
    zero_row = jnp.zeros((1, 128), F32)
    packed = []
    for r in range(8):
        gap = zero_row[:, 0 : 16 - SUB]
        at = 2 * SUB * r
        packed.append(
            jnp.concatenate(
                [io[:, at : at + SUB], gap, io[:, at + SUB : at + 2 * SUB], gap,
                 norm[:, SUB * r : SUB * r + SUB], zero_row[:, 0 : 128 - 32 - SUB]], axis=1
            )
        )
    ionbuf[x, c, z, y] = jnp.concatenate(packed, axis=0).astype(BF16).astype(F32)
    pl.semaphore_wait(barrier, DEVICES - 1)

    zero_copy = remote(give, land, g_s.at[0, 0], g_r.at[0, 0], sibling)
    def ot_copy(j):
        there = (dp + j) % (Z * Y)
        return remote(ot_ref, otbuf.at[dp], ot_s.at[j], ot_r.at[j], (there, mp))

    def ion_z(j):
        part = ionbuf.at[x, c, z, y]
        return remote(part, part, ion_s.at[j], ion_r.at[j], place((z + j) % Z, y, x, c))

    def ion_u(core):
        part = ionbuf.at[x, c, :, y]
        return remote(part, part, ion_s.at[4], ion_r.at[4], first)

    def ion_v(core):
        part = ionbuf.at[x, 0] if core == 0 else ionbuf.at[:, 1, :, y]
        return remote(part, part, ion_s.at[5], ion_r.at[5], second)

    def ion_c(core):
        part = ionbuf.at[:, c]
        return remote(part, part, ion_s.at[6], ion_r.at[6], sibling)

    def merge(m, carry):
        mats[m, x, z, y, c] = mats[m, x, z, y, c] + land[m]
        return carry

    def span(i):
        return pl.ds(CHUNKS[i][0], CHUNKS[i][1])

    def z_copy(i, j):
        part = mats.at[span(i), x, z, y, c]
        return remote(part, part, g_s.at[i + 1, j], g_r.at[i + 1, j], place((z + j) % Z, y, x, c))

    def u_copy(i):
        part = mats.at[span(i), x, :, y, c]
        return remote(part, part, g_s.at[i + 1, 4], g_r.at[i + 1, 4], first)

    def v_copy(i, core):
        part = mats.at[span(i), x, :, :, 0] if core == 0 else mats.at[span(i), :, :, y, 1]
        return remote(part, part, g_s.at[i + 1, 5], g_r.at[i + 1, 5], second)

    def e_copy(i, j):
        part = mats.at[span(i), :, z, :, c]
        return remote(part, part, g_s.at[i + 1, j], g_r.at[i + 1, j], place((z + j) % Z, y, x, c))

    def a_copy(i):
        part = mats.at[span(i), x, z, y, c]
        return remote(part, part, g_s.at[i + 1, 4], g_r.at[i + 1, 4], first)

    def b_copy(i, core):
        part = mats.at[span(i), x, z, :, 0] if core == 0 else mats.at[span(i), :, z, y, 1]
        return remote(part, part, g_s.at[i + 1, 5], g_r.at[i + 1, 5], second)

    def c_copy(i):
        part = mats.at[span(i), :, :, :, c]
        return remote(part, part, g_s.at[i + 1, 6], g_r.at[i + 1, 6], sibling)

    def on_core(act):
        for core in range(C):
            pl.when(c == core)(functools.partial(act, core))

    def start_all(copies):
        for copy in copies:
            copy.start()

    def wait_all(copies):
        for copy in copies:
            copy.wait()

    peers = range(1, Z)

    def gather_step(kind, i):
        if kind == "A":
            a_copy(i).start()
        elif kind == "B":
            a_copy(i).wait()
            on_core(lambda core: b_copy(i, core).start())
        elif kind == "E":
            on_core(lambda core: b_copy(i, core).wait())
            start_all(e_copy(i, j) for j in peers)
        elif kind == "Z":
            start_all(z_copy(i, j) for j in peers)
        elif kind == "U":
            wait_all(z_copy(i, j) for j in peers)
            u_copy(i).start()
        elif kind == "V":
            u_copy(i).wait()
            on_core(lambda core: v_copy(i, core).start())
        elif kind == "C":
            if i in EARLY:
                wait_all(e_copy(i, j) for j in peers)
            else:
                on_core(lambda core: v_copy(i, core).wait())
            c_copy(i).start()
        elif kind == "W":
            c_copy(i).wait()

    def other_step(kind):
        if kind == "zero":
            zero_copy.start()
        elif kind == "merge":
            zero_copy.wait()
            lax.fori_loop(0, MATS, merge, 0, unroll=6)
        elif kind == "ot":
            start_all(ot_copy(j) for j in range(1, Z * Y))
            otbuf[dp] = ot_ref[...]
        elif kind == "otw":
            wait_all(ot_copy(j) for j in range(1, Z * Y))
        elif kind == "iz":
            start_all(ion_z(j) for j in peers)
        elif kind == "iu":
            wait_all(ion_z(j) for j in peers)
            ion_u(0).start()
        elif kind == "iv":
            ion_u(0).wait()
            on_core(lambda core: ion_v(core).start())
        elif kind == "ic":
            on_core(lambda core: ion_v(core).wait())
            ion_c(0).start()
        elif kind == "iw":
            ion_c(0).wait()
        elif kind == "da":
            wait_all(dion_copy(j) for j in range(1, X * C))
            ionr[mp] = diont[mp]
            ions[...] = ionr[0] + ionr[1] + ionr[2] + ionr[3]
            start_all(dion_again(j) for j in range(1, Z * Y))
            ionq[dp] = ions[dp]
        elif kind == "db":
            wait_all(dion_again(j) for j in range(1, Z * Y))

    def do(steps):
        for kind in steps:
            if kind[1:].isdigit():
                i = int(kind[1:])
                if kind[0] in "RSTYXF":
                    reduce_step(kind[0], i)
                else:
                    gather_step(kind[0], i)
            else:
                other_step(kind)

    def pump(name):
        do(PLAN.get(name, ()))

    pump("start")
    rows = ot_ref.shape[0]
    for j in range(Z * Y):
        otwide[pl.ds(j * rows, rows), :] = otbuf[j].astype(F32)
    for r in range(2 * IMGS):
        for k in range(lines):
            xz[r // IMGS, (r % IMGS) * Z * Y : (r % IMGS + 1) * Z * Y, k * 128 : (k + 1) * 128] = otwide[
                pl.ds(k * 2 * IMGS + r, Z * Y, stride=rows), :
            ]
    spot = lax.broadcasted_iota(jnp.int32, (8, batch), 0)
    column = lax.broadcasted_iota(jnp.int32, (8, batch), 1)
    mine = jnp.where((column == spot * (Z * Y) + dp) & (spot < IMGS), 1.0, 0.0)
    active = jnp.where(mp < micro, 1.0, 0.0)

    def mat(m):
        return jnp.concatenate([mats[m, k].reshape(CH, 128) for k in range(X)], axis=1)

    def put(m, value):
        for k in range(X):
            dmats[m, k] = value[:, 128 * k : 128 * k + 128].reshape(Z, Y, C, 16, 128)

    mine_a = x * (1 - c) + y * c
    mine_b = y * (1 - c) + x * c

    def xy(a, b):
        return a * (1 - c) + b * c, b * (1 - c) + a * c

    def r_copy(i):
        return remote(
            dmats.at[span(i), :, :, :, 1 - c], other.at[span(i)], r_s.at[i, 0], r_r.at[i, 0], sibling
        )

    def base(i, per):
        return CHUNKS[i][0] * per + i

    def one_copy(i):
        part = pl.ds(base(i, 8), CHUNKS[i][1] * 8 + 1)
        return remote(s1q.at[part], s1r.at[part], r_s.at[i, 1], r_r.at[i, 1], second)

    def two_copy(i):
        part = pl.ds(base(i, 4), CHUNKS[i][1] * 4 + 1)
        return remote(s2q.at[part], s2r.at[part], r_s.at[i, 2], r_r.at[i, 2], first)

    def three_copy(i, j):
        part = pl.ds(base(i, 1), CHUNKS[i][1] + 1)
        return remote(
            zq.at[j - 1, part], zr.at[j - 1, part], r_s.at[i, 2 + j], r_r.at[i, 2 + j], place((z + j) % Z, y, x, c)
        )

    def four_copy(i):
        return remote(kept.at[span(i)], gother.at[span(i)], r_s.at[i, 6], r_r.at[i, 6], sibling)

    def exponent(tiles):
        top = jnp.max(jnp.abs(tiles[0]), axis=0, keepdims=True)
        for t in tiles[1:]:
            top = jnp.maximum(top, jnp.max(jnp.abs(t), axis=0, keepdims=True))
        return jnp.floor(jnp.log2(jnp.maximum(top, 1e-30))) + 1.0

    def coded(tile, power):
        return jnp.round(tile * (LEVELS * jnp.exp2(-power))).astype(jnp.int32).astype(jnp.int16)

    def decoded(tile, unit):
        return tile.astype(jnp.int32).astype(F32) * unit

    def units(ref, at, slot):
        expo[slot] = jnp.exp2(ref[at].astype(jnp.int32).astype(F32)) * (1.0 / LEVELS)

    def powers(ref, at):
        ref[at] = expo[0].astype(jnp.int32).astype(jnp.int16)

    def stage_one(i):
        r_copy(i).wait()
        first_m, count = CHUNKS[i]
        start = base(i, 8)

        def step(k, carry):
            m = first_m + k
            tiles = []
            for b in range(2):
                x_, y_ = xy(1 - mine_a, b)
                for zz in range(Z):
                    tiles.append(dmats[m, x_, zz, y_, c] + other[m, x_, zz, y_])
            power = exponent(tiles)
            expo[0, pl.ds(k, 1), :] = power
            for t, tile in enumerate(tiles):
                s1q[start + k * 8 + t] = coded(tile, power)
            return carry

        lax.fori_loop(0, count, step, 0, unroll=True)
        powers(s1q, start + count * 8)
        one_copy(i).start()

    def stage_two(i):
        one_copy(i).wait()
        first_m, count = CHUNKS[i]
        start, start_one = base(i, 4), base(i, 8)
        units(s1r, start_one + count * 8, 1)

        def step(k, carry):
            m = first_m + k
            unit = expo[1, pl.ds(k, 1), :]
            x_, y_ = xy(mine_a, 1 - mine_b)
            tiles = []
            for zz in range(Z):
                got = decoded(s1r[start_one + k * 8 + (1 - mine_b) * 4 + zz], unit)
                tiles.append(dmats[m, x_, zz, y_, c] + other[m, x_, zz, y_] + got)
            power = exponent(tiles)
            expo[0, pl.ds(k, 1), :] = power
            for t, tile in enumerate(tiles):
                s2q[start + k * 4 + t] = coded(tile, power)
            return carry

        lax.fori_loop(0, count, step, 0, unroll=True)
        powers(s2q, start + count * 4)
        two_copy(i).start()

    def stage_three(i):
        two_copy(i).wait()
        first_m, count = CHUNKS[i]
        start, start_one, start_two = base(i, 1), base(i, 8), base(i, 4)
        units(s1r, start_one + count * 8, 1)
        units(s2r, start_two + count * 4, 2)

        def step(k, carry):
            m = first_m + k
            unit_one = expo[1, pl.ds(k, 1), :]
            unit_two = expo[2, pl.ds(k, 1), :]

            def tile(zz):
                return (
                    dmats[m, x, zz, y, c]
                    + other[m, x, zz, y]
                    + decoded(s1r[start_one + k * 8 + mine_b * 4 + zz], unit_one)
                    + decoded(s2r[start_two + k * 4 + zz], unit_two)
                )

            tiles = [tile((z + j) % Z) for j in range(1, Z)]
            power = exponent(tiles)
            expo[0, pl.ds(k, 1), :] = power
            for j in range(1, Z):
                zq[j - 1, start + k] = coded(tiles[j - 1], power)
            kept[m] = tile(z)
            return carry

        lax.fori_loop(0, count, step, 0, unroll=True)
        for j in range(1, Z):
            powers(zq.at[j - 1], start + count)
        for j in range(1, Z):
            three_copy(i, j).start()

    def stage_four(i):
        for j in range(1, Z):
            three_copy(i, j).wait()
        first_m, count = CHUNKS[i]
        start = base(i, 1)
        for j in range(1, Z):
            units(zr.at[j - 1], start + count, j)

        def step(k, carry):
            m = first_m + k
            total = kept[m]
            for j in range(1, Z):
                total = total + decoded(zr[j - 1, start + k], expo[j, pl.ds(k, 1), :])
            kept[m] = total
            return carry + total * total

        square = lax.fori_loop(0, count, step, jnp.zeros((16, 128), F32), unroll=True)
        four_copy(i).start()
        return square

    squares = []

    def reduce_step(kind, i):
        if kind == "R":
            r_copy(i).start()
        elif kind == "S":
            stage_one(i)
        elif kind == "T":
            stage_two(i)
        elif kind == "Y":
            stage_three(i)
        elif kind == "X":
            squares.append(stage_four(i))
        else:
            finish(i)

    def finish(i):
        four_copy(i).wait()

        def step(k, carry):
            m = CHUNKS[i][0] + k
            for half in range(C):
                tile = jnp.where(c == half, kept[m], gother[m])
                grads_ref[m, half * 16 : half * 16 + 16, :] = jnp.where(c == 0, tile[:, 0:64], tile[:, 64:128])
            return carry

        lax.fori_loop(0, CHUNKS[i][1], step, 0, unroll=True)

    seat = lax.broadcasted_iota(jnp.int32, (8, 1), 0)
    times = jnp.zeros((8, 1), F32)
    for n in range(IMGS):
        index = when_ref[pl.ds(turn, 1), n : n + 1]
        times = jnp.where(seat == n, (index + 0.5) / NT, times)
    angles = 1000.0 * times * freq_ref[...]
    feats = jnp.where(seat < IMGS, jnp.concatenate([jnp.sin(angles), jnp.cos(angles)], axis=1), 0.0).astype(BF16)
    train(
        xz[0].astype(BF16), xz[1].astype(BF16), mine, times[0:IMGS], feats, active, 2.0 / (micro * batch),
        lambda: ionbuf[...].reshape(CH, 128).T, mat, put, pump, dion, scal, *work,
    )

    diont[...] = (
        jnp.concatenate([dion[...], jnp.zeros((128 - 48, CH), F32)], axis=0).T.reshape(X * C, Z * Y, 8, 128)
    )

    def dion_copy(j):
        there = (mp + j) % (X * C)
        return remote(diont.at[there], ionr.at[mp], d_s.at[j], d_r.at[j], (dp, there))

    def dion_again(j):
        there = (dp + j) % (Z * Y)
        return remote(ions.at[there], ionq.at[dp], d_s.at[X * C + j], d_r.at[X * C + j], (there, mp))

    start_all(dion_copy(j) for j in range(1, X * C))
    pump("tail")
    small = jnp.sum(ionq[...], axis=0)
    gion_ref[...] = small
    square = small * small
    for part in squares:
        square = square + part[0:8] + part[8:16]

    loss, plan_cost = scal[0:1, 0:1], scal[0:1, 1:2]
    lane = lax.broadcasted_iota(jnp.int32, (8, 128), 1)
    line = lax.broadcasted_iota(jnp.int32, (8, 128), 0)
    tile = jnp.where(line == 7, 0.0, square) + jnp.where(line == 0, pltpu.roll(square, 1, 0), 0.0)
    tile = jnp.where((line == 7) & (lane == mp) & (mp < micro), loss, tile)
    tile = jnp.where((line == 7) & (lane == micro + mp) & (mp < micro) & (dp == 0), plan_cost, tile)
    scal[...] = tile
    scalr[flat] = tile

    def n_copy(j):
        return remote(scal, scalr.at[flat], n_s.at[j], n_r.at[j], from_flat((flat + j) % DEVICES))

    def n_start(j, carry):
        n_copy(j).start()
        return carry

    def n_wait(j, carry):
        n_copy(j).wait()
        return carry

    lax.fori_loop(1, DEVICES, n_start, 0)
    pump("end")
    lax.fori_loop(1, DEVICES, n_wait, 0)
    total_ref[...] = jnp.sum(scalr[...], axis=0)


def fused_network(micro, batch, order, when, images, noises, conv, time, attn, io, norm):
    whole = pl.BlockSpec(memory_space=pltpu.VMEM)
    scalar = pl.BlockSpec(memory_space=pltpu.SMEM)
    blocks = (X, Z, Y)
    rows = 2 * IMGS * SUB * POS // 128
    dma = pltpu.SemaphoreType.DMA
    count = len(CHUNKS)
    half = CH // 2
    freq = np.exp(np.float32(-math.log(10000.0)) * np.arange(half, dtype=np.float32) / np.float32(half))
    freq = jnp.asarray(freq.reshape(1, half))
    return pl.pallas_call(
        functools.partial(fused_kernel, micro, batch),
        out_shape=(
            jax.ShapeDtypeStruct((MATS, 32, 64), F32),
            jax.ShapeDtypeStruct((8, 128), F32),
            jax.ShapeDtypeStruct((8, 128), F32),
        ),
        in_specs=[scalar] + [whole] * 9,
        out_specs=(whole, whole, whole),
        scratch_shapes=[
            pltpu.VMEM((MATS,) + blocks + (C, 16, 128), BF16),
            pltpu.VMEM((MATS,) + blocks + (C, 16, 128), F32),
            pltpu.VMEM((MATS,) + blocks + (16, 128), F32),
            pltpu.VMEM((MATS, 16, 128), BF16),
            pltpu.VMEM((MATS, 16, 128), BF16),
            pltpu.VMEM((rows, 128), F32),
            pltpu.VMEM((rows, 128), BF16),
            pltpu.VMEM((Z * Y, rows, 128), BF16),
            pltpu.VMEM((Z * Y * rows, 128), F32),
            pltpu.VMEM((2, batch, SUB * POS), F32),
            pltpu.VMEM((X, C, Z, Y, 8, 128), F32),
            pltpu.VMEM((48, CH), F32),
            pltpu.VMEM((X * C, Z * Y, 8, 128), F32),
            pltpu.VMEM((X * C, Z * Y, 8, 128), F32),
            pltpu.VMEM((Z * Y, 8, 128), F32),
            pltpu.VMEM((Z * Y, 8, 128), F32),
            pltpu.VMEM((8, 128), F32),
            pltpu.VMEM((DEVICES, 8, 128), F32),
            pltpu.VMEM((MATS * 8 + count, 16, 128), jnp.int16),
            pltpu.VMEM((MATS * 8 + count, 16, 128), jnp.int16),
            pltpu.VMEM((MATS * 4 + count, 16, 128), jnp.int16),
            pltpu.VMEM((MATS * 4 + count, 16, 128), jnp.int16),
            pltpu.VMEM((Z - 1, MATS + count, 16, 128), jnp.int16),
            pltpu.VMEM((Z - 1, MATS + count, 16, 128), jnp.int16),
            pltpu.VMEM((Z, 16, 128), F32),
            pltpu.VMEM((MATS, 16, 128), F32),
            pltpu.VMEM((MATS, 16, 128), F32),
            dma((Z * Y,)), dma((Z * Y,)),
            dma((7,)), dma((7,)),
            dma((count + 1, 7)), dma((count + 1, 7)),
            dma((count, 7)), dma((count, 7)),
            dma((X * C + Z * Y,)), dma((X * C + Z * Y,)),
            dma((DEVICES,)), dma((DEVICES,)),
        ] + work_space(),
        compiler_params=pltpu.CompilerParams(
            vmem_limit_bytes=60 * 2**20, collective_id=0, has_side_effects=True
        ),
    )(order, when, images, noises, freq, conv, time, attn, io, norm)


def time_features(time_index):
    times = (time_index.astype(jnp.float32) + 0.5) / NT
    half = CH // 2
    frequency = jnp.exp(-math.log(10000.0) * jnp.arange(half, dtype=jnp.float32) / half)
    angles = 1000.0 * times[:, None] * frequency[None, :]
    return jnp.concatenate([jnp.sin(angles), jnp.cos(angles)], axis=1)


def adam_update(weight, first, second, average, gradient, rate):
    first = BETA_ONE * first + (1 - BETA_ONE) * gradient
    second = BETA_TWO * second + (1 - BETA_TWO) * gradient * gradient
    ratio = first / (1 - BETA_ONE**STEP) / (jnp.sqrt(second / (1 - BETA_TWO**STEP)) + ADAM_EPS)
    weight = weight - rate * (ratio + WEIGHT_DECAY * weight)
    average = EMA_DECAY * average + (1 - EMA_DECAY) * weight
    return (weight, first, second, average)


def adam_kernel(grads_ref, gion_ref, total_ref, *refs):
    old, new = refs[:20], refs[20:40]
    loss_ref, cost_ref, norm_ref = refs[40:]
    norm = jnp.sqrt(jnp.sum(total_ref[0:7], axis=(0, 1), keepdims=True))
    scale = CLIP_NORM / jnp.maximum(norm, CLIP_NORM)

    def update(kind, at, gradient):
        got = adam_update(*[old[5 * part + kind][at] for part in range(4)], gradient * scale, RATES[kind])
        for part in range(4):
            new[5 * part + kind][at] = got[part]

    for layer, start in enumerate(CONV_AT):
        update(1, (layer,), grads_ref[start : start + 9])
    for layer, start in enumerate(TIME_AT):
        update(2, (layer,), grads_ref[start])
    for j in range(4):
        update(3, (slice(None), j), grads_ref[ATTN_AT + j])
    tile = gion_ref[...]
    own = old[0].shape[0] // (2 * SUB)
    for kind, pieces in ((0, (0, 16)), (4, (32,))):
        flat = [tile[r : r + 1, at : at + SUB] for r in range(own) for at in pieces]
        flat = jnp.concatenate(flat, axis=1)
        got = adam_update(
            *[old[5 * part + kind][...].reshape(flat.shape) for part in range(4)], flat * scale, RATES[kind]
        )
        for part in range(4):
            new[5 * part + kind][...] = got[part].reshape(old[kind].shape)
    micro = loss_ref.shape[0]
    for m in range(micro):
        loss_ref[m] = total_ref[7, m]
        cost_ref[m] = total_ref[7, micro + m]
    norm_ref[0] = norm[0, 0]


def adam(micro, grads, gion, total, state):
    whole = pl.BlockSpec(memory_space=pltpu.VMEM)
    scalar = pl.BlockSpec(memory_space=pltpu.SMEM)

    return pl.pallas_call(
        adam_kernel,
        out_shape=tuple(jax.ShapeDtypeStruct(v.shape, F32) for v in state)
        + (jax.ShapeDtypeStruct((micro,), F32),) * 2
        + (jax.ShapeDtypeStruct((1,), F32),),
        in_specs=[whole] * (3 + len(state)),
        out_specs=(whole,) * len(state) + (scalar,) * 3,
        compiler_params=pltpu.CompilerParams(vmem_limit_bytes=60 * 2**20),
    )(grads, gion, total, *state)


def pack_mats(conv, time, attn):
    return jnp.concatenate(
        [time[0:1], conv[0], conv[1], attn.transpose(1, 0, 2), time[1:2], conv[2], conv[3]], axis=0
    )


def unpack_mats(mats):
    conv = jnp.stack([mats[at : at + 9] for at in CONV_AT])
    time = jnp.stack([mats[at] for at in TIME_AT])
    return conv, time, mats[ATTN_AT : ATTN_AT + 4].transpose(1, 0, 2)


def pack_small(io, norm):
    own = norm.shape[0] // SUB
    io = io.reshape(own, 2, SUB)
    norm = norm.reshape(own, SUB)
    gap = jnp.zeros((own, 16 - SUB), io.dtype)
    return jnp.concatenate(
        [io[:, 0], gap, io[:, 1], gap, norm, gap, jnp.zeros((own, 80), io.dtype)], axis=1
    )


def body(
    fused,
    images, noises, order, time_index, io_weight, conv_weight, time_weight, attn_weight, norm_param,
    io_first, conv_first, time_first, attn_first, norm_first,
    io_second, conv_second, time_second, attn_second, norm_second,
    io_average, conv_average, time_average, attn_average, norm_average,
):
    rank = lax.axis_index("mp")
    place = lax.axis_index("dp")
    micro, count, depth = noises.shape
    batch = count * lax.axis_size("dp")
    turn = jnp.minimum(rank, micro - 1)
    weights = (io_weight, conv_weight, time_weight, attn_weight, norm_param)
    firsts = (io_first, conv_first, time_first, attn_first, norm_first)
    seconds = (io_second, conv_second, time_second, attn_second, norm_second)
    averages = (io_average, conv_average, time_average, attn_average, norm_average)
    if fused:
        grads, gion, total = fused_network(
            micro, batch, order, time_index.astype(F32), images, noises, conv_weight, time_weight, attn_weight, io_weight, norm_param
        )
        out = adam(micro, grads, gion, total, weights + firsts + seconds + averages)
        return out[:22] + (out[22].reshape(()),)
    chosen = lax.dynamic_slice_in_dim(order, turn * count, count, 0)
    own_x = jnp.take(images, chosen, axis=0)
    own_z = lax.dynamic_index_in_dim(noises, turn, 0, keepdims=False)
    when = lax.dynamic_index_in_dim(time_index, turn, 0, keepdims=False)
    feat = jnp.pad(time_features(when).astype(BF16).astype(F32), ((0, 8 - count), (0, 0)))
    times = (when.astype(F32) + 0.5) / NT
    times = jnp.pad(jnp.broadcast_to(times[:, None], (count, 128)), ((0, 8 - count), (0, 0)))
    mats = pack_mats(conv_weight, time_weight, attn_weight).astype(BF16)
    mats = lax.all_gather(lax.all_gather(mats, "dp", axis=1, tiled=True), "mp", axis=2, tiled=True)
    ion = pack_small(io_weight, norm_param).astype(BF16)
    ion = lax.all_gather(ion, ("mp", "dp"), axis=0, tiled=True).astype(F32)
    both = lax.all_gather(jnp.stack([own_x, own_z]), "dp", axis=1, tiled=True)
    spot = jnp.arange(8)[:, None]
    mine = ((jnp.arange(batch)[None, :] == place * count + spot) & (spot < count)).astype(F32)
    active = (rank < micro).astype(F32)
    flag = jnp.stack([active, jnp.float32(2.0 / (micro * batch))]).reshape(1, 2)
    dmats, dion, scal = local_network(both[0], both[1], mine, times, feat, flag, mats, ion)
    dmats = lax.psum_scatter(dmats, "dp", scatter_dimension=1, tiled=True)
    dmats = lax.psum_scatter(dmats, "mp", scatter_dimension=2, tiled=True)
    dion = lax.psum_scatter(dion.T, ("mp", "dp"), scatter_dimension=0, tiled=True)
    hot = (jnp.arange(micro) == rank).astype(F32)
    squares = jnp.sum(dmats * dmats) + jnp.sum(dion * dion)
    total_sq, loss_sum, cost_sum = lax.psum(
        (squares, hot * scal[0, 0], jnp.where(place == 0, hot * scal[0, 1], 0.0)), ("dp", "mp")
    )
    grad_norm = jnp.sqrt(total_sq)
    scale = CLIP_NORM / jnp.maximum(grad_norm, CLIP_NORM)
    conv_grad, time_grad, attn_grad = unpack_mats(dmats)
    grads = (
        jnp.concatenate([dion[:, None, 0:SUB], dion[:, None, 16 : 16 + SUB]], axis=1).reshape(-1),
        conv_grad,
        time_grad,
        attn_grad,
        dion[:, 32 : 32 + SUB].reshape(-1),
    )
    results = [
        adam_update(weights[kind], firsts[kind], seconds[kind], averages[kind], grads[kind] * scale, RATES[kind])
        for kind in range(5)
    ]
    return tuple(results[kind][part] for part in range(4) for kind in range(5)) + (loss_sum, cost_sum, grad_norm)


def solution(mesh):
    flat = P(("mp", "dp"))
    state = (flat, P(None, None, "dp", "mp"), P(None, "dp", "mp"), P("dp", None, "mp"), flat)
    fused = mesh.shape["dp"] == Z * Y and mesh.shape["mp"] == X * C
    return jax.shard_map(
        functools.partial(body, fused),
        mesh=mesh,
        in_specs=(P("dp", None), P(None, "dp", None), P("dp"), P(None, "dp")) + state * 4,
        out_specs=state * 4 + (P(), P(), P()),
        check_vma=False,
    )
```

```python
import functools
import math

import jax
import numpy as np
import jax.numpy as jnp
from jax import lax
from jax.experimental import pallas as pl
from jax.experimental.pallas import tpu as pltpu
from jax.sharding import PartitionSpec as P

CH = 256
GROUPS = 32
HEADS = 4
HD = 64
SUB = 12
POS = 256
SIDE = 16
SINK = 10
NT = 1000
STEP = 5
MATS = 42
CONV_AT = (1, 10, 24, 33)
TIME_AT = (0, 23)
ATTN_AT = 19
CHUNKS = ((0, 5), (5, 5), (10, 5), (15, 4), (19, 4), (23, 5), (28, 5), (33, 5), (38, 4))
SPLITS = (5, 15, 28, 38)
EARLY = (4, 8)
PLAN = {
    "start": ("zero", "merge", "Z2", "A4", "Z0", "iz", "A8", "Z1", "Z3", "ot", "Z7", "Z5", "U2", "B8", "Z6", "U0",
        "B4", "U1", "V2", "iu", "U3", "V0", "E4", "V1", "iv", "U5", "otw", "C2", "V3", "U6"),
    "h0": ("C0", "E8", "ic", "U7", "C1", "V5", "iw", "W0"),
    "n0": ("W2", "V6", "C4", "C3"),
    "c0": ("W1",),
    "n1": ("V7",),
    "c1": ("W3", "W4"),
    "n2": ("C5",),
    "at0": ("C6",),
    "ao": ("C8", "W5"),
    "n3": ("C7",),
    "c2": ("W6",),
    "c3": ("W8", "W7"),
    "w3b": ("R7",),
    "w2a": ("R8",),
    "w2b": ("R5", "S7"),
    "b3": ("R6",),
    "do": ("S8",),
    "bt0": ("S5",),
    "b2": ("T7",),
    "w1b": ("T8", "R2", "S6", "R4"),
    "d1": ("R3",),
    "b1": ("T5",),
    "w0a": ("S2", "Y7"),
    "w0b": ("R0", "S4", "Y8"),
    "d0": ("R1", "T6", "S3"),
    "b0": ("Y5", "T2", "S1", "X7", "S0", "X8"),
    "win": ("T4", "Y6", "Y2", "T3", "T1", "X6", "Y4", "T0", "F7", "Y3", "X2"),
    "tail": ("Y1", "Y0", "F2", "X3", "da", "F3", "X1", "F6", "X5", "X4", "db", "X0"),
    "end": ("F5", "F4", "F8", "F1", "F0"),
}
LEVELS = 32000.0
MESH = pl.DeviceIdType.MESH


EPS_NORM = 1e-05
SINK_EPS = 0.01
CLIP_NORM = 1.0
BETA_ONE = 0.5
BETA_TWO = 0.5
ADAM_EPS = 1e-08
WEIGHT_DECAY = 0.01
EMA_DECAY = 0.9
RATES = (0.06, 0.01, 0.03, 0.03, 0.3)
F32 = jnp.float32
BF16 = jnp.bfloat16
ROWS = 32
PAD = SIDE
IMGS = 2
SPOTS = IMGS * POS


def dot(a, b, ca=1, cb=0):
    return lax.dot_general(a, b, (((ca,), (cb,)), ((), ())), preferred_element_type=F32)


def split3(v):
    one = v.astype(BF16)
    rest = v - one.astype(F32)
    two = rest.astype(BF16)
    three = (rest - two.astype(F32)).astype(BF16)
    return one, two, three


def group_sum(v):
    per = CH // GROUPS
    rows = lax.broadcasted_iota(jnp.int32, (CH, CH), 0) // per
    cols = lax.broadcasted_iota(jnp.int32, (CH, CH), 1) // per
    ones = jnp.where(rows == cols, 1.0, 0.0).astype(BF16)
    one, two, three = split3(v)
    got = dot(jnp.concatenate([one.astype(F32), two.astype(F32), three.astype(F32)], axis=0).astype(BF16), ones)
    n = v.shape[0]
    return got[:n] + got[n : 2 * n] + got[2 * n :]


def rows8(*rows):
    return jnp.concatenate(list(rows) + [jnp.zeros((8 - len(rows), CH), F32)], axis=0)


def for_blocks(step, init):
    return lax.fori_loop(0, POS // ROWS, lambda i, c: step(pl.multiple_of(i * ROWS, ROWS), c), init, unroll=True)


def norm_stats(field, stats, slot):
    zero = jnp.zeros((8, CH), F32)

    def fold(v):
        return v.reshape(ROWS // 8, 8, CH).sum(axis=0)

    sums = []
    for n in range(IMGS):
        acc = for_blocks(lambda at, c: c + fold(field[pl.ds(n * POS + at, ROWS), :]), zero)
        sums.append(jnp.sum(acc, axis=0, keepdims=True))
    scale = 1.0 / (POS * (CH // GROUPS))
    means = group_sum(rows8(*sums)) * scale
    sums = []
    for n in range(IMGS):
        mean = means[n : n + 1]

        def step(at, c):
            d = field[pl.ds(n * POS + at, ROWS), :] - mean
            return c + fold(d * d)

        sums.append(jnp.sum(for_blocks(step, zero), axis=0, keepdims=True))
    devs = group_sum(rows8(*sums)) * scale
    stats[slot, 0:8] = means
    stats[slot, 8:16] = lax.rsqrt(devs + EPS_NORM)


def put_shifts(pads, n, at, value):
    col = lax.broadcasted_iota(jnp.int32, value.shape, 0) % SIDE
    left = jnp.where(col == 0, 0.0, pltpu.roll(value, 1, 0))
    right = jnp.where(col == SIDE - 1, 0.0, pltpu.roll(value, value.shape[0] - 1, 0))
    rows = pl.ds(PAD + at, value.shape[0])
    pads[0, n, rows, :] = left.astype(BF16)
    pads[1, n, rows, :] = value.astype(BF16)
    pads[2, n, rows, :] = right.astype(BF16)


def tap(pads, r, c):
    return pads[c + 1, :, PAD + SIDE * r : PAD + SIDE * r + POS, :].reshape(SPOTS, CH)


OFFSETS = [(r, c) for r in (-1, 0, 1) for c in (-1, 0, 1)]


def train(
    x, z, mine, times, feats, active, step_scale, weights_small, mat, put, pump,
    dion_ref, scal_ref,
    h, flow, c1s, pads, acts, stats, start, goal, qkv, probs, mixed, tmp, smallf, dqkv,
):
    batch, depth = x.shape
    def gain(s):
        return ion[32 + 2 * s : 33 + 2 * s]

    def bias(s):
        return ion[33 + 2 * s : 34 + 2 * s]

    pump("pair")
    gram = dot(x, z, 1, 1)
    xf = x.astype(F32)
    zf = z.astype(F32)
    sq_x = jnp.sum(xf * xf, axis=1, keepdims=True)
    sq_z = jnp.sum(zf * zf, axis=1, keepdims=True)
    eye = lax.broadcasted_iota(jnp.int32, (batch, batch), 0) == lax.broadcasted_iota(jnp.int32, (batch, batch), 1)
    sq_z = jnp.sum(jnp.where(eye, sq_z, 0.0), axis=0, keepdims=True)
    cost = (sq_x + sq_z - 2.0 * gram) / depth
    affinity = 2.0 * gram / (depth * SINK_EPS)
    kern = jnp.exp(affinity - jnp.max(affinity, axis=1, keepdims=True))
    share = 1.0 / batch
    pump("sink")

    def sweep(i, c):
        left, right = c
        left = share / jnp.sum(kern * right, axis=1, keepdims=True)
        right = share / jnp.sum(left * kern, axis=0, keepdims=True)
        return left, right

    left, right = lax.fori_loop(0, SINK, sweep, (jnp.ones((batch, 1), F32), jnp.ones((1, batch), F32)))
    scaled = kern * right
    plan_cost = jnp.sum(left * scaled * cost)
    mixing = (scaled / jnp.sum(scaled, axis=1, keepdims=True)).astype(BF16)
    d = mine.astype(BF16)
    mix = dot(d, mixing).astype(BF16)
    paired = dot(mix, z)[0:IMGS]
    pixels = dot(d, x)[0:IMGS]
    inputs = ((1.0 - times) * paired + times * pixels).astype(BF16).astype(F32)
    target = pixels - paired
    start[...] = jnp.zeros_like(start)
    goal[...] = jnp.zeros_like(goal)
    for n in range(IMGS):
        for k in range(SUB):
            start[16 * n + k : 16 * n + k + 1, :] = inputs[n : n + 1, k * POS : (k + 1) * POS]
            goal[16 * n + k : 16 * n + k + 1, :] = target[n : n + 1, k * POS : (k + 1) * POS]
    begin = start[...].astype(BF16)

    for c in range(3):
        for n in range(IMGS):
            pads[c, n, 0:PAD, :] = jnp.zeros((PAD, CH), BF16)
            pads[c, n, PAD + POS :, :] = jnp.zeros((PAD, CH), BF16)

    def blocks(body):
        for n in range(IMGS):
            for_blocks(lambda at, c: (body(n, at), c)[1], 0)

    def norm_forward(field, slot, shifted, keep):
        norm_stats(field, stats, slot)
        g, b = gain(slot), bias(slot)

        def body(n, at):
            mean = stats[slot, n : n + 1]
            rstd = stats[slot, 8 + n : 9 + n]
            rows = pl.ds(n * POS + at, ROWS)
            y = (field[rows, :] - mean) * rstd * g + b
            if slot != 2:
                y = y * (1.0 / (1.0 + jnp.exp(-y)))
            acts[keep, rows, :] = y.astype(BF16)
            if shifted:
                put_shifts(pads, n, at, y)

        blocks(body)

    def conv(layer):
        acc = None
        for k, (r, c) in enumerate(OFFSETS):
            term = dot(tap(pads, r, c), mat(CONV_AT[layer] + k))
            acc = term if acc is None else acc + term
        return acc


    pump("h0")
    ion = weights_small()
    w_in = ion[0:16].astype(BF16)
    w_out = ion[16:32].astype(BF16)
    for n in range(IMGS):
        h[0, n * POS : (n + 1) * POS, :] = dot(begin[16 * n : 16 * n + 16], w_in, 0, 0)

    def residual(layer, slot, src, dst):
        pump(f"n{slot}")
        norm_forward(h.at[src], slot, True, slot)
        pump(f"c{2 * layer}")
        added = dot(feats, mat(TIME_AT[layer]))
        got = conv(2 * layer)
        for n in range(IMGS):
            c1s[layer, n * POS : (n + 1) * POS, :] = got[n * POS : (n + 1) * POS] + added[n : n + 1]
        pump(f"n{slot + 1}")
        norm_forward(c1s.at[layer], slot + 1, True, slot + 1)
        pump(f"c{2 * layer + 1}")
        h[dst] = h[src] + conv(2 * layer + 1)

    residual(0, 0, 0, 1)
    pump("n2")
    norm_forward(h.at[1], 2, False, 2)
    pump("qkv")
    normal = acts[2]
    for j in range(3):
        qkv[j] = dot(normal, mat(ATTN_AT + j)).astype(BF16)
    scale = HD ** (-0.5)

    def head_mask(hh):
        return lax.broadcasted_iota(jnp.int32, (POS, CH), 1) // HD == hh

    for n in range(IMGS):
        rows = slice(n * POS, (n + 1) * POS)
        pump(f"at{n}")
        tmp[...] = jnp.zeros_like(tmp)

        def head(hh, c):
            mask = head_mask(hh)
            q = jnp.where(mask, qkv[0, rows, :].astype(F32), 0.0).astype(BF16)
            scores = dot(q, qkv[1, rows, :], 1, 1) * scale
            e = jnp.exp(scores - jnp.max(scores, axis=1, keepdims=True))
            p = e / jnp.sum(e, axis=1, keepdims=True)
            probs[n, hh] = p
            o = dot(p.astype(BF16), qkv[2, rows, :])
            tmp[...] = jnp.where(mask, o, tmp[...])
            return c

        lax.fori_loop(0, HEADS, head, 0, unroll=HEADS)
        mixed[rows, :] = tmp[...].astype(BF16)
    pump("ao")
    h[2] = h[1] + dot(mixed[...], mat(ATTN_AT + 3), 1, 1)
    residual(1, 3, 2, 3)
    pump("n5")
    norm_forward(h.at[3], 5, False, 5)
    pump("head")

    dion_ref[...] = jnp.zeros_like(dion_ref)
    loss = jnp.zeros((), F32)
    for n in range(IMGS):
        rows = slice(n * POS, (n + 1) * POS)
        last = acts[5, rows, :]
        pred = dot(w_out, last, 1, 1)
        error = pred - goal[16 * n : 16 * n + 16, :]
        loss = loss + jnp.sum(error * error)
        low = (error * (step_scale * active)).astype(BF16)
        dion_ref[16:32, :] += dot(low, last)
        flow[rows, :] = dot(low, w_out, 0, 0)
    lane = lax.broadcasted_iota(jnp.int32, (8, 128), 1)
    scal_ref[...] = jnp.where(lane == 0, loss * active, jnp.where(lane == 1, plan_cost, 0.0))

    def norm_backward(field, slot, up, finish):
        g, b = gain(slot), bias(slot)
        zero = jnp.zeros((8, CH), F32)

        def fold(v):
            return v.reshape(ROWS // 8, 8, CH).sum(axis=0)

        dbs, dgs = [], []
        for n in range(IMGS):
            mean = stats[slot, n : n + 1]
            rstd = stats[slot, 8 + n : 9 + n]

            def step(at, c):
                rows = pl.ds(n * POS + at, ROWS)
                hat = (field[rows, :] - mean) * rstd
                dz = up[rows, :]
                if slot != 2:
                    y = hat * g + b
                    s = 1.0 / (1.0 + jnp.exp(-y))
                    dz = dz * (s * (1.0 + y * (1.0 - s)))
                    up[rows, :] = dz
                return (c[0] + fold(dz), c[1] + fold(dz * hat))

            db, dg = for_blocks(step, (zero, zero))
            dbs.append(jnp.sum(db, axis=0, keepdims=True))
            dgs.append(jnp.sum(dg, axis=0, keepdims=True))
        dion_ref[32 + 2 * slot : 33 + 2 * slot, :] = dgs[0] + dgs[1]
        dion_ref[33 + 2 * slot : 34 + 2 * slot, :] = dbs[0] + dbs[1]
        sums = group_sum(rows8(*[v * g for v in dbs + dgs])) * (1.0 / (POS * (CH // GROUPS)))
        for n in range(IMGS):
            mean = stats[slot, n : n + 1]
            rstd = stats[slot, 8 + n : 9 + n]
            m1 = sums[n : n + 1]
            m2 = sums[IMGS + n : IMGS + n + 1]

            def step(at, c):
                rows = pl.ds(n * POS + at, ROWS)
                hat = (field[rows, :] - mean) * rstd
                finish(n, at, rstd * (up[rows, :] * g - m1 - hat * m2))
                return c

            for_blocks(step, 0)

    def conv_backward(layer, keep):
        turned = acts[keep].T
        pump(f"w{layer}a")
        for k, (r, c) in enumerate(OFFSETS):
            put(CONV_AT[layer] + k, dot(turned, tap(pads, -r, -c)))
            if CONV_AT[layer] + k + 1 in SPLITS:
                pump(f"w{layer}b")
        pump(f"d{layer}")
        acc = None
        for k, (r, c) in enumerate(OFFSETS):
            term = dot(tap(pads, -r, -c), mat(CONV_AT[layer] + k), 1, 1)
            acc = term if acc is None else acc + term
        smallf[...] = acc

    def add_flow(shifted):
        def finish(n, at, dx):
            rows = pl.ds(n * POS + at, ROWS)
            total = flow[rows, :] + dx
            flow[rows, :] = total
            if shifted:
                put_shifts(pads, n, at, total)

        return finish

    def set_flow(n, at, dx):
        rows = pl.ds(n * POS + at, ROWS)
        flow[rows, :] = dx
        put_shifts(pads, n, at, dx)

    def only_shifts(n, at, dx):
        put_shifts(pads, n, at, dx)

    def residual_backward(layer, slot, src, last_one):
        conv_backward(2 * layer + 1, slot + 1)
        pump(f"b{slot + 1}")
        norm_backward(c1s.at[layer], slot + 1, smallf, only_shifts)
        sums = []
        for n in range(IMGS):
            low = pads[1, n, PAD : PAD + POS, :].astype(F32)
            sums.append(jnp.sum(low, axis=0, keepdims=True))
        one, two, three = split3(rows8(*sums))
        stack = jnp.concatenate([v.astype(F32) for v in (one, two, three)], axis=0).astype(BF16)
        feats3 = jnp.concatenate([feats.astype(F32)] * 3, axis=0).astype(BF16)
        put(TIME_AT[layer], dot(feats3, stack, 0, 0))
        conv_backward(2 * layer, slot)
        pump(f"b{slot}")
        norm_backward(h.at[src], slot, smallf, add_flow(False))

    pump("b5")
    norm_backward(h.at[3], 5, flow, set_flow)
    residual_backward(1, 3, 2, False)

    pump("do")
    dy = flow[...].astype(BF16)
    put(ATTN_AT + 3, dot(dy.T, mixed[...]))
    dqkv[3] = dot(dy, mat(ATTN_AT + 3)).astype(BF16)
    for n in range(IMGS):
        rows = slice(n * POS, (n + 1) * POS)
        pump(f"bt{n}")
        for j in range(3):
            smallf[j % 2 * POS : j % 2 * POS + POS, :] = jnp.zeros((POS, CH), F32)
        tmp[...] = jnp.zeros_like(tmp)

        def head(hh, c):
            mask = head_mask(hh)
            do = jnp.where(mask, dqkv[3, rows, :].astype(F32), 0.0).astype(BF16)
            q = jnp.where(mask, qkv[0, rows, :].astype(F32), 0.0).astype(BF16)
            p = probs[n, hh]
            dp = dot(do, qkv[2, rows, :], 1, 1)
            ds = (p * (dp - jnp.sum(p * dp, axis=1, keepdims=True))).astype(BF16)
            tmp[...] = jnp.where(mask, dot(ds, qkv[1, rows, :]), tmp[...])
            smallf[0:POS, :] += dot(ds, q, 0, 0)
            smallf[POS:, :] += dot(p.astype(BF16), do, 0, 0)
            return c

        lax.fori_loop(0, HEADS, head, 0, unroll=HEADS)
        dqkv[0, rows, :] = (tmp[...] * scale).astype(BF16)
        dqkv[1, rows, :] = (smallf[0:POS, :] * scale).astype(BF16)
        dqkv[2, rows, :] = smallf[POS:, :].astype(BF16)
    pump("proj")
    turned = acts[2].T
    acc = None
    for j in range(3):
        put(ATTN_AT + j, dot(turned, dqkv[j]))
        term = dot(dqkv[j], mat(ATTN_AT + j), 1, 1)
        acc = term if acc is None else acc + term
    smallf[...] = acc
    pump("b2")
    norm_backward(h.at[1], 2, smallf, add_flow(True))
    residual_backward(0, 0, 0, True)
    pump("win")
    for n in range(IMGS):
        rows = slice(n * POS, (n + 1) * POS)
        dion_ref[0:16, :] += dot(begin[16 * n : 16 * n + 16], flow[rows, :].astype(BF16))


def work_space():
    return [
        pltpu.VMEM((4, SPOTS, CH), F32),
        pltpu.VMEM((SPOTS, CH), F32),
        pltpu.VMEM((2, SPOTS, CH), F32),
        pltpu.VMEM((3, IMGS, POS + 2 * PAD, CH), BF16),
        pltpu.VMEM((6, SPOTS, CH), BF16),
        pltpu.VMEM((6, 16, CH), F32),
        pltpu.VMEM((16 * IMGS, POS), F32),
        pltpu.VMEM((16 * IMGS, POS), F32),
        pltpu.VMEM((3, SPOTS, CH), BF16),
        pltpu.VMEM((IMGS, HEADS, POS, POS), F32),
        pltpu.VMEM((SPOTS, CH), BF16),
        pltpu.VMEM((POS, CH), F32),
        pltpu.VMEM((SPOTS, CH), F32),
        pltpu.VMEM((4, SPOTS, CH), BF16),
    ]


def local_kernel(x_ref, z_ref, mine_ref, when_ref, feat_ref, flag_ref, mats, ion_ref, dmats, dion_ref, scal_ref, *work):
    def put(m, value):
        dmats[m] = value

    train(
        x_ref[...], z_ref[...], mine_ref[...], when_ref[0:IMGS, 0:1], feat_ref[...].astype(BF16),
        flag_ref[0, 0], flag_ref[0, 1],
        lambda: ion_ref[...].T, lambda m: mats[m], put, lambda name: None,
        dion_ref, scal_ref, *work,
    )


def local_network(x, z, mine, when, feat, flag, mats, ion):
    whole = pl.BlockSpec(memory_space=pltpu.VMEM)
    return pl.pallas_call(
        local_kernel,
        out_shape=(
            jax.ShapeDtypeStruct((MATS, CH, CH), F32),
            jax.ShapeDtypeStruct((48, CH), F32),
            jax.ShapeDtypeStruct((8, 128), F32),
        ),
        in_specs=[whole] * 5 + [pl.BlockSpec(memory_space=pltpu.SMEM)] + [whole] * 2,
        out_specs=(whole, whole, whole),
        scratch_shapes=work_space(),
        compiler_params=pltpu.CompilerParams(vmem_limit_bytes=56 * 2**20),
    )(x, z, mine, when, feat, flag, mats, ion)


Z, Y, X, C = 4, 2, 2, 2
DEVICES = Z * Y * X * C
PLANE = DEVICES // Z


def fused_kernel(
    micro, batch,
    order_ref, when_ref, images_ref, noises_ref, freq_ref, conv_ref, time_ref, attn_ref, io_ref, norm_ref,
    grads_ref, gion_ref, total_ref,
    mats, dmats, other, give, land, ottmp, ot_ref, otbuf, otwide, xz, ionbuf, dion, diont, ionr, ions, ionq, scal, scalr,
    s1q, s1r, s2q, s2r, zq, zr, expo, kept, gother,
    ot_s, ot_r, ion_s, ion_r, g_s, g_r, r_s, r_r, d_s, d_r, n_s, n_r,
    *work,
):
    dp = lax.axis_index("dp")
    mp = lax.axis_index("mp")
    z, y, x, c = dp // Y, dp % Y, mp // C, mp % C
    flat = mp * (Z * Y) + dp

    def place(z_, y_, x_, c_):
        return (z_ * Y + y_, x_ * C + c_)

    def from_flat(f):
        return (f % (Z * Y), f // (Z * Y))

    sibling = place(z, y, x, 1 - c)
    first = place(z, y * c + (1 - y) * (1 - c), x * (1 - c) + (1 - x) * c, c)
    second = place(z, (1 - y) * c + y * (1 - c), (1 - x) * (1 - c) + x * c, c)

    def remote(src, dst, send, recv, where):
        return pltpu.make_async_remote_copy(
            src_ref=src, dst_ref=dst, send_sem=send, recv_sem=recv, device_id=where, device_id_type=MESH
        )

    barrier = pltpu.get_barrier_semaphore()

    def greet(j, carry):
        pl.semaphore_signal(
            barrier, inc=1, device_id=from_flat((flat + j) % DEVICES), device_id_type=MESH
        )
        return carry

    lax.fori_loop(1, DEVICES, greet, 0)

    def wide(v):
        v = v.astype(BF16).astype(F32)
        none = jnp.zeros_like(v)
        return jnp.where(c == 0, jnp.concatenate([v, none], axis=1), jnp.concatenate([none, v], axis=1)).astype(BF16)

    def pack(m, whole):
        mats[m, x, z, y, c] = wide(jnp.where(c == 0, whole[0:16], whole[16:32]))
        give[m] = wide(jnp.where(c == 0, whole[16:32], whole[0:16]))

    for layer, at in enumerate(CONV_AT):

        def pack_step(k, carry):
            pack(at + k, conv_ref[layer, k])
            return carry

        lax.fori_loop(0, 9, pack_step, 0)
    for layer, at in enumerate(TIME_AT):
        pack(at, time_ref[layer])
    for j in range(4):
        pack(ATTN_AT + j, attn_ref[:, j, :])

    turn = mp - (mp // micro) * (mp - micro + 1)
    row = lax.broadcasted_iota(jnp.int32, (8, images_ref.shape[0]), 0)
    column = lax.broadcasted_iota(jnp.int32, (8, images_ref.shape[0]), 1)
    pick = jnp.zeros(row.shape, F32)
    for n in range(IMGS):
        pick = jnp.where((row == n) & (column == order_ref[turn * IMGS + n]), 1.0, pick)
    own_x = dot(pick.astype(BF16), images_ref[...])
    own_z = noises_ref[turn].astype(F32)
    lines = SUB * POS // 128
    for k in range(lines):
        ottmp[2 * IMGS * k : 2 * IMGS * k + IMGS, :] = own_x[0:IMGS, 128 * k : 128 * k + 128]
        ottmp[2 * IMGS * k + IMGS : 2 * IMGS * (k + 1), :] = own_z[:, 128 * k : 128 * k + 128]
    ot_ref[...] = ottmp[...].astype(BF16)
    io = io_ref[...].reshape(1, io_ref.shape[0])
    norm = norm_ref[...].reshape(1, norm_ref.shape[0])
    zero_row = jnp.zeros((1, 128), F32)
    packed = []
    for r in range(8):
        gap = zero_row[:, 0 : 16 - SUB]
        at = 2 * SUB * r
        packed.append(
            jnp.concatenate(
                [io[:, at : at + SUB], gap, io[:, at + SUB : at + 2 * SUB], gap,
                 norm[:, SUB * r : SUB * r + SUB], zero_row[:, 0 : 128 - 32 - SUB]], axis=1
            )
        )
    ionbuf[x, c, z, y] = jnp.concatenate(packed, axis=0).astype(BF16).astype(F32)
    pl.semaphore_wait(barrier, DEVICES - 1)

    zero_copy = remote(give, land, g_s.at[0, 0], g_r.at[0, 0], sibling)
    def ot_copy(j):
        there = (dp + j) % (Z * Y)
        return remote(ot_ref, otbuf.at[dp], ot_s.at[j], ot_r.at[j], (there, mp))

    def ion_z(j):
        part = ionbuf.at[x, c, z, y]
        return remote(part, part, ion_s.at[j], ion_r.at[j], place((z + j) % Z, y, x, c))

    def ion_u(core):
        part = ionbuf.at[x, c, :, y]
        return remote(part, part, ion_s.at[4], ion_r.at[4], first)

    def ion_v(core):
        part = ionbuf.at[x, 0] if core == 0 else ionbuf.at[:, 1, :, y]
        return remote(part, part, ion_s.at[5], ion_r.at[5], second)

    def ion_c(core):
        part = ionbuf.at[:, c]
        return remote(part, part, ion_s.at[6], ion_r.at[6], sibling)

    def merge(m, carry):
        mats[m, x, z, y, c] = mats[m, x, z, y, c] + land[m]
        return carry

    def span(i):
        return pl.ds(CHUNKS[i][0], CHUNKS[i][1])

    def z_copy(i, j):
        part = mats.at[span(i), x, z, y, c]
        return remote(part, part, g_s.at[i + 1, j], g_r.at[i + 1, j], place((z + j) % Z, y, x, c))

    def u_copy(i):
        part = mats.at[span(i), x, :, y, c]
        return remote(part, part, g_s.at[i + 1, 4], g_r.at[i + 1, 4], first)

    def v_copy(i, core):
        part = mats.at[span(i), x, :, :, 0] if core == 0 else mats.at[span(i), :, :, y, 1]
        return remote(part, part, g_s.at[i + 1, 5], g_r.at[i + 1, 5], second)

    def e_copy(i, j):
        part = mats.at[span(i), :, z, :, c]
        return remote(part, part, g_s.at[i + 1, j], g_r.at[i + 1, j], place((z + j) % Z, y, x, c))

    def a_copy(i):
        part = mats.at[span(i), x, z, y, c]
        return remote(part, part, g_s.at[i + 1, 4], g_r.at[i + 1, 4], first)

    def b_copy(i, core):
        part = mats.at[span(i), x, z, :, 0] if core == 0 else mats.at[span(i), :, z, y, 1]
        return remote(part, part, g_s.at[i + 1, 5], g_r.at[i + 1, 5], second)

    def c_copy(i):
        part = mats.at[span(i), :, :, :, c]
        return remote(part, part, g_s.at[i + 1, 6], g_r.at[i + 1, 6], sibling)

    def on_core(act):
        for core in range(C):
            pl.when(c == core)(functools.partial(act, core))

    def start_all(copies):
        for copy in copies:
            copy.start()

    def wait_all(copies):
        for copy in copies:
            copy.wait()

    peers = range(1, Z)

    def gather_step(kind, i):
        if kind == "A":
            a_copy(i).start()
        elif kind == "B":
            a_copy(i).wait()
            on_core(lambda core: b_copy(i, core).start())
        elif kind == "E":
            on_core(lambda core: b_copy(i, core).wait())
            start_all(e_copy(i, j) for j in peers)
        elif kind == "Z":
            start_all(z_copy(i, j) for j in peers)
        elif kind == "U":
            wait_all(z_copy(i, j) for j in peers)
            u_copy(i).start()
        elif kind == "V":
            u_copy(i).wait()
            on_core(lambda core: v_copy(i, core).start())
        elif kind == "C":
            if i in EARLY:
                wait_all(e_copy(i, j) for j in peers)
            else:
                on_core(lambda core: v_copy(i, core).wait())
            c_copy(i).start()
        elif kind == "W":
            c_copy(i).wait()

    def other_step(kind):
        if kind == "zero":
            zero_copy.start()
        elif kind == "merge":
            zero_copy.wait()
            lax.fori_loop(0, MATS, merge, 0, unroll=6)
        elif kind == "ot":
            start_all(ot_copy(j) for j in range(1, Z * Y))
            otbuf[dp] = ot_ref[...]
        elif kind == "otw":
            wait_all(ot_copy(j) for j in range(1, Z * Y))
        elif kind == "iz":
            start_all(ion_z(j) for j in peers)
        elif kind == "iu":
            wait_all(ion_z(j) for j in peers)
            ion_u(0).start()
        elif kind == "iv":
            ion_u(0).wait()
            on_core(lambda core: ion_v(core).start())
        elif kind == "ic":
            on_core(lambda core: ion_v(core).wait())
            ion_c(0).start()
        elif kind == "iw":
            ion_c(0).wait()
        elif kind == "da":
            wait_all(dion_copy(j) for j in range(1, X * C))
            ionr[mp] = diont[mp]
            ions[...] = ionr[0] + ionr[1] + ionr[2] + ionr[3]
            start_all(dion_again(j) for j in range(1, Z * Y))
            ionq[dp] = ions[dp]
        elif kind == "db":
            wait_all(dion_again(j) for j in range(1, Z * Y))

    def do(steps):
        for kind in steps:
            if kind[1:].isdigit():
                i = int(kind[1:])
                if kind[0] in "RSTYXF":
                    reduce_step(kind[0], i)
                else:
                    gather_step(kind[0], i)
            else:
                other_step(kind)

    def pump(name):
        do(PLAN.get(name, ()))

    pump("start")
    rows = ot_ref.shape[0]
    for j in range(Z * Y):
        otwide[pl.ds(j * rows, rows), :] = otbuf[j].astype(F32)
    for r in range(2 * IMGS):
        for k in range(lines):
            xz[r // IMGS, (r % IMGS) * Z * Y : (r % IMGS + 1) * Z * Y, k * 128 : (k + 1) * 128] = otwide[
                pl.ds(k * 2 * IMGS + r, Z * Y, stride=rows), :
            ]
    spot = lax.broadcasted_iota(jnp.int32, (8, batch), 0)
    column = lax.broadcasted_iota(jnp.int32, (8, batch), 1)
    mine = jnp.where((column == spot * (Z * Y) + dp) & (spot < IMGS), 1.0, 0.0)
    active = jnp.where(mp < micro, 1.0, 0.0)

    def mat(m):
        return jnp.concatenate([mats[m, k].reshape(CH, 128) for k in range(X)], axis=1)

    def put(m, value):
        for k in range(X):
            dmats[m, k] = value[:, 128 * k : 128 * k + 128].reshape(Z, Y, C, 16, 128)

    mine_a = x * (1 - c) + y * c
    mine_b = y * (1 - c) + x * c

    def xy(a, b):
        return a * (1 - c) + b * c, b * (1 - c) + a * c

    def r_copy(i):
        return remote(
            dmats.at[span(i), :, :, :, 1 - c], other.at[span(i)], r_s.at[i, 0], r_r.at[i, 0], sibling
        )

    def base(i, per):
        return CHUNKS[i][0] * per + i

    def one_copy(i):
        part = pl.ds(base(i, 8), CHUNKS[i][1] * 8 + 1)
        return remote(s1q.at[part], s1r.at[part], r_s.at[i, 1], r_r.at[i, 1], second)

    def two_copy(i):
        part = pl.ds(base(i, 4), CHUNKS[i][1] * 4 + 1)
        return remote(s2q.at[part], s2r.at[part], r_s.at[i, 2], r_r.at[i, 2], first)

    def three_copy(i, j):
        part = pl.ds(base(i, 1), CHUNKS[i][1] + 1)
        return remote(
            zq.at[j - 1, part], zr.at[j - 1, part], r_s.at[i, 2 + j], r_r.at[i, 2 + j], place((z + j) % Z, y, x, c)
        )

    def four_copy(i):
        return remote(kept.at[span(i)], gother.at[span(i)], r_s.at[i, 6], r_r.at[i, 6], sibling)

    def exponent(tiles):
        top = jnp.max(jnp.abs(tiles[0]), axis=0, keepdims=True)
        for t in tiles[1:]:
            top = jnp.maximum(top, jnp.max(jnp.abs(t), axis=0, keepdims=True))
        return jnp.floor(jnp.log2(jnp.maximum(top, 1e-30))) + 1.0

    def coded(tile, power):
        return jnp.round(tile * (LEVELS * jnp.exp2(-power))).astype(jnp.int32).astype(jnp.int16)

    def decoded(tile, unit):
        return tile.astype(jnp.int32).astype(F32) * unit

    def units(ref, at, slot):
        expo[slot] = jnp.exp2(ref[at].astype(jnp.int32).astype(F32)) * (1.0 / LEVELS)

    def powers(ref, at):
        ref[at] = expo[0].astype(jnp.int32).astype(jnp.int16)

    def stage_one(i):
        r_copy(i).wait()
        first_m, count = CHUNKS[i]
        start = base(i, 8)

        def step(k, carry):
            m = first_m + k
            tiles = []
            for b in range(2):
                x_, y_ = xy(1 - mine_a, b)
                for zz in range(Z):
                    tiles.append(dmats[m, x_, zz, y_, c] + other[m, x_, zz, y_])
            power = exponent(tiles)
            expo[0, pl.ds(k, 1), :] = power
            for t, tile in enumerate(tiles):
                s1q[start + k * 8 + t] = coded(tile, power)
            return carry

        lax.fori_loop(0, count, step, 0, unroll=True)
        powers(s1q, start + count * 8)
        one_copy(i).start()

    def stage_two(i):
        one_copy(i).wait()
        first_m, count = CHUNKS[i]
        start, start_one = base(i, 4), base(i, 8)
        units(s1r, start_one + count * 8, 1)

        def step(k, carry):
            m = first_m + k
            unit = expo[1, pl.ds(k, 1), :]
            x_, y_ = xy(mine_a, 1 - mine_b)
            tiles = []
            for zz in range(Z):
                got = decoded(s1r[start_one + k * 8 + (1 - mine_b) * 4 + zz], unit)
                tiles.append(dmats[m, x_, zz, y_, c] + other[m, x_, zz, y_] + got)
            power = exponent(tiles)
            expo[0, pl.ds(k, 1), :] = power
            for t, tile in enumerate(tiles):
                s2q[start + k * 4 + t] = coded(tile, power)
            return carry

        lax.fori_loop(0, count, step, 0, unroll=True)
        powers(s2q, start + count * 4)
        two_copy(i).start()

    def stage_three(i):
        two_copy(i).wait()
        first_m, count = CHUNKS[i]
        start, start_one, start_two = base(i, 1), base(i, 8), base(i, 4)
        units(s1r, start_one + count * 8, 1)
        units(s2r, start_two + count * 4, 2)

        def step(k, carry):
            m = first_m + k
            unit_one = expo[1, pl.ds(k, 1), :]
            unit_two = expo[2, pl.ds(k, 1), :]

            def tile(zz):
                return (
                    dmats[m, x, zz, y, c]
                    + other[m, x, zz, y]
                    + decoded(s1r[start_one + k * 8 + mine_b * 4 + zz], unit_one)
                    + decoded(s2r[start_two + k * 4 + zz], unit_two)
                )

            tiles = [tile((z + j) % Z) for j in range(1, Z)]
            power = exponent(tiles)
            expo[0, pl.ds(k, 1), :] = power
            for j in range(1, Z):
                zq[j - 1, start + k] = coded(tiles[j - 1], power)
            kept[m] = tile(z)
            return carry

        lax.fori_loop(0, count, step, 0, unroll=True)
        for j in range(1, Z):
            powers(zq.at[j - 1], start + count)
        for j in range(1, Z):
            three_copy(i, j).start()

    def stage_four(i):
        for j in range(1, Z):
            three_copy(i, j).wait()
        first_m, count = CHUNKS[i]
        start = base(i, 1)
        for j in range(1, Z):
            units(zr.at[j - 1], start + count, j)

        def step(k, carry):
            m = first_m + k
            total = kept[m]
            for j in range(1, Z):
                total = total + decoded(zr[j - 1, start + k], expo[j, pl.ds(k, 1), :])
            kept[m] = total
            return carry + total * total

        square = lax.fori_loop(0, count, step, jnp.zeros((16, 128), F32), unroll=True)
        four_copy(i).start()
        return square

    squares = []

    def reduce_step(kind, i):
        if kind == "R":
            r_copy(i).start()
        elif kind == "S":
            stage_one(i)
        elif kind == "T":
            stage_two(i)
        elif kind == "Y":
            stage_three(i)
        elif kind == "X":
            squares.append(stage_four(i))
        else:
            finish(i)

    def finish(i):
        four_copy(i).wait()

        def step(k, carry):
            m = CHUNKS[i][0] + k
            for half in range(C):
                tile = jnp.where(c == half, kept[m], gother[m])
                grads_ref[m, half * 16 : half * 16 + 16, :] = jnp.where(c == 0, tile[:, 0:64], tile[:, 64:128])
            return carry

        lax.fori_loop(0, CHUNKS[i][1], step, 0, unroll=True)

    seat = lax.broadcasted_iota(jnp.int32, (8, 1), 0)
    times = jnp.zeros((8, 1), F32)
    for n in range(IMGS):
        index = when_ref[pl.ds(turn, 1), n : n + 1]
        times = jnp.where(seat == n, (index + 0.5) / NT, times)
    angles = 1000.0 * times * freq_ref[...]
    feats = jnp.where(seat < IMGS, jnp.concatenate([jnp.sin(angles), jnp.cos(angles)], axis=1), 0.0).astype(BF16)
    train(
        xz[0].astype(BF16), xz[1].astype(BF16), mine, times[0:IMGS], feats, active, 2.0 / (micro * batch),
        lambda: ionbuf[...].reshape(CH, 128).T, mat, put, pump, dion, scal, *work,
    )

    diont[...] = (
        jnp.concatenate([dion[...], jnp.zeros((128 - 48, CH), F32)], axis=0).T.reshape(X * C, Z * Y, 8, 128)
    )

    def dion_copy(j):
        there = (mp + j) % (X * C)
        return remote(diont.at[there], ionr.at[mp], d_s.at[j], d_r.at[j], (dp, there))

    def dion_again(j):
        there = (dp + j) % (Z * Y)
        return remote(ions.at[there], ionq.at[dp], d_s.at[X * C + j], d_r.at[X * C + j], (there, mp))

    start_all(dion_copy(j) for j in range(1, X * C))
    pump("tail")
    small = jnp.sum(ionq[...], axis=0)
    gion_ref[...] = small
    square = small * small
    for part in squares:
        square = square + part[0:8] + part[8:16]

    loss, plan_cost = scal[0:1, 0:1], scal[0:1, 1:2]
    lane = lax.broadcasted_iota(jnp.int32, (8, 128), 1)
    line = lax.broadcasted_iota(jnp.int32, (8, 128), 0)
    tile = jnp.where(line == 7, 0.0, square) + jnp.where(line == 0, pltpu.roll(square, 1, 0), 0.0)
    tile = jnp.where((line == 7) & (lane == mp) & (mp < micro), loss, tile)
    tile = jnp.where((line == 7) & (lane == micro + mp) & (mp < micro) & (dp == 0), plan_cost, tile)
    scal[...] = tile
    spread = z * PLANE + y * (X * C) + mp
    scalr[spread] = tile

    def n_start(j, carry):
        there = (spread + j) % DEVICES
        remote(
            scal, scalr.at[spread], n_s.at[0], n_r.at[0],
            (there // PLANE * Y + there % PLANE // (X * C), there % (X * C)),
        ).start()
        return carry

    for low, high in ((2 * PLANE, DEVICES), (PLANE, 2 * PLANE), (1, PLANE)):
        lax.fori_loop(low, high, n_start, 0)
    pump("end")
    rest = pl.ds(0, DEVICES - 1)
    remote(scalr.at[rest], scalr.at[rest], n_s.at[0], n_r.at[0], sibling).wait()
    total_ref[...] = jnp.sum(scalr[...], axis=0)


def fused_network(micro, batch, order, when, images, noises, conv, time, attn, io, norm):
    whole = pl.BlockSpec(memory_space=pltpu.VMEM)
    scalar = pl.BlockSpec(memory_space=pltpu.SMEM)
    blocks = (X, Z, Y)
    rows = 2 * IMGS * SUB * POS // 128
    dma = pltpu.SemaphoreType.DMA
    count = len(CHUNKS)
    half = CH // 2
    freq = np.exp(np.float32(-math.log(10000.0)) * np.arange(half, dtype=np.float32) / np.float32(half))
    freq = jnp.asarray(freq.reshape(1, half))
    return pl.pallas_call(
        functools.partial(fused_kernel, micro, batch),
        out_shape=(
            jax.ShapeDtypeStruct((MATS, 32, 64), F32),
            jax.ShapeDtypeStruct((8, 128), F32),
            jax.ShapeDtypeStruct((8, 128), F32),
        ),
        in_specs=[scalar] + [whole] * 9,
        out_specs=(whole, whole, whole),
        scratch_shapes=[
            pltpu.VMEM((MATS,) + blocks + (C, 16, 128), BF16),
            pltpu.VMEM((MATS,) + blocks + (C, 16, 128), F32),
            pltpu.VMEM((MATS,) + blocks + (16, 128), F32),
            pltpu.VMEM((MATS, 16, 128), BF16),
            pltpu.VMEM((MATS, 16, 128), BF16),
            pltpu.VMEM((rows, 128), F32),
            pltpu.VMEM((rows, 128), BF16),
            pltpu.VMEM((Z * Y, rows, 128), BF16),
            pltpu.VMEM((Z * Y * rows, 128), F32),
            pltpu.VMEM((2, batch, SUB * POS), F32),
            pltpu.VMEM((X, C, Z, Y, 8, 128), F32),
            pltpu.VMEM((48, CH), F32),
            pltpu.VMEM((X * C, Z * Y, 8, 128), F32),
            pltpu.VMEM((X * C, Z * Y, 8, 128), F32),
            pltpu.VMEM((Z * Y, 8, 128), F32),
            pltpu.VMEM((Z * Y, 8, 128), F32),
            pltpu.VMEM((8, 128), F32),
            pltpu.VMEM((DEVICES, 8, 128), F32),
            pltpu.VMEM((MATS * 8 + count, 16, 128), jnp.int16),
            pltpu.VMEM((MATS * 8 + count, 16, 128), jnp.int16),
            pltpu.VMEM((MATS * 4 + count, 16, 128), jnp.int16),
            pltpu.VMEM((MATS * 4 + count, 16, 128), jnp.int16),
            pltpu.VMEM((Z - 1, MATS + count, 16, 128), jnp.int16),
            pltpu.VMEM((Z - 1, MATS + count, 16, 128), jnp.int16),
            pltpu.VMEM((Z, 16, 128), F32),
            pltpu.VMEM((MATS, 16, 128), F32),
            pltpu.VMEM((MATS, 16, 128), F32),
            dma((Z * Y,)), dma((Z * Y,)),
            dma((7,)), dma((7,)),
            dma((count + 1, 7)), dma((count + 1, 7)),
            dma((count, 7)), dma((count, 7)),
            dma((X * C + Z * Y,)), dma((X * C + Z * Y,)),
            dma((1,)), dma((1,)),
        ] + work_space(),
        compiler_params=pltpu.CompilerParams(
            vmem_limit_bytes=60 * 2**20, collective_id=0, has_side_effects=True
        ),
    )(order, when, images, noises, freq, conv, time, attn, io, norm)


def time_features(time_index):
    times = (time_index.astype(jnp.float32) + 0.5) / NT
    half = CH // 2
    frequency = jnp.exp(-math.log(10000.0) * jnp.arange(half, dtype=jnp.float32) / half)
    angles = 1000.0 * times[:, None] * frequency[None, :]
    return jnp.concatenate([jnp.sin(angles), jnp.cos(angles)], axis=1)


def adam_update(weight, first, second, average, gradient, rate):
    first = BETA_ONE * first + (1 - BETA_ONE) * gradient
    second = BETA_TWO * second + (1 - BETA_TWO) * gradient * gradient
    ratio = first / (1 - BETA_ONE**STEP) / (jnp.sqrt(second / (1 - BETA_TWO**STEP)) + ADAM_EPS)
    weight = weight - rate * (ratio + WEIGHT_DECAY * weight)
    average = EMA_DECAY * average + (1 - EMA_DECAY) * weight
    return (weight, first, second, average)


def adam_kernel(grads_ref, gion_ref, total_ref, *refs):
    old, new = refs[:20], refs[20:40]
    loss_ref, cost_ref, norm_ref = refs[40:]
    norm = jnp.sqrt(jnp.sum(total_ref[0:7], axis=(0, 1), keepdims=True))
    scale = CLIP_NORM / jnp.maximum(norm, CLIP_NORM)

    def update(kind, at, gradient):
        got = adam_update(*[old[5 * part + kind][at] for part in range(4)], gradient * scale, RATES[kind])
        for part in range(4):
            new[5 * part + kind][at] = got[part]

    for layer, start in enumerate(CONV_AT):
        update(1, (layer,), grads_ref[start : start + 9])
    for layer, start in enumerate(TIME_AT):
        update(2, (layer,), grads_ref[start])
    for j in range(4):
        update(3, (slice(None), j), grads_ref[ATTN_AT + j])
    tile = gion_ref[...]
    own = old[0].shape[0] // (2 * SUB)
    for kind, pieces in ((0, (0, 16)), (4, (32,))):
        flat = [tile[r : r + 1, at : at + SUB] for r in range(own) for at in pieces]
        flat = jnp.concatenate(flat, axis=1)
        got = adam_update(
            *[old[5 * part + kind][...].reshape(flat.shape) for part in range(4)], flat * scale, RATES[kind]
        )
        for part in range(4):
            new[5 * part + kind][...] = got[part].reshape(old[kind].shape)
    micro = loss_ref.shape[0]
    for m in range(micro):
        loss_ref[m] = total_ref[7, m]
        cost_ref[m] = total_ref[7, micro + m]
    norm_ref[0] = norm[0, 0]


def adam(micro, grads, gion, total, state):
    whole = pl.BlockSpec(memory_space=pltpu.VMEM)
    scalar = pl.BlockSpec(memory_space=pltpu.SMEM)

    return pl.pallas_call(
        adam_kernel,
        out_shape=tuple(jax.ShapeDtypeStruct(v.shape, F32) for v in state)
        + (jax.ShapeDtypeStruct((micro,), F32),) * 2
        + (jax.ShapeDtypeStruct((1,), F32),),
        in_specs=[whole] * (3 + len(state)),
        out_specs=(whole,) * len(state) + (scalar,) * 3,
        compiler_params=pltpu.CompilerParams(vmem_limit_bytes=60 * 2**20),
    )(grads, gion, total, *state)


def pack_mats(conv, time, attn):
    return jnp.concatenate(
        [time[0:1], conv[0], conv[1], attn.transpose(1, 0, 2), time[1:2], conv[2], conv[3]], axis=0
    )


def unpack_mats(mats):
    conv = jnp.stack([mats[at : at + 9] for at in CONV_AT])
    time = jnp.stack([mats[at] for at in TIME_AT])
    return conv, time, mats[ATTN_AT : ATTN_AT + 4].transpose(1, 0, 2)


def pack_small(io, norm):
    own = norm.shape[0] // SUB
    io = io.reshape(own, 2, SUB)
    norm = norm.reshape(own, SUB)
    gap = jnp.zeros((own, 16 - SUB), io.dtype)
    return jnp.concatenate(
        [io[:, 0], gap, io[:, 1], gap, norm, gap, jnp.zeros((own, 80), io.dtype)], axis=1
    )


def body(
    fused,
    images, noises, order, time_index, io_weight, conv_weight, time_weight, attn_weight, norm_param,
    io_first, conv_first, time_first, attn_first, norm_first,
    io_second, conv_second, time_second, attn_second, norm_second,
    io_average, conv_average, time_average, attn_average, norm_average,
):
    rank = lax.axis_index("mp")
    place = lax.axis_index("dp")
    micro, count, depth = noises.shape
    batch = count * lax.axis_size("dp")
    turn = jnp.minimum(rank, micro - 1)
    weights = (io_weight, conv_weight, time_weight, attn_weight, norm_param)
    firsts = (io_first, conv_first, time_first, attn_first, norm_first)
    seconds = (io_second, conv_second, time_second, attn_second, norm_second)
    averages = (io_average, conv_average, time_average, attn_average, norm_average)
    if fused:
        grads, gion, total = fused_network(
            micro, batch, order, time_index.astype(F32), images, noises, conv_weight, time_weight, attn_weight, io_weight, norm_param
        )
        out = adam(micro, grads, gion, total, weights + firsts + seconds + averages)
        return out[:22] + (out[22].reshape(()),)
    chosen = lax.dynamic_slice_in_dim(order, turn * count, count, 0)
    own_x = jnp.take(images, chosen, axis=0)
    own_z = lax.dynamic_index_in_dim(noises, turn, 0, keepdims=False)
    when = lax.dynamic_index_in_dim(time_index, turn, 0, keepdims=False)
    feat = jnp.pad(time_features(when).astype(BF16).astype(F32), ((0, 8 - count), (0, 0)))
    times = (when.astype(F32) + 0.5) / NT
    times = jnp.pad(jnp.broadcast_to(times[:, None], (count, 128)), ((0, 8 - count), (0, 0)))
    mats = pack_mats(conv_weight, time_weight, attn_weight).astype(BF16)
    mats = lax.all_gather(lax.all_gather(mats, "dp", axis=1, tiled=True), "mp", axis=2, tiled=True)
    ion = pack_small(io_weight, norm_param).astype(BF16)
    ion = lax.all_gather(ion, ("mp", "dp"), axis=0, tiled=True).astype(F32)
    both = lax.all_gather(jnp.stack([own_x, own_z]), "dp", axis=1, tiled=True)
    spot = jnp.arange(8)[:, None]
    mine = ((jnp.arange(batch)[None, :] == place * count + spot) & (spot < count)).astype(F32)
    active = (rank < micro).astype(F32)
    flag = jnp.stack([active, jnp.float32(2.0 / (micro * batch))]).reshape(1, 2)
    dmats, dion, scal = local_network(both[0], both[1], mine, times, feat, flag, mats, ion)
    dmats = lax.psum_scatter(dmats, "dp", scatter_dimension=1, tiled=True)
    dmats = lax.psum_scatter(dmats, "mp", scatter_dimension=2, tiled=True)
    dion = lax.psum_scatter(dion.T, ("mp", "dp"), scatter_dimension=0, tiled=True)
    hot = (jnp.arange(micro) == rank).astype(F32)
    squares = jnp.sum(dmats * dmats) + jnp.sum(dion * dion)
    total_sq, loss_sum, cost_sum = lax.psum(
        (squares, hot * scal[0, 0], jnp.where(place == 0, hot * scal[0, 1], 0.0)), ("dp", "mp")
    )
    grad_norm = jnp.sqrt(total_sq)
    scale = CLIP_NORM / jnp.maximum(grad_norm, CLIP_NORM)
    conv_grad, time_grad, attn_grad = unpack_mats(dmats)
    grads = (
        jnp.concatenate([dion[:, None, 0:SUB], dion[:, None, 16 : 16 + SUB]], axis=1).reshape(-1),
        conv_grad,
        time_grad,
        attn_grad,
        dion[:, 32 : 32 + SUB].reshape(-1),
    )
    results = [
        adam_update(weights[kind], firsts[kind], seconds[kind], averages[kind], grads[kind] * scale, RATES[kind])
        for kind in range(5)
    ]
    return tuple(results[kind][part] for part in range(4) for kind in range(5)) + (loss_sum, cost_sum, grad_norm)


def solution(mesh):
    flat = P(("mp", "dp"))
    state = (flat, P(None, None, "dp", "mp"), P(None, "dp", "mp"), P("dp", None, "mp"), flat)
    fused = mesh.shape["dp"] == Z * Y and mesh.shape["mp"] == X * C
    return jax.shard_map(
        functools.partial(body, fused),
        mesh=mesh,
        in_specs=(P("dp", None), P(None, "dp", None), P("dp"), P(None, "dp")) + state * 4,
        out_specs=state * 4 + (P(), P(), P()),
        check_vma=False,
    )
```

```python
import functools
import math

import jax
import numpy as np
import jax.numpy as jnp
from jax import lax
from jax.experimental import pallas as pl
from jax.experimental.pallas import tpu as pltpu
from jax.sharding import PartitionSpec as P

CH = 256
GROUPS = 32
HEADS = 4
HD = 64
SUB = 12
POS = 256
SIDE = 16
SINK = 10
NT = 1000
STEP = 5
MATS = 42
CONV_AT = (1, 10, 24, 33)
TIME_AT = (0, 23)
ATTN_AT = 19
CHUNKS = ((0, 5), (5, 5), (10, 5), (15, 4), (19, 4), (23, 5), (28, 5), (33, 5), (38, 4))
SPLITS = (5, 15, 28, 38)
EARLY = (4, 8)
PLAN = {
    "start": ("zero", "ot", "merge", "Z3", "A4", "Z5", "Z0", "iz", "A8", "U3", "B4", "Z2", "Z1", "U5", "Z7", "iu",
        "B8", "U0", "V3", "U2", "iv", "Z6", "U1", "V0", "otw", "E4", "U7", "U6", "V1", "ic", "C3"),
    "sink": ("V2", "E8", "C0", "W3", "V6"),
    "h0": ("V5", "iw", "C1"),
    "c0": ("C4", "V7", "W0", "C2", "W1"),
    "c1": ("C6", "W4", "W2"),
    "at0": ("C5",),
    "n3": ("C8", "W6", "C7"),
    "c2": ("W5",),
    "c3": ("W8", "W7"),
    "w3b": ("R7",),
    "d3": ("R8",),
    "w2b": ("R5", "S7"),
    "d2": ("R6",),
    "b3": ("S8",),
    "do": ("S5",),
    "bt1": ("S6",),
    "b2": ("R4", "T7"),
    "d1": ("T8", "R3", "T5", "R2", "S4"),
    "w0a": ("T6",),
    "w0b": ("S3",),
    "d0": ("R1", "Y7", "S2", "R0"),
    "b0": ("T4", "Y5", "S1", "Y6", "S0", "T3", "Y8"),
    "win": ("X7", "Y4", "T2", "T1"),
    "tail": ("X6", "Y3", "T0", "Y2", "da", "Y1", "X3", "Y0", "F6", "X4", "X5", "X1", "X2", "X8", "db", "X0"),
    "end": ("F8", "F5", "F2", "F7", "F3", "F1", "F4", "F0"),
}
LEVELS = 32000.0
MESH = pl.DeviceIdType.MESH


EPS_NORM = 1e-05
SINK_EPS = 0.01
CLIP_NORM = 1.0
BETA_ONE = 0.5
BETA_TWO = 0.5
ADAM_EPS = 1e-08
WEIGHT_DECAY = 0.01
EMA_DECAY = 0.9
RATES = (0.06, 0.01, 0.03, 0.03, 0.3)
F32 = jnp.float32
BF16 = jnp.bfloat16
ROWS = 32
PAD = SIDE
IMGS = 2
SPOTS = IMGS * POS


def dot(a, b, ca=1, cb=0):
    return lax.dot_general(a, b, (((ca,), (cb,)), ((), ())), preferred_element_type=F32)


def split3(v):
    one = v.astype(BF16)
    rest = v - one.astype(F32)
    two = rest.astype(BF16)
    three = (rest - two.astype(F32)).astype(BF16)
    return one, two, three


def group_sum(v):
    per = CH // GROUPS
    rows = lax.broadcasted_iota(jnp.int32, (CH, CH), 0) // per
    cols = lax.broadcasted_iota(jnp.int32, (CH, CH), 1) // per
    ones = jnp.where(rows == cols, 1.0, 0.0).astype(BF16)
    one, two, three = split3(v)
    got = dot(jnp.concatenate([one.astype(F32), two.astype(F32), three.astype(F32)], axis=0).astype(BF16), ones)
    n = v.shape[0]
    return got[:n] + got[n : 2 * n] + got[2 * n :]


def rows8(*rows):
    return jnp.concatenate(list(rows) + [jnp.zeros((8 - len(rows), CH), F32)], axis=0)


def for_blocks(step, init):
    return lax.fori_loop(0, POS // ROWS, lambda i, c: step(pl.multiple_of(i * ROWS, ROWS), c), init, unroll=True)


def norm_stats(field, stats, slot):
    zero = jnp.zeros((8, CH), F32)

    def fold(v):
        return v.reshape(ROWS // 8, 8, CH).sum(axis=0)

    sums = []
    for n in range(IMGS):
        acc = for_blocks(lambda at, c: c + fold(field[pl.ds(n * POS + at, ROWS), :]), zero)
        sums.append(jnp.sum(acc, axis=0, keepdims=True))
    scale = 1.0 / (POS * (CH // GROUPS))
    means = group_sum(rows8(*sums)) * scale
    sums = []
    for n in range(IMGS):
        mean = means[n : n + 1]

        def step(at, c):
            d = field[pl.ds(n * POS + at, ROWS), :] - mean
            return c + fold(d * d)

        sums.append(jnp.sum(for_blocks(step, zero), axis=0, keepdims=True))
    devs = group_sum(rows8(*sums)) * scale
    stats[slot, 0:8] = means
    stats[slot, 8:16] = lax.rsqrt(devs + EPS_NORM)


def put_shifts(pads, n, at, value):
    col = lax.broadcasted_iota(jnp.int32, value.shape, 0) % SIDE
    left = jnp.where(col == 0, 0.0, pltpu.roll(value, 1, 0))
    right = jnp.where(col == SIDE - 1, 0.0, pltpu.roll(value, value.shape[0] - 1, 0))
    rows = pl.ds(PAD + at, value.shape[0])
    pads[0, n, rows, :] = left.astype(BF16)
    pads[1, n, rows, :] = value.astype(BF16)
    pads[2, n, rows, :] = right.astype(BF16)


def tap(pads, r, c):
    return pads[c + 1, :, PAD + SIDE * r : PAD + SIDE * r + POS, :].reshape(SPOTS, CH)


OFFSETS = [(r, c) for r in (-1, 0, 1) for c in (-1, 0, 1)]


def train(
    x, z, mine, times, feats, active, step_scale, weights_small, mat, put, pump,
    dion_ref, scal_ref,
    h, flow, c1s, pads, acts, stats, start, goal, qkv, probs, mixed, tmp, smallf, dqkv,
):
    batch, depth = x.shape
    def gain(s):
        return ion[32 + 2 * s : 33 + 2 * s]

    def bias(s):
        return ion[33 + 2 * s : 34 + 2 * s]

    pump("pair")
    gram = dot(x, z, 1, 1)
    xf = x.astype(F32)
    zf = z.astype(F32)
    sq_x = jnp.sum(xf * xf, axis=1, keepdims=True)
    sq_z = jnp.sum(zf * zf, axis=1, keepdims=True)
    eye = lax.broadcasted_iota(jnp.int32, (batch, batch), 0) == lax.broadcasted_iota(jnp.int32, (batch, batch), 1)
    sq_z = jnp.sum(jnp.where(eye, sq_z, 0.0), axis=0, keepdims=True)
    cost = (sq_x + sq_z - 2.0 * gram) / depth
    affinity = 2.0 * gram / (depth * SINK_EPS)
    kern = jnp.exp(affinity - jnp.max(affinity, axis=1, keepdims=True))
    share = 1.0 / batch
    pump("sink")

    def sweep(i, c):
        left, right = c
        left = share / jnp.sum(kern * right, axis=1, keepdims=True)
        right = share / jnp.sum(left * kern, axis=0, keepdims=True)
        return left, right

    left, right = lax.fori_loop(0, SINK, sweep, (jnp.ones((batch, 1), F32), jnp.ones((1, batch), F32)))
    scaled = kern * right
    plan_cost = jnp.sum(left * scaled * cost)
    mixing = (scaled / jnp.sum(scaled, axis=1, keepdims=True)).astype(BF16)
    d = mine.astype(BF16)
    mix = dot(d, mixing).astype(BF16)
    paired = dot(mix, z)[0:IMGS]
    pixels = dot(d, x)[0:IMGS]
    inputs = ((1.0 - times) * paired + times * pixels).astype(BF16).astype(F32)
    target = pixels - paired
    start[...] = jnp.zeros_like(start)
    goal[...] = jnp.zeros_like(goal)
    for n in range(IMGS):
        for k in range(SUB):
            start[16 * n + k : 16 * n + k + 1, :] = inputs[n : n + 1, k * POS : (k + 1) * POS]
            goal[16 * n + k : 16 * n + k + 1, :] = target[n : n + 1, k * POS : (k + 1) * POS]
    begin = start[...].astype(BF16)

    for c in range(3):
        for n in range(IMGS):
            pads[c, n, 0:PAD, :] = jnp.zeros((PAD, CH), BF16)
            pads[c, n, PAD + POS :, :] = jnp.zeros((PAD, CH), BF16)

    def blocks(body):
        for n in range(IMGS):
            for_blocks(lambda at, c: (body(n, at), c)[1], 0)

    def norm_forward(field, slot, shifted, keep):
        norm_stats(field, stats, slot)
        g, b = gain(slot), bias(slot)

        def body(n, at):
            mean = stats[slot, n : n + 1]
            rstd = stats[slot, 8 + n : 9 + n]
            rows = pl.ds(n * POS + at, ROWS)
            y = (field[rows, :] - mean) * rstd * g + b
            if slot != 2:
                y = y * (1.0 / (1.0 + jnp.exp(-y)))
            acts[keep, rows, :] = y.astype(BF16)
            if shifted:
                put_shifts(pads, n, at, y)

        blocks(body)

    def conv(layer):
        acc = None
        for k, (r, c) in enumerate(OFFSETS):
            term = dot(tap(pads, r, c), mat(CONV_AT[layer] + k))
            acc = term if acc is None else acc + term
        return acc


    pump("h0")
    ion = weights_small()
    w_in = ion[0:16].astype(BF16)
    w_out = ion[16:32].astype(BF16)
    for n in range(IMGS):
        h[0, n * POS : (n + 1) * POS, :] = dot(begin[16 * n : 16 * n + 16], w_in, 0, 0)

    def residual(layer, slot, src, dst):
        pump(f"n{slot}")
        norm_forward(h.at[src], slot, True, slot)
        pump(f"c{2 * layer}")
        added = dot(feats, mat(TIME_AT[layer]))
        got = conv(2 * layer)
        for n in range(IMGS):
            c1s[layer, n * POS : (n + 1) * POS, :] = got[n * POS : (n + 1) * POS] + added[n : n + 1]
        pump(f"n{slot + 1}")
        norm_forward(c1s.at[layer], slot + 1, True, slot + 1)
        pump(f"c{2 * layer + 1}")
        h[dst] = h[src] + conv(2 * layer + 1)

    residual(0, 0, 0, 1)
    pump("n2")
    norm_forward(h.at[1], 2, False, 2)
    pump("qkv")
    normal = acts[2]
    for j in range(3):
        qkv[j] = dot(normal, mat(ATTN_AT + j)).astype(BF16)
    scale = HD ** (-0.5)

    def head_mask(hh):
        return lax.broadcasted_iota(jnp.int32, (POS, CH), 1) // HD == hh

    for n in range(IMGS):
        rows = slice(n * POS, (n + 1) * POS)
        pump(f"at{n}")
        tmp[...] = jnp.zeros_like(tmp)

        def head(hh, c):
            mask = head_mask(hh)
            q = jnp.where(mask, qkv[0, rows, :].astype(F32), 0.0).astype(BF16)
            scores = dot(q, qkv[1, rows, :], 1, 1) * scale
            e = jnp.exp(scores - jnp.max(scores, axis=1, keepdims=True))
            p = e / jnp.sum(e, axis=1, keepdims=True)
            probs[n, hh] = p
            o = dot(p.astype(BF16), qkv[2, rows, :])
            tmp[...] = jnp.where(mask, o, tmp[...])
            return c

        lax.fori_loop(0, HEADS, head, 0, unroll=HEADS)
        mixed[rows, :] = tmp[...].astype(BF16)
    pump("ao")
    h[2] = h[1] + dot(mixed[...], mat(ATTN_AT + 3), 1, 1)
    residual(1, 3, 2, 3)
    pump("n5")
    norm_forward(h.at[3], 5, False, 5)
    pump("head")

    dion_ref[...] = jnp.zeros_like(dion_ref)
    loss = jnp.zeros((), F32)
    for n in range(IMGS):
        rows = slice(n * POS, (n + 1) * POS)
        last = acts[5, rows, :]
        pred = dot(w_out, last, 1, 1)
        error = pred - goal[16 * n : 16 * n + 16, :]
        loss = loss + jnp.sum(error * error)
        low = (error * (step_scale * active)).astype(BF16)
        dion_ref[16:32, :] += dot(low, last)
        flow[rows, :] = dot(low, w_out, 0, 0)
    lane = lax.broadcasted_iota(jnp.int32, (8, 128), 1)
    scal_ref[...] = jnp.where(lane == 0, loss * active, jnp.where(lane == 1, plan_cost, 0.0))

    def norm_backward(field, slot, up, finish):
        g, b = gain(slot), bias(slot)
        zero = jnp.zeros((8, CH), F32)

        def fold(v):
            return v.reshape(ROWS // 8, 8, CH).sum(axis=0)

        dbs, dgs = [], []
        for n in range(IMGS):
            mean = stats[slot, n : n + 1]
            rstd = stats[slot, 8 + n : 9 + n]

            def step(at, c):
                rows = pl.ds(n * POS + at, ROWS)
                hat = (field[rows, :] - mean) * rstd
                dz = up[rows, :]
                if slot != 2:
                    y = hat * g + b
                    s = 1.0 / (1.0 + jnp.exp(-y))
                    dz = dz * (s * (1.0 + y * (1.0 - s)))
                    up[rows, :] = dz
                return (c[0] + fold(dz), c[1] + fold(dz * hat))

            db, dg = for_blocks(step, (zero, zero))
            dbs.append(jnp.sum(db, axis=0, keepdims=True))
            dgs.append(jnp.sum(dg, axis=0, keepdims=True))
        dion_ref[32 + 2 * slot : 33 + 2 * slot, :] = dgs[0] + dgs[1]
        dion_ref[33 + 2 * slot : 34 + 2 * slot, :] = dbs[0] + dbs[1]
        sums = group_sum(rows8(*[v * g for v in dbs + dgs])) * (1.0 / (POS * (CH // GROUPS)))
        for n in range(IMGS):
            mean = stats[slot, n : n + 1]
            rstd = stats[slot, 8 + n : 9 + n]
            m1 = sums[n : n + 1]
            m2 = sums[IMGS + n : IMGS + n + 1]

            def step(at, c):
                rows = pl.ds(n * POS + at, ROWS)
                hat = (field[rows, :] - mean) * rstd
                finish(n, at, rstd * (up[rows, :] * g - m1 - hat * m2))
                return c

            for_blocks(step, 0)

    def conv_backward(layer, keep):
        turned = acts[keep].T
        pump(f"w{layer}a")
        for k, (r, c) in enumerate(OFFSETS):
            put(CONV_AT[layer] + k, dot(turned, tap(pads, -r, -c)))
            if CONV_AT[layer] + k + 1 in SPLITS:
                pump(f"w{layer}b")
        pump(f"d{layer}")
        acc = None
        for k, (r, c) in enumerate(OFFSETS):
            term = dot(tap(pads, -r, -c), mat(CONV_AT[layer] + k), 1, 1)
            acc = term if acc is None else acc + term
        smallf[...] = acc

    def add_flow(shifted):
        def finish(n, at, dx):
            rows = pl.ds(n * POS + at, ROWS)
            total = flow[rows, :] + dx
            flow[rows, :] = total
            if shifted:
                put_shifts(pads, n, at, total)

        return finish

    def set_flow(n, at, dx):
        rows = pl.ds(n * POS + at, ROWS)
        flow[rows, :] = dx
        put_shifts(pads, n, at, dx)

    def only_shifts(n, at, dx):
        put_shifts(pads, n, at, dx)

    def residual_backward(layer, slot, src, last_one):
        conv_backward(2 * layer + 1, slot + 1)
        pump(f"b{slot + 1}")
        norm_backward(c1s.at[layer], slot + 1, smallf, only_shifts)
        sums = []
        for n in range(IMGS):
            low = pads[1, n, PAD : PAD + POS, :].astype(F32)
            sums.append(jnp.sum(low, axis=0, keepdims=True))
        one, two, three = split3(rows8(*sums))
        stack = jnp.concatenate([v.astype(F32) for v in (one, two, three)], axis=0).astype(BF16)
        feats3 = jnp.concatenate([feats.astype(F32)] * 3, axis=0).astype(BF16)
        put(TIME_AT[layer], dot(feats3, stack, 0, 0))
        conv_backward(2 * layer, slot)
        pump(f"b{slot}")
        norm_backward(h.at[src], slot, smallf, add_flow(False))

    pump("b5")
    norm_backward(h.at[3], 5, flow, set_flow)
    residual_backward(1, 3, 2, False)

    pump("do")
    dy = flow[...].astype(BF16)
    put(ATTN_AT + 3, dot(dy.T, mixed[...]))
    dqkv[3] = dot(dy, mat(ATTN_AT + 3)).astype(BF16)
    for n in range(IMGS):
        rows = slice(n * POS, (n + 1) * POS)
        pump(f"bt{n}")
        for j in range(3):
            smallf[j % 2 * POS : j % 2 * POS + POS, :] = jnp.zeros((POS, CH), F32)
        tmp[...] = jnp.zeros_like(tmp)

        def head(hh, c):
            mask = head_mask(hh)
            do = jnp.where(mask, dqkv[3, rows, :].astype(F32), 0.0).astype(BF16)
            q = jnp.where(mask, qkv[0, rows, :].astype(F32), 0.0).astype(BF16)
            p = probs[n, hh]
            dp = dot(do, qkv[2, rows, :], 1, 1)
            ds = (p * (dp - jnp.sum(p * dp, axis=1, keepdims=True))).astype(BF16)
            tmp[...] = jnp.where(mask, dot(ds, qkv[1, rows, :]), tmp[...])
            smallf[0:POS, :] += dot(ds, q, 0, 0)
            smallf[POS:, :] += dot(p.astype(BF16), do, 0, 0)
            return c

        lax.fori_loop(0, HEADS, head, 0, unroll=HEADS)
        dqkv[0, rows, :] = (tmp[...] * scale).astype(BF16)
        dqkv[1, rows, :] = (smallf[0:POS, :] * scale).astype(BF16)
        dqkv[2, rows, :] = smallf[POS:, :].astype(BF16)
    pump("proj")
    turned = acts[2].T
    acc = None
    for j in range(3):
        put(ATTN_AT + j, dot(turned, dqkv[j]))
        term = dot(dqkv[j], mat(ATTN_AT + j), 1, 1)
        acc = term if acc is None else acc + term
    smallf[...] = acc
    pump("b2")
    norm_backward(h.at[1], 2, smallf, add_flow(True))
    residual_backward(0, 0, 0, True)
    pump("win")
    for n in range(IMGS):
        rows = slice(n * POS, (n + 1) * POS)
        dion_ref[0:16, :] += dot(begin[16 * n : 16 * n + 16], flow[rows, :].astype(BF16))


def work_space():
    return [
        pltpu.VMEM((4, SPOTS, CH), F32),
        pltpu.VMEM((SPOTS, CH), F32),
        pltpu.VMEM((2, SPOTS, CH), F32),
        pltpu.VMEM((3, IMGS, POS + 2 * PAD, CH), BF16),
        pltpu.VMEM((6, SPOTS, CH), BF16),
        pltpu.VMEM((6, 16, CH), F32),
        pltpu.VMEM((16 * IMGS, POS), F32),
        pltpu.VMEM((16 * IMGS, POS), F32),
        pltpu.VMEM((3, SPOTS, CH), BF16),
        pltpu.VMEM((IMGS, HEADS, POS, POS), F32),
        pltpu.VMEM((SPOTS, CH), BF16),
        pltpu.VMEM((POS, CH), F32),
        pltpu.VMEM((SPOTS, CH), F32),
        pltpu.VMEM((4, SPOTS, CH), BF16),
    ]


def local_kernel(x_ref, z_ref, mine_ref, when_ref, feat_ref, flag_ref, mats, ion_ref, dmats, dion_ref, scal_ref, *work):
    def put(m, value):
        dmats[m] = value

    train(
        x_ref[...], z_ref[...], mine_ref[...], when_ref[0:IMGS, 0:1], feat_ref[...].astype(BF16),
        flag_ref[0, 0], flag_ref[0, 1],
        lambda: ion_ref[...].T, lambda m: mats[m], put, lambda name: None,
        dion_ref, scal_ref, *work,
    )


def local_network(x, z, mine, when, feat, flag, mats, ion):
    whole = pl.BlockSpec(memory_space=pltpu.VMEM)
    return pl.pallas_call(
        local_kernel,
        out_shape=(
            jax.ShapeDtypeStruct((MATS, CH, CH), F32),
            jax.ShapeDtypeStruct((48, CH), F32),
            jax.ShapeDtypeStruct((8, 128), F32),
        ),
        in_specs=[whole] * 5 + [pl.BlockSpec(memory_space=pltpu.SMEM)] + [whole] * 2,
        out_specs=(whole, whole, whole),
        scratch_shapes=work_space(),
        compiler_params=pltpu.CompilerParams(vmem_limit_bytes=56 * 2**20),
    )(x, z, mine, when, feat, flag, mats, ion)


Z, Y, X, C = 4, 2, 2, 2
DEVICES = Z * Y * X * C
PLANE = DEVICES // Z


def fused_kernel(
    micro, batch,
    order_ref, when_ref, images_ref, noises_ref, freq_ref, conv_ref, time_ref, attn_ref, io_ref, norm_ref,
    grads_ref, gion_ref, total_ref,
    mats, dmats, other, give, land, ottmp, ot_ref, otbuf, otwide, xz, ionbuf, dion, diont, ionr, ions, ionq, scal, scalr,
    s1q, s1r, s2q, s2r, zq, zr, expo, kept, gother,
    ot_s, ot_r, ion_s, ion_r, g_s, g_r, r_s, r_r, d_s, d_r, n_s, n_r,
    *work,
):
    dp = lax.axis_index("dp")
    mp = lax.axis_index("mp")
    z, y, x, c = dp // Y, dp % Y, mp // C, mp % C
    flat = mp * (Z * Y) + dp

    def place(z_, y_, x_, c_):
        return (z_ * Y + y_, x_ * C + c_)

    def from_flat(f):
        return (f % (Z * Y), f // (Z * Y))

    sibling = place(z, y, x, 1 - c)
    first = place(z, y * c + (1 - y) * (1 - c), x * (1 - c) + (1 - x) * c, c)
    second = place(z, (1 - y) * c + y * (1 - c), (1 - x) * (1 - c) + x * c, c)

    def remote(src, dst, send, recv, where):
        return pltpu.make_async_remote_copy(
            src_ref=src, dst_ref=dst, send_sem=send, recv_sem=recv, device_id=where, device_id_type=MESH
        )

    barrier = pltpu.get_barrier_semaphore()

    def greet(j, carry):
        pl.semaphore_signal(
            barrier, inc=1, device_id=from_flat((flat + j) % DEVICES), device_id_type=MESH
        )
        return carry

    lax.fori_loop(1, DEVICES, greet, 0)

    def wide(v):
        v = v.astype(BF16).astype(F32)
        none = jnp.zeros_like(v)
        return jnp.where(c == 0, jnp.concatenate([v, none], axis=1), jnp.concatenate([none, v], axis=1)).astype(BF16)

    def pack(m, whole):
        mats[m, x, z, y, c] = wide(jnp.where(c == 0, whole[0:16], whole[16:32]))
        give[m] = wide(jnp.where(c == 0, whole[16:32], whole[0:16]))

    for layer, at in enumerate(CONV_AT):

        def pack_step(k, carry):
            pack(at + k, conv_ref[layer, k])
            return carry

        lax.fori_loop(0, 9, pack_step, 0)
    for layer, at in enumerate(TIME_AT):
        pack(at, time_ref[layer])
    for j in range(4):
        pack(ATTN_AT + j, attn_ref[:, j, :])

    turn = mp - (mp // micro) * (mp - micro + 1)
    row = lax.broadcasted_iota(jnp.int32, (8, images_ref.shape[0]), 0)
    column = lax.broadcasted_iota(jnp.int32, (8, images_ref.shape[0]), 1)
    pick = jnp.zeros(row.shape, F32)
    for n in range(IMGS):
        pick = jnp.where((row == n) & (column == order_ref[turn * IMGS + n]), 1.0, pick)
    own_x = dot(pick.astype(BF16), images_ref[...])
    own_z = noises_ref[turn].astype(F32)
    lines = SUB * POS // 128
    for k in range(lines):
        ottmp[2 * IMGS * k : 2 * IMGS * k + IMGS, :] = own_x[0:IMGS, 128 * k : 128 * k + 128]
        ottmp[2 * IMGS * k + IMGS : 2 * IMGS * (k + 1), :] = own_z[:, 128 * k : 128 * k + 128]
    ot_ref[...] = ottmp[...].astype(BF16)
    io = io_ref[...].reshape(1, io_ref.shape[0])
    norm = norm_ref[...].reshape(1, norm_ref.shape[0])
    zero_row = jnp.zeros((1, 128), F32)
    packed = []
    for r in range(8):
        gap = zero_row[:, 0 : 16 - SUB]
        at = 2 * SUB * r
        packed.append(
            jnp.concatenate(
                [io[:, at : at + SUB], gap, io[:, at + SUB : at + 2 * SUB], gap,
                 norm[:, SUB * r : SUB * r + SUB], zero_row[:, 0 : 128 - 32 - SUB]], axis=1
            )
        )
    ionbuf[x, c, z, y] = jnp.concatenate(packed, axis=0).astype(BF16).astype(F32)
    pl.semaphore_wait(barrier, DEVICES - 1)

    zero_copy = remote(give, land, g_s.at[0, 0], g_r.at[0, 0], sibling)
    def ot_copy(j):
        there = (dp + j) % (Z * Y)
        return remote(ot_ref, otbuf.at[dp], ot_s.at[j], ot_r.at[j], (there, mp))

    def ion_z(j):
        part = ionbuf.at[x, c, z, y]
        return remote(part, part, ion_s.at[j], ion_r.at[j], place((z + j) % Z, y, x, c))

    def ion_u(core):
        part = ionbuf.at[x, c, :, y]
        return remote(part, part, ion_s.at[4], ion_r.at[4], first)

    def ion_v(core):
        part = ionbuf.at[x, 0] if core == 0 else ionbuf.at[:, 1, :, y]
        return remote(part, part, ion_s.at[5], ion_r.at[5], second)

    def ion_c(core):
        part = ionbuf.at[:, c]
        return remote(part, part, ion_s.at[6], ion_r.at[6], sibling)

    def merge(m, carry):
        mats[m, x, z, y, c] = mats[m, x, z, y, c] + land[m]
        return carry

    def span(i):
        return pl.ds(CHUNKS[i][0], CHUNKS[i][1])

    def z_copy(i, j):
        part = mats.at[span(i), x, z, y, c]
        return remote(part, part, g_s.at[i + 1, j], g_r.at[i + 1, j], place((z + j) % Z, y, x, c))

    def u_copy(i):
        part = mats.at[span(i), x, :, y, c]
        return remote(part, part, g_s.at[i + 1, 4], g_r.at[i + 1, 4], first)

    def v_copy(i, core):
        part = mats.at[span(i), x, :, :, 0] if core == 0 else mats.at[span(i), :, :, y, 1]
        return remote(part, part, g_s.at[i + 1, 5], g_r.at[i + 1, 5], second)

    def e_copy(i, j):
        part = mats.at[span(i), :, z, :, c]
        return remote(part, part, g_s.at[i + 1, j], g_r.at[i + 1, j], place((z + j) % Z, y, x, c))

    def a_copy(i):
        part = mats.at[span(i), x, z, y, c]
        return remote(part, part, g_s.at[i + 1, 4], g_r.at[i + 1, 4], first)

    def b_copy(i, core):
        part = mats.at[span(i), x, z, :, 0] if core == 0 else mats.at[span(i), :, z, y, 1]
        return remote(part, part, g_s.at[i + 1, 5], g_r.at[i + 1, 5], second)

    def c_copy(i):
        part = mats.at[span(i), :, :, :, c]
        return remote(part, part, g_s.at[i + 1, 6], g_r.at[i + 1, 6], sibling)

    def on_core(act):
        for core in range(C):
            pl.when(c == core)(functools.partial(act, core))

    def start_all(copies):
        for copy in copies:
            copy.start()

    def wait_all(copies):
        for copy in copies:
            copy.wait()

    peers = range(1, Z)

    def gather_step(kind, i):
        if kind == "A":
            a_copy(i).start()
        elif kind == "B":
            a_copy(i).wait()
            on_core(lambda core: b_copy(i, core).start())
        elif kind == "E":
            on_core(lambda core: b_copy(i, core).wait())
            start_all(e_copy(i, j) for j in peers)
        elif kind == "Z":
            start_all(z_copy(i, j) for j in peers)
        elif kind == "U":
            wait_all(z_copy(i, j) for j in peers)
            u_copy(i).start()
        elif kind == "V":
            u_copy(i).wait()
            on_core(lambda core: v_copy(i, core).start())
        elif kind == "C":
            if i in EARLY:
                wait_all(e_copy(i, j) for j in peers)
            else:
                on_core(lambda core: v_copy(i, core).wait())
            c_copy(i).start()
        elif kind == "W":
            c_copy(i).wait()

    def other_step(kind):
        if kind == "zero":
            zero_copy.start()
        elif kind == "merge":
            zero_copy.wait()
            lax.fori_loop(0, MATS, merge, 0, unroll=6)
        elif kind == "ot":
            start_all(ot_copy(j) for j in range(1, Z * Y))
            otbuf[dp] = ot_ref[...]
        elif kind == "otw":
            wait_all(ot_copy(j) for j in range(1, Z * Y))
        elif kind == "iz":
            start_all(ion_z(j) for j in peers)
        elif kind == "iu":
            wait_all(ion_z(j) for j in peers)
            ion_u(0).start()
        elif kind == "iv":
            ion_u(0).wait()
            on_core(lambda core: ion_v(core).start())
        elif kind == "ic":
            on_core(lambda core: ion_v(core).wait())
            ion_c(0).start()
        elif kind == "iw":
            ion_c(0).wait()
        elif kind == "da":
            wait_all(dion_copy(j) for j in range(1, X * C))
            ionr[mp] = diont[mp]
            ions[...] = ionr[0] + ionr[1] + ionr[2] + ionr[3]
            start_all(dion_again(j) for j in range(1, Z * Y))
            ionq[dp] = ions[dp]
        elif kind == "db":
            wait_all(dion_again(j) for j in range(1, Z * Y))

    def do(steps):
        for kind in steps:
            if kind[1:].isdigit():
                i = int(kind[1:])
                if kind[0] in "RSTYXF":
                    reduce_step(kind[0], i)
                else:
                    gather_step(kind[0], i)
            else:
                other_step(kind)

    def pump(name):
        do(PLAN.get(name, ()))

    pump("start")
    rows = ot_ref.shape[0]
    for j in range(Z * Y):
        otwide[pl.ds(j * rows, rows), :] = otbuf[j].astype(F32)
    for r in range(2 * IMGS):
        for k in range(lines):
            xz[r // IMGS, (r % IMGS) * Z * Y : (r % IMGS + 1) * Z * Y, k * 128 : (k + 1) * 128] = otwide[
                pl.ds(k * 2 * IMGS + r, Z * Y, stride=rows), :
            ]
    spot = lax.broadcasted_iota(jnp.int32, (8, batch), 0)
    column = lax.broadcasted_iota(jnp.int32, (8, batch), 1)
    mine = jnp.where((column == spot * (Z * Y) + dp) & (spot < IMGS), 1.0, 0.0)
    active = jnp.where(mp < micro, 1.0, 0.0)

    def mat(m):
        return jnp.concatenate([mats[m, k].reshape(CH, 128) for k in range(X)], axis=1)

    def put(m, value):
        for k in range(X):
            dmats[m, k] = value[:, 128 * k : 128 * k + 128].reshape(Z, Y, C, 16, 128)

    mine_a = x * (1 - c) + y * c
    mine_b = y * (1 - c) + x * c

    def xy(a, b):
        return a * (1 - c) + b * c, b * (1 - c) + a * c

    def r_copy(i):
        return remote(
            dmats.at[span(i), :, :, :, 1 - c], other.at[span(i)], r_s.at[i, 0], r_r.at[i, 0], sibling
        )

    def base(i, per):
        return CHUNKS[i][0] * per + i

    def one_copy(i):
        part = pl.ds(base(i, 8), CHUNKS[i][1] * 8 + 1)
        return remote(s1q.at[part], s1r.at[part], r_s.at[i, 1], r_r.at[i, 1], second)

    def two_copy(i):
        part = pl.ds(base(i, 4), CHUNKS[i][1] * 4 + 1)
        return remote(s2q.at[part], s2r.at[part], r_s.at[i, 2], r_r.at[i, 2], first)

    def three_copy(i, j):
        part = pl.ds(base(i, 1), CHUNKS[i][1] + 1)
        return remote(
            zq.at[j - 1, part], zr.at[j - 1, part], r_s.at[i, 2 + j], r_r.at[i, 2 + j], place((z + j) % Z, y, x, c)
        )

    def four_copy(i):
        return remote(kept.at[span(i)], gother.at[span(i)], r_s.at[i, 6], r_r.at[i, 6], sibling)

    def exponent(tiles):
        top = jnp.max(jnp.abs(tiles[0]), axis=0, keepdims=True)
        for t in tiles[1:]:
            top = jnp.maximum(top, jnp.max(jnp.abs(t), axis=0, keepdims=True))
        return jnp.floor(jnp.log2(jnp.maximum(top, 1e-30))) + 1.0

    def coded(tile, power):
        return jnp.round(tile * (LEVELS * jnp.exp2(-power))).astype(jnp.int32).astype(jnp.int16)

    def decoded(tile, unit):
        return tile.astype(jnp.int32).astype(F32) * unit

    def units(ref, at, slot):
        expo[slot] = jnp.exp2(ref[at].astype(jnp.int32).astype(F32)) * (1.0 / LEVELS)

    def powers(ref, at):
        ref[at] = expo[0].astype(jnp.int32).astype(jnp.int16)

    def stage_one(i):
        r_copy(i).wait()
        first_m, count = CHUNKS[i]
        start = base(i, 8)

        def step(k, carry):
            m = first_m + k
            tiles = []
            for b in range(2):
                x_, y_ = xy(1 - mine_a, b)
                for zz in range(Z):
                    tiles.append(dmats[m, x_, zz, y_, c] + other[m, x_, zz, y_])
            power = exponent(tiles)
            expo[0, pl.ds(k, 1), :] = power
            for t, tile in enumerate(tiles):
                s1q[start + k * 8 + t] = coded(tile, power)
            return carry

        lax.fori_loop(0, count, step, 0, unroll=True)
        powers(s1q, start + count * 8)
        one_copy(i).start()

    def stage_two(i):
        one_copy(i).wait()
        first_m, count = CHUNKS[i]
        start, start_one = base(i, 4), base(i, 8)
        units(s1r, start_one + count * 8, 1)

        def step(k, carry):
            m = first_m + k
            unit = expo[1, pl.ds(k, 1), :]
            x_, y_ = xy(mine_a, 1 - mine_b)
            tiles = []
            for zz in range(Z):
                got = decoded(s1r[start_one + k * 8 + (1 - mine_b) * 4 + zz], unit)
                tiles.append(dmats[m, x_, zz, y_, c] + other[m, x_, zz, y_] + got)
            power = exponent(tiles)
            expo[0, pl.ds(k, 1), :] = power
            for t, tile in enumerate(tiles):
                s2q[start + k * 4 + t] = coded(tile, power)
            return carry

        lax.fori_loop(0, count, step, 0, unroll=True)
        powers(s2q, start + count * 4)
        two_copy(i).start()

    def stage_three(i):
        two_copy(i).wait()
        first_m, count = CHUNKS[i]
        start, start_one, start_two = base(i, 1), base(i, 8), base(i, 4)
        units(s1r, start_one + count * 8, 1)
        units(s2r, start_two + count * 4, 2)

        def step(k, carry):
            m = first_m + k
            unit_one = expo[1, pl.ds(k, 1), :]
            unit_two = expo[2, pl.ds(k, 1), :]

            def tile(zz):
                return (
                    dmats[m, x, zz, y, c]
                    + other[m, x, zz, y]
                    + decoded(s1r[start_one + k * 8 + mine_b * 4 + zz], unit_one)
                    + decoded(s2r[start_two + k * 4 + zz], unit_two)
                )

            tiles = [tile((z + j) % Z) for j in range(1, Z)]
            power = exponent(tiles)
            expo[0, pl.ds(k, 1), :] = power
            for j in range(1, Z):
                zq[j - 1, start + k] = coded(tiles[j - 1], power)
            kept[m] = tile(z)
            return carry

        lax.fori_loop(0, count, step, 0, unroll=True)
        for j in range(1, Z):
            powers(zq.at[j - 1], start + count)
        for j in range(1, Z):
            three_copy(i, j).start()

    def stage_four(i):
        for j in range(1, Z):
            three_copy(i, j).wait()
        first_m, count = CHUNKS[i]
        start = base(i, 1)
        for j in range(1, Z):
            units(zr.at[j - 1], start + count, j)

        def step(k, carry):
            m = first_m + k
            total = kept[m]
            for j in range(1, Z):
                total = total + decoded(zr[j - 1, start + k], expo[j, pl.ds(k, 1), :])
            kept[m] = total
            return carry + total * total

        square = lax.fori_loop(0, count, step, jnp.zeros((16, 128), F32), unroll=True)
        four_copy(i).start()
        return square

    squares = []

    def reduce_step(kind, i):
        if kind == "R":
            r_copy(i).start()
        elif kind == "S":
            stage_one(i)
        elif kind == "T":
            stage_two(i)
        elif kind == "Y":
            stage_three(i)
        elif kind == "X":
            squares.append(stage_four(i))
        else:
            finish(i)

    def finish(i):
        four_copy(i).wait()

        def step(k, carry):
            m = CHUNKS[i][0] + k
            for half in range(C):
                tile = jnp.where(c == half, kept[m], gother[m])
                grads_ref[m, half * 16 : half * 16 + 16, :] = jnp.where(c == 0, tile[:, 0:64], tile[:, 64:128])
            return carry

        lax.fori_loop(0, CHUNKS[i][1], step, 0, unroll=True)

    seat = lax.broadcasted_iota(jnp.int32, (8, 1), 0)
    times = jnp.zeros((8, 1), F32)
    for n in range(IMGS):
        index = when_ref[pl.ds(turn, 1), n : n + 1]
        times = jnp.where(seat == n, (index + 0.5) / NT, times)
    angles = 1000.0 * times * freq_ref[...]
    feats = jnp.where(seat < IMGS, jnp.concatenate([jnp.sin(angles), jnp.cos(angles)], axis=1), 0.0).astype(BF16)
    train(
        xz[0].astype(BF16), xz[1].astype(BF16), mine, times[0:IMGS], feats, active, 2.0 / (micro * batch),
        lambda: ionbuf[...].reshape(CH, 128).T, mat, put, pump, dion, scal, *work,
    )

    diont[...] = (
        jnp.concatenate([dion[...], jnp.zeros((128 - 48, CH), F32)], axis=0).T.reshape(X * C, Z * Y, 8, 128)
    )

    def dion_copy(j):
        there = (mp + j) % (X * C)
        return remote(diont.at[there], ionr.at[mp], d_s.at[j], d_r.at[j], (dp, there))

    def dion_again(j):
        there = (dp + j) % (Z * Y)
        return remote(ions.at[there], ionq.at[dp], d_s.at[X * C + j], d_r.at[X * C + j], (there, mp))

    start_all(dion_copy(j) for j in range(1, X * C))
    pump("tail")
    small = jnp.sum(ionq[...], axis=0)
    gion_ref[...] = small
    square = small * small
    for part in squares:
        square = square + part[0:8] + part[8:16]

    loss, plan_cost = scal[0:1, 0:1], scal[0:1, 1:2]
    lane = lax.broadcasted_iota(jnp.int32, (8, 128), 1)
    line = lax.broadcasted_iota(jnp.int32, (8, 128), 0)
    tile = jnp.where(line == 7, 0.0, square) + jnp.where(line == 0, pltpu.roll(square, 1, 0), 0.0)
    tile = jnp.where((line == 7) & (lane == mp) & (mp < micro), loss, tile)
    tile = jnp.where((line == 7) & (lane == micro + mp) & (mp < micro) & (dp == 0), plan_cost, tile)
    scal[...] = tile
    spread = z * PLANE + y * (X * C) + mp
    scalr[spread] = tile

    def n_start(j, carry):
        there = (spread + j) % DEVICES
        remote(
            scal, scalr.at[spread], n_s.at[0], n_r.at[0],
            (there // PLANE * Y + there % PLANE // (X * C), there % (X * C)),
        ).start()
        return carry

    for low, high in ((2 * PLANE, DEVICES), (PLANE, 2 * PLANE), (1, PLANE)):
        lax.fori_loop(low, high, n_start, 0)
    pump("end")
    rest = pl.ds(0, DEVICES - 1)
    remote(scalr.at[rest], scalr.at[rest], n_s.at[0], n_r.at[0], sibling).wait()
    total_ref[...] = jnp.sum(scalr[...], axis=0)


def fused_network(micro, batch, order, when, images, noises, conv, time, attn, io, norm):
    whole = pl.BlockSpec(memory_space=pltpu.VMEM)
    scalar = pl.BlockSpec(memory_space=pltpu.SMEM)
    blocks = (X, Z, Y)
    rows = 2 * IMGS * SUB * POS // 128
    dma = pltpu.SemaphoreType.DMA
    count = len(CHUNKS)
    half = CH // 2
    freq = np.exp(np.float32(-math.log(10000.0)) * np.arange(half, dtype=np.float32) / np.float32(half))
    freq = jnp.asarray(freq.reshape(1, half))
    return pl.pallas_call(
        functools.partial(fused_kernel, micro, batch),
        out_shape=(
            jax.ShapeDtypeStruct((MATS, 32, 64), F32),
            jax.ShapeDtypeStruct((8, 128), F32),
            jax.ShapeDtypeStruct((8, 128), F32),
        ),
        in_specs=[scalar] + [whole] * 9,
        out_specs=(whole, whole, whole),
        scratch_shapes=[
            pltpu.VMEM((MATS,) + blocks + (C, 16, 128), BF16),
            pltpu.VMEM((MATS,) + blocks + (C, 16, 128), F32),
            pltpu.VMEM((MATS,) + blocks + (16, 128), F32),
            pltpu.VMEM((MATS, 16, 128), BF16),
            pltpu.VMEM((MATS, 16, 128), BF16),
            pltpu.VMEM((rows, 128), F32),
            pltpu.VMEM((rows, 128), BF16),
            pltpu.VMEM((Z * Y, rows, 128), BF16),
            pltpu.VMEM((Z * Y * rows, 128), F32),
            pltpu.VMEM((2, batch, SUB * POS), F32),
            pltpu.VMEM((X, C, Z, Y, 8, 128), F32),
            pltpu.VMEM((48, CH), F32),
            pltpu.VMEM((X * C, Z * Y, 8, 128), F32),
            pltpu.VMEM((X * C, Z * Y, 8, 128), F32),
            pltpu.VMEM((Z * Y, 8, 128), F32),
            pltpu.VMEM((Z * Y, 8, 128), F32),
            pltpu.VMEM((8, 128), F32),
            pltpu.VMEM((DEVICES, 8, 128), F32),
            pltpu.VMEM((MATS * 8 + count, 16, 128), jnp.int16),
            pltpu.VMEM((MATS * 8 + count, 16, 128), jnp.int16),
            pltpu.VMEM((MATS * 4 + count, 16, 128), jnp.int16),
            pltpu.VMEM((MATS * 4 + count, 16, 128), jnp.int16),
            pltpu.VMEM((Z - 1, MATS + count, 16, 128), jnp.int16),
            pltpu.VMEM((Z - 1, MATS + count, 16, 128), jnp.int16),
            pltpu.VMEM((Z, 16, 128), F32),
            pltpu.VMEM((MATS, 16, 128), F32),
            pltpu.VMEM((MATS, 16, 128), F32),
            dma((Z * Y,)), dma((Z * Y,)),
            dma((7,)), dma((7,)),
            dma((count + 1, 7)), dma((count + 1, 7)),
            dma((count, 7)), dma((count, 7)),
            dma((X * C + Z * Y,)), dma((X * C + Z * Y,)),
            dma((1,)), dma((1,)),
        ] + work_space(),
        compiler_params=pltpu.CompilerParams(
            vmem_limit_bytes=60 * 2**20, collective_id=0, has_side_effects=True
        ),
    )(order, when, images, noises, freq, conv, time, attn, io, norm)


def time_features(time_index):
    times = (time_index.astype(jnp.float32) + 0.5) / NT
    half = CH // 2
    frequency = jnp.exp(-math.log(10000.0) * jnp.arange(half, dtype=jnp.float32) / half)
    angles = 1000.0 * times[:, None] * frequency[None, :]
    return jnp.concatenate([jnp.sin(angles), jnp.cos(angles)], axis=1)


def adam_update(weight, first, second, average, gradient, rate):
    first = BETA_ONE * first + (1 - BETA_ONE) * gradient
    second = BETA_TWO * second + (1 - BETA_TWO) * gradient * gradient
    ratio = first / (1 - BETA_ONE**STEP) / (jnp.sqrt(second / (1 - BETA_TWO**STEP)) + ADAM_EPS)
    weight = weight - rate * (ratio + WEIGHT_DECAY * weight)
    average = EMA_DECAY * average + (1 - EMA_DECAY) * weight
    return (weight, first, second, average)


def adam_kernel(grads_ref, gion_ref, total_ref, *refs):
    old, new = refs[:20], refs[20:40]
    loss_ref, cost_ref, norm_ref = refs[40:]
    norm = jnp.sqrt(jnp.sum(total_ref[0:7], axis=(0, 1), keepdims=True))
    scale = CLIP_NORM / jnp.maximum(norm, CLIP_NORM)

    def update(kind, at, gradient):
        got = adam_update(*[old[5 * part + kind][at] for part in range(4)], gradient * scale, RATES[kind])
        for part in range(4):
            new[5 * part + kind][at] = got[part]

    for layer, start in enumerate(CONV_AT):
        update(1, (layer,), grads_ref[start : start + 9])
    for layer, start in enumerate(TIME_AT):
        update(2, (layer,), grads_ref[start])
    for j in range(4):
        update(3, (slice(None), j), grads_ref[ATTN_AT + j])
    tile = gion_ref[...]
    own = old[0].shape[0] // (2 * SUB)
    for kind, pieces in ((0, (0, 16)), (4, (32,))):
        flat = [tile[r : r + 1, at : at + SUB] for r in range(own) for at in pieces]
        flat = jnp.concatenate(flat, axis=1)
        got = adam_update(
            *[old[5 * part + kind][...].reshape(flat.shape) for part in range(4)], flat * scale, RATES[kind]
        )
        for part in range(4):
            new[5 * part + kind][...] = got[part].reshape(old[kind].shape)
    micro = loss_ref.shape[0]
    for m in range(micro):
        loss_ref[m] = total_ref[7, m]
        cost_ref[m] = total_ref[7, micro + m]
    norm_ref[0] = norm[0, 0]


def adam(micro, grads, gion, total, state):
    whole = pl.BlockSpec(memory_space=pltpu.VMEM)
    scalar = pl.BlockSpec(memory_space=pltpu.SMEM)

    return pl.pallas_call(
        adam_kernel,
        out_shape=tuple(jax.ShapeDtypeStruct(v.shape, F32) for v in state)
        + (jax.ShapeDtypeStruct((micro,), F32),) * 2
        + (jax.ShapeDtypeStruct((1,), F32),),
        in_specs=[whole] * (3 + len(state)),
        out_specs=(whole,) * len(state) + (scalar,) * 3,
        compiler_params=pltpu.CompilerParams(vmem_limit_bytes=60 * 2**20),
    )(grads, gion, total, *state)


def pack_mats(conv, time, attn):
    return jnp.concatenate(
        [time[0:1], conv[0], conv[1], attn.transpose(1, 0, 2), time[1:2], conv[2], conv[3]], axis=0
    )


def unpack_mats(mats):
    conv = jnp.stack([mats[at : at + 9] for at in CONV_AT])
    time = jnp.stack([mats[at] for at in TIME_AT])
    return conv, time, mats[ATTN_AT : ATTN_AT + 4].transpose(1, 0, 2)


def pack_small(io, norm):
    own = norm.shape[0] // SUB
    io = io.reshape(own, 2, SUB)
    norm = norm.reshape(own, SUB)
    gap = jnp.zeros((own, 16 - SUB), io.dtype)
    return jnp.concatenate(
        [io[:, 0], gap, io[:, 1], gap, norm, gap, jnp.zeros((own, 80), io.dtype)], axis=1
    )


def body(
    fused,
    images, noises, order, time_index, io_weight, conv_weight, time_weight, attn_weight, norm_param,
    io_first, conv_first, time_first, attn_first, norm_first,
    io_second, conv_second, time_second, attn_second, norm_second,
    io_average, conv_average, time_average, attn_average, norm_average,
):
    rank = lax.axis_index("mp")
    place = lax.axis_index("dp")
    micro, count, depth = noises.shape
    batch = count * lax.axis_size("dp")
    turn = jnp.minimum(rank, micro - 1)
    weights = (io_weight, conv_weight, time_weight, attn_weight, norm_param)
    firsts = (io_first, conv_first, time_first, attn_first, norm_first)
    seconds = (io_second, conv_second, time_second, attn_second, norm_second)
    averages = (io_average, conv_average, time_average, attn_average, norm_average)
    if fused:
        grads, gion, total = fused_network(
            micro, batch, order, time_index.astype(F32), images, noises, conv_weight, time_weight, attn_weight, io_weight, norm_param
        )
        out = adam(micro, grads, gion, total, weights + firsts + seconds + averages)
        return out[:22] + (out[22].reshape(()),)
    chosen = lax.dynamic_slice_in_dim(order, turn * count, count, 0)
    own_x = jnp.take(images, chosen, axis=0)
    own_z = lax.dynamic_index_in_dim(noises, turn, 0, keepdims=False)
    when = lax.dynamic_index_in_dim(time_index, turn, 0, keepdims=False)
    feat = jnp.pad(time_features(when).astype(BF16).astype(F32), ((0, 8 - count), (0, 0)))
    times = (when.astype(F32) + 0.5) / NT
    times = jnp.pad(jnp.broadcast_to(times[:, None], (count, 128)), ((0, 8 - count), (0, 0)))
    mats = pack_mats(conv_weight, time_weight, attn_weight).astype(BF16)
    mats = lax.all_gather(lax.all_gather(mats, "dp", axis=1, tiled=True), "mp", axis=2, tiled=True)
    ion = pack_small(io_weight, norm_param).astype(BF16)
    ion = lax.all_gather(ion, ("mp", "dp"), axis=0, tiled=True).astype(F32)
    both = lax.all_gather(jnp.stack([own_x, own_z]), "dp", axis=1, tiled=True)
    spot = jnp.arange(8)[:, None]
    mine = ((jnp.arange(batch)[None, :] == place * count + spot) & (spot < count)).astype(F32)
    active = (rank < micro).astype(F32)
    flag = jnp.stack([active, jnp.float32(2.0 / (micro * batch))]).reshape(1, 2)
    dmats, dion, scal = local_network(both[0], both[1], mine, times, feat, flag, mats, ion)
    dmats = lax.psum_scatter(dmats, "dp", scatter_dimension=1, tiled=True)
    dmats = lax.psum_scatter(dmats, "mp", scatter_dimension=2, tiled=True)
    dion = lax.psum_scatter(dion.T, ("mp", "dp"), scatter_dimension=0, tiled=True)
    hot = (jnp.arange(micro) == rank).astype(F32)
    squares = jnp.sum(dmats * dmats) + jnp.sum(dion * dion)
    total_sq, loss_sum, cost_sum = lax.psum(
        (squares, hot * scal[0, 0], jnp.where(place == 0, hot * scal[0, 1], 0.0)), ("dp", "mp")
    )
    grad_norm = jnp.sqrt(total_sq)
    scale = CLIP_NORM / jnp.maximum(grad_norm, CLIP_NORM)
    conv_grad, time_grad, attn_grad = unpack_mats(dmats)
    grads = (
        jnp.concatenate([dion[:, None, 0:SUB], dion[:, None, 16 : 16 + SUB]], axis=1).reshape(-1),
        conv_grad,
        time_grad,
        attn_grad,
        dion[:, 32 : 32 + SUB].reshape(-1),
    )
    results = [
        adam_update(weights[kind], firsts[kind], seconds[kind], averages[kind], grads[kind] * scale, RATES[kind])
        for kind in range(5)
    ]
    return tuple(results[kind][part] for part in range(4) for kind in range(5)) + (loss_sum, cost_sum, grad_norm)


def solution(mesh):
    flat = P(("mp", "dp"))
    state = (flat, P(None, None, "dp", "mp"), P(None, "dp", "mp"), P("dp", None, "mp"), flat)
    fused = mesh.shape["dp"] == Z * Y and mesh.shape["mp"] == X * C
    return jax.shard_map(
        functools.partial(body, fused),
        mesh=mesh,
        in_specs=(P("dp", None), P(None, "dp", None), P("dp"), P(None, "dp")) + state * 4,
        out_specs=state * 4 + (P(), P(), P()),
        check_vma=False,
    )
```

```python
import functools
import math

import jax
import numpy as np
import jax.numpy as jnp
from jax import lax
from jax.experimental import pallas as pl
from jax.experimental.pallas import tpu as pltpu
from jax.sharding import PartitionSpec as P

CH = 256
GROUPS = 32
HEADS = 4
HD = 64
SUB = 12
POS = 256
SIDE = 16
SINK = 10
NT = 1000
STEP = 5
MATS = 42
CONV_AT = (1, 10, 24, 33)
TIME_AT = (0, 23)
ATTN_AT = 19
CHUNKS = ((0, 5), (5, 5), (10, 5), (15, 4), (19, 4), (23, 5), (28, 5), (33, 5), (38, 4))
SPLITS = (5, 15, 28, 38)
EARLY = (4, 8)
PLAN = {
    "start": ("zero", "ot", "merge", "Z3", "A4", "Z5", "Z0", "iz", "A8", "U3", "B4", "Z2", "Z1", "U5", "Z7", "iu",
        "B8", "U0", "V3", "U2", "iv", "Z6", "U1", "V0", "otw", "E4", "U7", "U6", "V1", "ic", "C3"),
    "sink": ("V2", "E8", "C0", "W3", "V6"),
    "h0": ("V5", "iw", "C1"),
    "c0": ("C4", "V7", "W0", "C2", "W1"),
    "c1": ("C6", "W4", "W2"),
    "at0": ("C5",),
    "n3": ("C8", "W6", "C7"),
    "c2": ("W5",),
    "c3": ("W8", "W7"),
    "w3b": ("R7",),
    "d3": ("R8",),
    "w2b": ("R5", "S7"),
    "d2": ("R6",),
    "b3": ("S8",),
    "do": ("S5",),
    "bt1": ("S6",),
    "b2": ("R4", "T7"),
    "d1": ("T8", "R3", "T5", "R2", "S4"),
    "w0a": ("T6",),
    "w0b": ("S3",),
    "d0": ("R1", "Y7", "S2", "R0"),
    "b0": ("T4", "Y5", "S1", "Y6", "S0", "T3", "Y8"),
    "win": ("X7", "Y4", "T2", "T1"),
    "tail": ("X6", "Y3", "T0", "Y2", "da", "Y1", "X3", "Y0", "F6", "X4", "X5", "X1", "X2", "X8", "db", "X0"),
    "end": ("F8", "F5", "F2", "F7", "F3", "F1", "F4", "F0"),
}
LEVELS = 32000.0
MESH = pl.DeviceIdType.MESH


EPS_NORM = 1e-05
SINK_EPS = 0.01
CLIP_NORM = 1.0
BETA_ONE = 0.5
BETA_TWO = 0.5
ADAM_EPS = 1e-08
WEIGHT_DECAY = 0.01
EMA_DECAY = 0.9
RATES = (0.06, 0.01, 0.03, 0.03, 0.3)
F32 = jnp.float32
BF16 = jnp.bfloat16
ROWS = 32
PAD = SIDE
IMGS = 2
SPOTS = IMGS * POS


def dot(a, b, ca=1, cb=0):
    return lax.dot_general(a, b, (((ca,), (cb,)), ((), ())), preferred_element_type=F32)


def split3(v):
    one = v.astype(BF16)
    rest = v - one.astype(F32)
    two = rest.astype(BF16)
    three = (rest - two.astype(F32)).astype(BF16)
    return one, two, three


def group_sum(v):
    per = CH // GROUPS
    rows = lax.broadcasted_iota(jnp.int32, (CH, CH), 0) // per
    cols = lax.broadcasted_iota(jnp.int32, (CH, CH), 1) // per
    ones = jnp.where(rows == cols, 1.0, 0.0).astype(BF16)
    one, two, three = split3(v)
    got = dot(jnp.concatenate([one.astype(F32), two.astype(F32), three.astype(F32)], axis=0).astype(BF16), ones)
    n = v.shape[0]
    return got[:n] + got[n : 2 * n] + got[2 * n :]


def rows8(*rows):
    return jnp.concatenate(list(rows) + [jnp.zeros((8 - len(rows), CH), F32)], axis=0)


def for_blocks(step, init):
    return lax.fori_loop(0, POS // ROWS, lambda i, c: step(pl.multiple_of(i * ROWS, ROWS), c), init, unroll=True)


def norm_stats(field, stats, slot):
    zero = jnp.zeros((8, CH), F32)

    def fold(v):
        return v.reshape(ROWS // 8, 8, CH).sum(axis=0)

    sums = []
    for n in range(IMGS):
        acc = for_blocks(lambda at, c: c + fold(field[pl.ds(n * POS + at, ROWS), :]), zero)
        sums.append(jnp.sum(acc, axis=0, keepdims=True))
    scale = 1.0 / (POS * (CH // GROUPS))
    means = group_sum(rows8(*sums)) * scale
    sums = []
    for n in range(IMGS):
        mean = means[n : n + 1]

        def step(at, c):
            d = field[pl.ds(n * POS + at, ROWS), :] - mean
            return c + fold(d * d)

        sums.append(jnp.sum(for_blocks(step, zero), axis=0, keepdims=True))
    devs = group_sum(rows8(*sums)) * scale
    stats[slot, 0:8] = means
    stats[slot, 8:16] = lax.rsqrt(devs + EPS_NORM)


def put_shifts(pads, n, at, value):
    col = lax.broadcasted_iota(jnp.int32, value.shape, 0) % SIDE
    left = jnp.where(col == 0, 0.0, pltpu.roll(value, 1, 0))
    right = jnp.where(col == SIDE - 1, 0.0, pltpu.roll(value, value.shape[0] - 1, 0))
    rows = pl.ds(PAD + at, value.shape[0])
    pads[0, n, rows, :] = left.astype(BF16)
    pads[1, n, rows, :] = value.astype(BF16)
    pads[2, n, rows, :] = right.astype(BF16)


def tap(pads, r, c):
    return pads[c + 1, :, PAD + SIDE * r : PAD + SIDE * r + POS, :].reshape(SPOTS, CH)


OFFSETS = [(r, c) for r in (-1, 0, 1) for c in (-1, 0, 1)]


def train(
    x, z, mine, times, feats, active, step_scale, weights_small, mat, put, pump,
    dion_ref, scal_ref,
    h, flow, c1s, pads, acts, stats, start, goal, qkv, probs, mixed, tmp, smallf, dqkv,
):
    batch, depth = x.shape
    def gain(s):
        return ion[32 + 2 * s : 33 + 2 * s]

    def bias(s):
        return ion[33 + 2 * s : 34 + 2 * s]

    pump("pair")
    gram = dot(x, z, 1, 1)
    xf = x.astype(F32)
    zf = z.astype(F32)
    sq_x = jnp.sum(xf * xf, axis=1, keepdims=True)
    sq_z = jnp.sum(zf * zf, axis=1, keepdims=True)
    eye = lax.broadcasted_iota(jnp.int32, (batch, batch), 0) == lax.broadcasted_iota(jnp.int32, (batch, batch), 1)
    sq_z = jnp.sum(jnp.where(eye, sq_z, 0.0), axis=0, keepdims=True)
    cost = (sq_x + sq_z - 2.0 * gram) / depth
    affinity = 2.0 * gram / (depth * SINK_EPS)
    kern = jnp.exp(affinity - jnp.max(affinity, axis=1, keepdims=True))
    share = 1.0 / batch
    pump("sink")

    def sweep(i, c):
        left, right = c
        left = share / jnp.sum(kern * right, axis=1, keepdims=True)
        right = share / jnp.sum(left * kern, axis=0, keepdims=True)
        return left, right

    left, right = lax.fori_loop(0, SINK, sweep, (jnp.ones((batch, 1), F32), jnp.ones((1, batch), F32)))
    scaled = kern * right
    plan_cost = jnp.sum(left * scaled * cost)
    mixing = (scaled / jnp.sum(scaled, axis=1, keepdims=True)).astype(BF16)
    d = mine.astype(BF16)
    mix = dot(d, mixing).astype(BF16)
    paired = dot(mix, z)[0:IMGS]
    pixels = dot(d, x)[0:IMGS]
    inputs = ((1.0 - times) * paired + times * pixels).astype(BF16).astype(F32)
    target = pixels - paired
    start[...] = jnp.zeros_like(start)
    goal[...] = jnp.zeros_like(goal)
    for n in range(IMGS):
        for k in range(SUB):
            start[16 * n + k : 16 * n + k + 1, :] = inputs[n : n + 1, k * POS : (k + 1) * POS]
            goal[16 * n + k : 16 * n + k + 1, :] = target[n : n + 1, k * POS : (k + 1) * POS]
    begin = start[...].astype(BF16)

    for c in range(3):
        for n in range(IMGS):
            pads[c, n, 0:PAD, :] = jnp.zeros((PAD, CH), BF16)
            pads[c, n, PAD + POS :, :] = jnp.zeros((PAD, CH), BF16)

    def blocks(body):
        for n in range(IMGS):
            for_blocks(lambda at, c: (body(n, at), c)[1], 0)

    def norm_forward(field, slot, shifted, keep):
        norm_stats(field, stats, slot)
        g, b = gain(slot), bias(slot)

        def body(n, at):
            mean = stats[slot, n : n + 1]
            rstd = stats[slot, 8 + n : 9 + n]
            rows = pl.ds(n * POS + at, ROWS)
            y = (field[rows, :] - mean) * rstd * g + b
            if slot != 2:
                y = y * (1.0 / (1.0 + jnp.exp(-y)))
            acts[keep, rows, :] = y.astype(BF16)
            if shifted:
                put_shifts(pads, n, at, y)

        blocks(body)

    def conv(layer):
        acc = None
        for k, (r, c) in enumerate(OFFSETS):
            term = dot(tap(pads, r, c), mat(CONV_AT[layer] + k))
            acc = term if acc is None else acc + term
        return acc


    pump("h0")
    ion = weights_small()
    w_in = ion[0:16].astype(BF16)
    w_out = ion[16:32].astype(BF16)
    for n in range(IMGS):
        h[0, n * POS : (n + 1) * POS, :] = dot(begin[16 * n : 16 * n + 16], w_in, 0, 0)

    def residual(layer, slot, src, dst):
        pump(f"n{slot}")
        norm_forward(h.at[src], slot, True, slot)
        pump(f"c{2 * layer}")
        added = dot(feats, mat(TIME_AT[layer]))
        got = conv(2 * layer)
        for n in range(IMGS):
            c1s[layer, n * POS : (n + 1) * POS, :] = got[n * POS : (n + 1) * POS] + added[n : n + 1]
        pump(f"n{slot + 1}")
        norm_forward(c1s.at[layer], slot + 1, True, slot + 1)
        pump(f"c{2 * layer + 1}")
        h[dst] = h[src] + conv(2 * layer + 1)

    residual(0, 0, 0, 1)
    pump("n2")
    norm_forward(h.at[1], 2, False, 2)
    pump("qkv")
    normal = acts[2]
    for j in range(3):
        qkv[j] = dot(normal, mat(ATTN_AT + j)).astype(BF16)
    scale = HD ** (-0.5)

    def head_mask(hh):
        return lax.broadcasted_iota(jnp.int32, (POS, CH), 1) // HD == hh

    for n in range(IMGS):
        rows = slice(n * POS, (n + 1) * POS)
        pump(f"at{n}")
        tmp[...] = jnp.zeros_like(tmp)

        def head(hh, c):
            mask = head_mask(hh)
            q = jnp.where(mask, qkv[0, rows, :].astype(F32), 0.0).astype(BF16)
            scores = dot(q, qkv[1, rows, :], 1, 1) * scale
            e = jnp.exp(scores - jnp.max(scores, axis=1, keepdims=True))
            p = e / jnp.sum(e, axis=1, keepdims=True)
            probs[n, hh] = p
            o = dot(p.astype(BF16), qkv[2, rows, :])
            tmp[...] = jnp.where(mask, o, tmp[...])
            return c

        lax.fori_loop(0, HEADS, head, 0, unroll=HEADS)
        mixed[rows, :] = tmp[...].astype(BF16)
    pump("ao")
    h[2] = h[1] + dot(mixed[...], mat(ATTN_AT + 3), 1, 1)
    residual(1, 3, 2, 3)
    pump("n5")
    norm_forward(h.at[3], 5, False, 5)
    pump("head")

    dion_ref[...] = jnp.zeros_like(dion_ref)
    loss = jnp.zeros((), F32)
    for n in range(IMGS):
        rows = slice(n * POS, (n + 1) * POS)
        last = acts[5, rows, :]
        pred = dot(w_out, last, 1, 1)
        error = pred - goal[16 * n : 16 * n + 16, :]
        loss = loss + jnp.sum(error * error)
        low = (error * (step_scale * active)).astype(BF16)
        dion_ref[16:32, :] += dot(low, last)
        flow[rows, :] = dot(low, w_out, 0, 0)
    lane = lax.broadcasted_iota(jnp.int32, (8, 128), 1)
    scal_ref[...] = jnp.where(lane == 0, loss * active, jnp.where(lane == 1, plan_cost, 0.0))

    def norm_backward(field, slot, up, finish):
        g, b = gain(slot), bias(slot)
        zero = jnp.zeros((8, CH), F32)

        def fold(v):
            return v.reshape(ROWS // 8, 8, CH).sum(axis=0)

        dbs, dgs = [], []
        for n in range(IMGS):
            mean = stats[slot, n : n + 1]
            rstd = stats[slot, 8 + n : 9 + n]

            def step(at, c):
                rows = pl.ds(n * POS + at, ROWS)
                hat = (field[rows, :] - mean) * rstd
                dz = up[rows, :]
                if slot != 2:
                    y = hat * g + b
                    s = 1.0 / (1.0 + jnp.exp(-y))
                    dz = dz * (s * (1.0 + y * (1.0 - s)))
                    up[rows, :] = dz
                return (c[0] + fold(dz), c[1] + fold(dz * hat))

            db, dg = for_blocks(step, (zero, zero))
            dbs.append(jnp.sum(db, axis=0, keepdims=True))
            dgs.append(jnp.sum(dg, axis=0, keepdims=True))
        dion_ref[32 + 2 * slot : 33 + 2 * slot, :] = dgs[0] + dgs[1]
        dion_ref[33 + 2 * slot : 34 + 2 * slot, :] = dbs[0] + dbs[1]
        sums = group_sum(rows8(*[v * g for v in dbs + dgs])) * (1.0 / (POS * (CH // GROUPS)))
        for n in range(IMGS):
            mean = stats[slot, n : n + 1]
            rstd = stats[slot, 8 + n : 9 + n]
            m1 = sums[n : n + 1]
            m2 = sums[IMGS + n : IMGS + n + 1]

            def step(at, c):
                rows = pl.ds(n * POS + at, ROWS)
                hat = (field[rows, :] - mean) * rstd
                finish(n, at, rstd * (up[rows, :] * g - m1 - hat * m2))
                return c

            for_blocks(step, 0)

    def conv_backward(layer, keep):
        turned = acts[keep].T
        pump(f"w{layer}a")
        for k, (r, c) in enumerate(OFFSETS):
            put(CONV_AT[layer] + k, dot(turned, tap(pads, -r, -c)))
            if CONV_AT[layer] + k + 1 in SPLITS:
                pump(f"w{layer}b")
        pump(f"d{layer}")
        acc = None
        for k, (r, c) in enumerate(OFFSETS):
            term = dot(tap(pads, -r, -c), mat(CONV_AT[layer] + k), 1, 1)
            acc = term if acc is None else acc + term
        smallf[...] = acc

    def add_flow(shifted):
        def finish(n, at, dx):
            rows = pl.ds(n * POS + at, ROWS)
            total = flow[rows, :] + dx
            flow[rows, :] = total
            if shifted:
                put_shifts(pads, n, at, total)

        return finish

    def set_flow(n, at, dx):
        rows = pl.ds(n * POS + at, ROWS)
        flow[rows, :] = dx
        put_shifts(pads, n, at, dx)

    def only_shifts(n, at, dx):
        put_shifts(pads, n, at, dx)

    def residual_backward(layer, slot, src, last_one):
        conv_backward(2 * layer + 1, slot + 1)
        pump(f"b{slot + 1}")
        norm_backward(c1s.at[layer], slot + 1, smallf, only_shifts)
        sums = []
        for n in range(IMGS):
            low = pads[1, n, PAD : PAD + POS, :].astype(F32)
            sums.append(jnp.sum(low, axis=0, keepdims=True))
        one, two, three = split3(rows8(*sums))
        stack = jnp.concatenate([v.astype(F32) for v in (one, two, three)], axis=0).astype(BF16)
        feats3 = jnp.concatenate([feats.astype(F32)] * 3, axis=0).astype(BF16)
        put(TIME_AT[layer], dot(feats3, stack, 0, 0))
        conv_backward(2 * layer, slot)
        pump(f"b{slot}")
        norm_backward(h.at[src], slot, smallf, add_flow(False))

    pump("b5")
    norm_backward(h.at[3], 5, flow, set_flow)
    residual_backward(1, 3, 2, False)

    pump("do")
    dy = flow[...].astype(BF16)
    put(ATTN_AT + 3, dot(dy.T, mixed[...]))
    dqkv[3] = dot(dy, mat(ATTN_AT + 3)).astype(BF16)
    for n in range(IMGS):
        rows = slice(n * POS, (n + 1) * POS)
        pump(f"bt{n}")
        for j in range(3):
            smallf[j % 2 * POS : j % 2 * POS + POS, :] = jnp.zeros((POS, CH), F32)
        tmp[...] = jnp.zeros_like(tmp)

        def head(hh, c):
            mask = head_mask(hh)
            do = jnp.where(mask, dqkv[3, rows, :].astype(F32), 0.0).astype(BF16)
            q = jnp.where(mask, qkv[0, rows, :].astype(F32), 0.0).astype(BF16)
            p = probs[n, hh]
            dp = dot(do, qkv[2, rows, :], 1, 1)
            ds = (p * (dp - jnp.sum(p * dp, axis=1, keepdims=True))).astype(BF16)
            tmp[...] = jnp.where(mask, dot(ds, qkv[1, rows, :]), tmp[...])
            smallf[0:POS, :] += dot(ds, q, 0, 0)
            smallf[POS:, :] += dot(p.astype(BF16), do, 0, 0)
            return c

        lax.fori_loop(0, HEADS, head, 0, unroll=HEADS)
        dqkv[0, rows, :] = (tmp[...] * scale).astype(BF16)
        dqkv[1, rows, :] = (smallf[0:POS, :] * scale).astype(BF16)
        dqkv[2, rows, :] = smallf[POS:, :].astype(BF16)
    pump("proj")
    turned = acts[2].T
    acc = None
    for j in range(3):
        put(ATTN_AT + j, dot(turned, dqkv[j]))
        term = dot(dqkv[j], mat(ATTN_AT + j), 1, 1)
        acc = term if acc is None else acc + term
    smallf[...] = acc
    pump("b2")
    norm_backward(h.at[1], 2, smallf, add_flow(True))
    residual_backward(0, 0, 0, True)
    pump("win")
    for n in range(IMGS):
        rows = slice(n * POS, (n + 1) * POS)
        dion_ref[0:16, :] += dot(begin[16 * n : 16 * n + 16], flow[rows, :].astype(BF16))


def work_space():
    return [
        pltpu.VMEM((4, SPOTS, CH), F32),
        pltpu.VMEM((SPOTS, CH), F32),
        pltpu.VMEM((2, SPOTS, CH), F32),
        pltpu.VMEM((3, IMGS, POS + 2 * PAD, CH), BF16),
        pltpu.VMEM((6, SPOTS, CH), BF16),
        pltpu.VMEM((6, 16, CH), F32),
        pltpu.VMEM((16 * IMGS, POS), F32),
        pltpu.VMEM((16 * IMGS, POS), F32),
        pltpu.VMEM((3, SPOTS, CH), BF16),
        pltpu.VMEM((IMGS, HEADS, POS, POS), F32),
        pltpu.VMEM((SPOTS, CH), BF16),
        pltpu.VMEM((POS, CH), F32),
        pltpu.VMEM((SPOTS, CH), F32),
        pltpu.VMEM((4, SPOTS, CH), BF16),
    ]


def local_kernel(x_ref, z_ref, mine_ref, when_ref, feat_ref, flag_ref, mats, ion_ref, dmats, dion_ref, scal_ref, *work):
    def put(m, value):
        dmats[m] = value

    train(
        x_ref[...], z_ref[...], mine_ref[...], when_ref[0:IMGS, 0:1], feat_ref[...].astype(BF16),
        flag_ref[0, 0], flag_ref[0, 1],
        lambda: ion_ref[...].T, lambda m: mats[m], put, lambda name: None,
        dion_ref, scal_ref, *work,
    )


def local_network(x, z, mine, when, feat, flag, mats, ion):
    whole = pl.BlockSpec(memory_space=pltpu.VMEM)
    return pl.pallas_call(
        local_kernel,
        out_shape=(
            jax.ShapeDtypeStruct((MATS, CH, CH), F32),
            jax.ShapeDtypeStruct((48, CH), F32),
            jax.ShapeDtypeStruct((8, 128), F32),
        ),
        in_specs=[whole] * 5 + [pl.BlockSpec(memory_space=pltpu.SMEM)] + [whole] * 2,
        out_specs=(whole, whole, whole),
        scratch_shapes=work_space(),
        compiler_params=pltpu.CompilerParams(vmem_limit_bytes=56 * 2**20),
    )(x, z, mine, when, feat, flag, mats, ion)


Z, Y, X, C = 4, 2, 2, 2
DEVICES = Z * Y * X * C
PLANE = DEVICES // Z


def fused_kernel(
    micro, batch,
    order_ref, when_ref, images_ref, noises_ref, freq_ref, conv_ref, time_ref, attn_ref, io_ref, norm_ref,
    grads_ref, gion_ref, total_ref,
    mats, dmats, other, give, land, ottmp, ot_ref, otbuf, otwide, xz, ionbuf, dion, diont, ionr, ions, ionq, scal, scalr,
    s1q, s1r, s2q, s2r, zq, zr, expo, kept, gother,
    ot_s, ot_r, ion_s, ion_r, g_s, g_r, r_s, r_r, d_s, d_r, n_s, n_r,
    *work,
):
    dp = lax.axis_index("dp")
    mp = lax.axis_index("mp")
    z, y, x, c = dp // Y, dp % Y, mp // C, mp % C
    flat = mp * (Z * Y) + dp

    def place(z_, y_, x_, c_):
        return (z_ * Y + y_, x_ * C + c_)

    def from_flat(f):
        return (f % (Z * Y), f // (Z * Y))

    sibling = place(z, y, x, 1 - c)
    first = place(z, y * c + (1 - y) * (1 - c), x * (1 - c) + (1 - x) * c, c)
    second = place(z, (1 - y) * c + y * (1 - c), (1 - x) * (1 - c) + x * c, c)

    def remote(src, dst, send, recv, where):
        return pltpu.make_async_remote_copy(
            src_ref=src, dst_ref=dst, send_sem=send, recv_sem=recv, device_id=where, device_id_type=MESH
        )

    barrier = pltpu.get_barrier_semaphore()

    def greet(j, carry):
        pl.semaphore_signal(
            barrier, inc=1, device_id=from_flat((flat + j) % DEVICES), device_id_type=MESH
        )
        return carry

    lax.fori_loop(1, DEVICES, greet, 0, unroll=True)

    def wide(v):
        v = v.astype(BF16).astype(F32)
        none = jnp.zeros_like(v)
        return jnp.where(c == 0, jnp.concatenate([v, none], axis=1), jnp.concatenate([none, v], axis=1)).astype(BF16)

    def pack(m, whole):
        mats[m, x, z, y, c] = wide(jnp.where(c == 0, whole[0:16], whole[16:32]))
        give[m] = wide(jnp.where(c == 0, whole[16:32], whole[0:16]))

    for layer, at in enumerate(CONV_AT):

        def pack_step(k, carry):
            pack(at + k, conv_ref[layer, k])
            return carry

        lax.fori_loop(0, 9, pack_step, 0)
    for layer, at in enumerate(TIME_AT):
        pack(at, time_ref[layer])
    for j in range(4):
        pack(ATTN_AT + j, attn_ref[:, j, :])

    turn = mp - (mp // micro) * (mp - micro + 1)
    row = lax.broadcasted_iota(jnp.int32, (8, images_ref.shape[0]), 0)
    column = lax.broadcasted_iota(jnp.int32, (8, images_ref.shape[0]), 1)
    pick = jnp.zeros(row.shape, F32)
    for n in range(IMGS):
        pick = jnp.where((row == n) & (column == order_ref[turn * IMGS + n]), 1.0, pick)
    own_x = dot(pick.astype(BF16), images_ref[...])
    own_z = noises_ref[turn].astype(F32)
    lines = SUB * POS // 128
    for k in range(lines):
        ottmp[2 * IMGS * k : 2 * IMGS * k + IMGS, :] = own_x[0:IMGS, 128 * k : 128 * k + 128]
        ottmp[2 * IMGS * k + IMGS : 2 * IMGS * (k + 1), :] = own_z[:, 128 * k : 128 * k + 128]
    ot_ref[...] = ottmp[...].astype(BF16)
    io = io_ref[...].reshape(1, io_ref.shape[0])
    norm = norm_ref[...].reshape(1, norm_ref.shape[0])
    zero_row = jnp.zeros((1, 128), F32)
    packed = []
    for r in range(8):
        gap = zero_row[:, 0 : 16 - SUB]
        at = 2 * SUB * r
        packed.append(
            jnp.concatenate(
                [io[:, at : at + SUB], gap, io[:, at + SUB : at + 2 * SUB], gap,
                 norm[:, SUB * r : SUB * r + SUB], zero_row[:, 0 : 128 - 32 - SUB]], axis=1
            )
        )
    ionbuf[x, c, z, y] = jnp.concatenate(packed, axis=0).astype(BF16).astype(F32)
    pl.semaphore_wait(barrier, DEVICES - 1)

    zero_copy = remote(give, land, g_s.at[0, 0], g_r.at[0, 0], sibling)
    def ot_copy(j):
        there = (dp + j) % (Z * Y)
        return remote(ot_ref, otbuf.at[dp], ot_s.at[j], ot_r.at[j], (there, mp))

    def ion_z(j):
        part = ionbuf.at[x, c, z, y]
        return remote(part, part, ion_s.at[j], ion_r.at[j], place((z + j) % Z, y, x, c))

    def ion_u(core):
        part = ionbuf.at[x, c, :, y]
        return remote(part, part, ion_s.at[4], ion_r.at[4], first)

    def ion_v(core):
        part = ionbuf.at[x, 0] if core == 0 else ionbuf.at[:, 1, :, y]
        return remote(part, part, ion_s.at[5], ion_r.at[5], second)

    def ion_c(core):
        part = ionbuf.at[:, c]
        return remote(part, part, ion_s.at[6], ion_r.at[6], sibling)

    def merge(m, carry):
        mats[m, x, z, y, c] = mats[m, x, z, y, c] + land[m]
        return carry

    def span(i):
        return pl.ds(CHUNKS[i][0], CHUNKS[i][1])

    def z_copy(i, j):
        part = mats.at[span(i), x, z, y, c]
        return remote(part, part, g_s.at[i + 1, j], g_r.at[i + 1, j], place((z + j) % Z, y, x, c))

    def u_copy(i):
        part = mats.at[span(i), x, :, y, c]
        return remote(part, part, g_s.at[i + 1, 4], g_r.at[i + 1, 4], first)

    def v_copy(i, core):
        part = mats.at[span(i), x, :, :, 0] if core == 0 else mats.at[span(i), :, :, y, 1]
        return remote(part, part, g_s.at[i + 1, 5], g_r.at[i + 1, 5], second)

    def e_copy(i, j):
        part = mats.at[span(i), :, z, :, c]
        return remote(part, part, g_s.at[i + 1, j], g_r.at[i + 1, j], place((z + j) % Z, y, x, c))

    def a_copy(i):
        part = mats.at[span(i), x, z, y, c]
        return remote(part, part, g_s.at[i + 1, 4], g_r.at[i + 1, 4], first)

    def b_copy(i, core):
        part = mats.at[span(i), x, z, :, 0] if core == 0 else mats.at[span(i), :, z, y, 1]
        return remote(part, part, g_s.at[i + 1, 5], g_r.at[i + 1, 5], second)

    def c_copy(i):
        part = mats.at[span(i), :, :, :, c]
        return remote(part, part, g_s.at[i + 1, 6], g_r.at[i + 1, 6], sibling)

    def on_core(act):
        for core in range(C):
            pl.when(c == core)(functools.partial(act, core))

    def start_all(copies):
        for copy in copies:
            copy.start()

    def wait_all(copies):
        for copy in copies:
            copy.wait()

    peers = range(1, Z)

    def gather_step(kind, i):
        if kind == "A":
            a_copy(i).start()
        elif kind == "B":
            a_copy(i).wait()
            on_core(lambda core: b_copy(i, core).start())
        elif kind == "E":
            on_core(lambda core: b_copy(i, core).wait())
            start_all(e_copy(i, j) for j in peers)
        elif kind == "Z":
            start_all(z_copy(i, j) for j in peers)
        elif kind == "U":
            wait_all(z_copy(i, j) for j in peers)
            u_copy(i).start()
        elif kind == "V":
            u_copy(i).wait()
            on_core(lambda core: v_copy(i, core).start())
        elif kind == "C":
            if i in EARLY:
                wait_all(e_copy(i, j) for j in peers)
            else:
                on_core(lambda core: v_copy(i, core).wait())
            c_copy(i).start()
        elif kind == "W":
            c_copy(i).wait()

    def other_step(kind):
        if kind == "zero":
            zero_copy.start()
        elif kind == "merge":
            zero_copy.wait()
            lax.fori_loop(0, MATS, merge, 0, unroll=6)
        elif kind == "ot":
            start_all(ot_copy(j) for j in range(1, Z * Y))
            otbuf[dp] = ot_ref[...]
        elif kind == "otw":
            wait_all(ot_copy(j) for j in range(1, Z * Y))
        elif kind == "iz":
            start_all(ion_z(j) for j in peers)
        elif kind == "iu":
            wait_all(ion_z(j) for j in peers)
            ion_u(0).start()
        elif kind == "iv":
            ion_u(0).wait()
            on_core(lambda core: ion_v(core).start())
        elif kind == "ic":
            on_core(lambda core: ion_v(core).wait())
            ion_c(0).start()
        elif kind == "iw":
            ion_c(0).wait()
        elif kind == "da":
            wait_all(dion_copy(j) for j in range(1, X * C))
            ionr[mp] = diont[mp]
            ions[...] = ionr[0] + ionr[1] + ionr[2] + ionr[3]
            start_all(dion_again(j) for j in range(1, Z * Y))
            ionq[dp] = ions[dp]
        elif kind == "db":
            wait_all(dion_again(j) for j in range(1, Z * Y))

    def do(steps):
        for kind in steps:
            if kind[1:].isdigit():
                i = int(kind[1:])
                if kind[0] in "RSTYXF":
                    reduce_step(kind[0], i)
                else:
                    gather_step(kind[0], i)
            else:
                other_step(kind)

    def pump(name):
        do(PLAN.get(name, ()))

    pump("start")
    rows = ot_ref.shape[0]
    for j in range(Z * Y):
        otwide[pl.ds(j * rows, rows), :] = otbuf[j].astype(F32)
    for r in range(2 * IMGS):
        for k in range(lines):
            xz[r // IMGS, (r % IMGS) * Z * Y : (r % IMGS + 1) * Z * Y, k * 128 : (k + 1) * 128] = otwide[
                pl.ds(k * 2 * IMGS + r, Z * Y, stride=rows), :
            ]
    spot = lax.broadcasted_iota(jnp.int32, (8, batch), 0)
    column = lax.broadcasted_iota(jnp.int32, (8, batch), 1)
    mine = jnp.where((column == spot * (Z * Y) + dp) & (spot < IMGS), 1.0, 0.0)
    active = jnp.where(mp < micro, 1.0, 0.0)

    def mat(m):
        return jnp.concatenate([mats[m, k].reshape(CH, 128) for k in range(X)], axis=1)

    def put(m, value):
        for k in range(X):
            dmats[m, k] = value[:, 128 * k : 128 * k + 128].reshape(Z, Y, C, 16, 128)

    mine_a = x * (1 - c) + y * c
    mine_b = y * (1 - c) + x * c

    def xy(a, b):
        return a * (1 - c) + b * c, b * (1 - c) + a * c

    def r_copy(i):
        return remote(
            dmats.at[span(i), :, :, :, 1 - c], other.at[span(i)], r_s.at[i, 0], r_r.at[i, 0], sibling
        )

    def base(i, per):
        return CHUNKS[i][0] * per + i

    def one_copy(i):
        part = pl.ds(base(i, 8), CHUNKS[i][1] * 8 + 1)
        return remote(s1q.at[part], s1r.at[part], r_s.at[i, 1], r_r.at[i, 1], second)

    def two_copy(i):
        part = pl.ds(base(i, 4), CHUNKS[i][1] * 4 + 1)
        return remote(s2q.at[part], s2r.at[part], r_s.at[i, 2], r_r.at[i, 2], first)

    def three_copy(i, j):
        part = pl.ds(base(i, 1), CHUNKS[i][1] + 1)
        return remote(
            zq.at[j - 1, part], zr.at[j - 1, part], r_s.at[i, 2 + j], r_r.at[i, 2 + j], place((z + j) % Z, y, x, c)
        )

    def four_copy(i):
        return remote(kept.at[span(i)], gother.at[span(i)], r_s.at[i, 6], r_r.at[i, 6], sibling)

    def exponent(tiles):
        top = jnp.max(jnp.abs(tiles[0]), axis=0, keepdims=True)
        for t in tiles[1:]:
            top = jnp.maximum(top, jnp.max(jnp.abs(t), axis=0, keepdims=True))
        return jnp.floor(jnp.log2(jnp.maximum(top, 1e-30))) + 1.0

    def coded(tile, power):
        return jnp.round(tile * (LEVELS * jnp.exp2(-power))).astype(jnp.int32).astype(jnp.int16)

    def decoded(tile, unit):
        return tile.astype(jnp.int32).astype(F32) * unit

    def units(ref, at, slot):
        expo[slot] = jnp.exp2(ref[at].astype(jnp.int32).astype(F32)) * (1.0 / LEVELS)

    def powers(ref, at):
        ref[at] = expo[0].astype(jnp.int32).astype(jnp.int16)

    def stage_one(i):
        r_copy(i).wait()
        first_m, count = CHUNKS[i]
        start = base(i, 8)

        def step(k, carry):
            m = first_m + k
            tiles = []
            for b in range(2):
                x_, y_ = xy(1 - mine_a, b)
                for zz in range(Z):
                    tiles.append(dmats[m, x_, zz, y_, c] + other[m, x_, zz, y_])
            power = exponent(tiles)
            expo[0, pl.ds(k, 1), :] = power
            for t, tile in enumerate(tiles):
                s1q[start + k * 8 + t] = coded(tile, power)
            return carry

        lax.fori_loop(0, count, step, 0, unroll=True)
        powers(s1q, start + count * 8)
        one_copy(i).start()

    def stage_two(i):
        one_copy(i).wait()
        first_m, count = CHUNKS[i]
        start, start_one = base(i, 4), base(i, 8)
        units(s1r, start_one + count * 8, 1)

        def step(k, carry):
            m = first_m + k
            unit = expo[1, pl.ds(k, 1), :]
            x_, y_ = xy(mine_a, 1 - mine_b)
            tiles = []
            for zz in range(Z):
                got = decoded(s1r[start_one + k * 8 + (1 - mine_b) * 4 + zz], unit)
                tiles.append(dmats[m, x_, zz, y_, c] + other[m, x_, zz, y_] + got)
            power = exponent(tiles)
            expo[0, pl.ds(k, 1), :] = power
            for t, tile in enumerate(tiles):
                s2q[start + k * 4 + t] = coded(tile, power)
            return carry

        lax.fori_loop(0, count, step, 0, unroll=True)
        powers(s2q, start + count * 4)
        two_copy(i).start()

    def stage_three(i):
        two_copy(i).wait()
        first_m, count = CHUNKS[i]
        start, start_one, start_two = base(i, 1), base(i, 8), base(i, 4)
        units(s1r, start_one + count * 8, 1)
        units(s2r, start_two + count * 4, 2)

        def step(k, carry):
            m = first_m + k
            unit_one = expo[1, pl.ds(k, 1), :]
            unit_two = expo[2, pl.ds(k, 1), :]

            def tile(zz):
                return (
                    dmats[m, x, zz, y, c]
                    + other[m, x, zz, y]
                    + decoded(s1r[start_one + k * 8 + mine_b * 4 + zz], unit_one)
                    + decoded(s2r[start_two + k * 4 + zz], unit_two)
                )

            tiles = [tile((z + j) % Z) for j in range(1, Z)]
            power = exponent(tiles)
            expo[0, pl.ds(k, 1), :] = power
            for j in range(1, Z):
                zq[j - 1, start + k] = coded(tiles[j - 1], power)
            kept[m] = tile(z)
            return carry

        lax.fori_loop(0, count, step, 0, unroll=True)
        for j in range(1, Z):
            powers(zq.at[j - 1], start + count)
        for j in range(1, Z):
            three_copy(i, j).start()

    def stage_four(i):
        for j in range(1, Z):
            three_copy(i, j).wait()
        first_m, count = CHUNKS[i]
        start = base(i, 1)
        for j in range(1, Z):
            units(zr.at[j - 1], start + count, j)

        def step(k, carry):
            m = first_m + k
            total = kept[m]
            for j in range(1, Z):
                total = total + decoded(zr[j - 1, start + k], expo[j, pl.ds(k, 1), :])
            kept[m] = total
            return carry + total * total

        square = lax.fori_loop(0, count, step, jnp.zeros((16, 128), F32), unroll=True)
        four_copy(i).start()
        return square

    squares = []

    def reduce_step(kind, i):
        if kind == "R":
            r_copy(i).start()
        elif kind == "S":
            stage_one(i)
        elif kind == "T":
            stage_two(i)
        elif kind == "Y":
            stage_three(i)
        elif kind == "X":
            squares.append(stage_four(i))
        else:
            finish(i)

    def finish(i):
        four_copy(i).wait()

        def step(k, carry):
            m = CHUNKS[i][0] + k
            for half in range(C):
                tile = jnp.where(c == half, kept[m], gother[m])
                grads_ref[m, half * 16 : half * 16 + 16, :] = jnp.where(c == 0, tile[:, 0:64], tile[:, 64:128])
            return carry

        lax.fori_loop(0, CHUNKS[i][1], step, 0, unroll=True)

    seat = lax.broadcasted_iota(jnp.int32, (8, 1), 0)
    times = jnp.zeros((8, 1), F32)
    for n in range(IMGS):
        index = when_ref[pl.ds(turn, 1), n : n + 1]
        times = jnp.where(seat == n, (index + 0.5) / NT, times)
    angles = 1000.0 * times * freq_ref[...]
    feats = jnp.where(seat < IMGS, jnp.concatenate([jnp.sin(angles), jnp.cos(angles)], axis=1), 0.0).astype(BF16)
    train(
        xz[0].astype(BF16), xz[1].astype(BF16), mine, times[0:IMGS], feats, active, 2.0 / (micro * batch),
        lambda: ionbuf[...].reshape(CH, 128).T, mat, put, pump, dion, scal, *work,
    )

    diont[...] = (
        jnp.concatenate([dion[...], jnp.zeros((128 - 48, CH), F32)], axis=0).T.reshape(X * C, Z * Y, 8, 128)
    )

    def dion_copy(j):
        there = (mp + j) % (X * C)
        return remote(diont.at[there], ionr.at[mp], d_s.at[j], d_r.at[j], (dp, there))

    def dion_again(j):
        there = (dp + j) % (Z * Y)
        return remote(ions.at[there], ionq.at[dp], d_s.at[X * C + j], d_r.at[X * C + j], (there, mp))

    start_all(dion_copy(j) for j in range(1, X * C))
    pump("tail")
    small = jnp.sum(ionq[...], axis=0)
    gion_ref[...] = small
    square = small * small
    for part in squares:
        square = square + part[0:8] + part[8:16]

    loss, plan_cost = scal[0:1, 0:1], scal[0:1, 1:2]
    lane = lax.broadcasted_iota(jnp.int32, (8, 128), 1)
    line = lax.broadcasted_iota(jnp.int32, (8, 128), 0)
    tile = jnp.where(line == 7, 0.0, square) + jnp.where(line == 0, pltpu.roll(square, 1, 0), 0.0)
    tile = jnp.where((line == 7) & (lane == mp) & (mp < micro), loss, tile)
    tile = jnp.where((line == 7) & (lane == micro + mp) & (mp < micro) & (dp == 0), plan_cost, tile)
    scal[...] = tile
    spread = z * PLANE + y * (X * C) + mp
    scalr[spread] = tile

    def n_start(j, carry):
        there = (spread + j) % DEVICES
        remote(
            scal, scalr.at[spread], n_s.at[0], n_r.at[0],
            (there // PLANE * Y + there % PLANE // (X * C), there % (X * C)),
        ).start()
        return carry

    for low, high in ((2 * PLANE, DEVICES), (PLANE, 2 * PLANE), (1, PLANE)):
        lax.fori_loop(low, high, n_start, 0, unroll=True)
    pump("end")
    rest = pl.ds(0, DEVICES - 1)
    remote(scalr.at[rest], scalr.at[rest], n_s.at[0], n_r.at[0], sibling).wait()
    total_ref[...] = jnp.sum(scalr[...], axis=0)


def fused_network(micro, batch, order, when, images, noises, conv, time, attn, io, norm):
    whole = pl.BlockSpec(memory_space=pltpu.VMEM)
    scalar = pl.BlockSpec(memory_space=pltpu.SMEM)
    blocks = (X, Z, Y)
    rows = 2 * IMGS * SUB * POS // 128
    dma = pltpu.SemaphoreType.DMA
    count = len(CHUNKS)
    half = CH // 2
    freq = np.exp(np.float32(-math.log(10000.0)) * np.arange(half, dtype=np.float32) / np.float32(half))
    freq = jnp.asarray(freq.reshape(1, half))
    return pl.pallas_call(
        functools.partial(fused_kernel, micro, batch),
        out_shape=(
            jax.ShapeDtypeStruct((MATS, 32, 64), F32),
            jax.ShapeDtypeStruct((8, 128), F32),
            jax.ShapeDtypeStruct((8, 128), F32),
        ),
        in_specs=[scalar] + [whole] * 9,
        out_specs=(whole, whole, whole),
        scratch_shapes=[
            pltpu.VMEM((MATS,) + blocks + (C, 16, 128), BF16),
            pltpu.VMEM((MATS,) + blocks + (C, 16, 128), F32),
            pltpu.VMEM((MATS,) + blocks + (16, 128), F32),
            pltpu.VMEM((MATS, 16, 128), BF16),
            pltpu.VMEM((MATS, 16, 128), BF16),
            pltpu.VMEM((rows, 128), F32),
            pltpu.VMEM((rows, 128), BF16),
            pltpu.VMEM((Z * Y, rows, 128), BF16),
            pltpu.VMEM((Z * Y * rows, 128), F32),
            pltpu.VMEM((2, batch, SUB * POS), F32),
            pltpu.VMEM((X, C, Z, Y, 8, 128), F32),
            pltpu.VMEM((48, CH), F32),
            pltpu.VMEM((X * C, Z * Y, 8, 128), F32),
            pltpu.VMEM((X * C, Z * Y, 8, 128), F32),
            pltpu.VMEM((Z * Y, 8, 128), F32),
            pltpu.VMEM((Z * Y, 8, 128), F32),
            pltpu.VMEM((8, 128), F32),
            pltpu.VMEM((DEVICES, 8, 128), F32),
            pltpu.VMEM((MATS * 8 + count, 16, 128), jnp.int16),
            pltpu.VMEM((MATS * 8 + count, 16, 128), jnp.int16),
            pltpu.VMEM((MATS * 4 + count, 16, 128), jnp.int16),
            pltpu.VMEM((MATS * 4 + count, 16, 128), jnp.int16),
            pltpu.VMEM((Z - 1, MATS + count, 16, 128), jnp.int16),
            pltpu.VMEM((Z - 1, MATS + count, 16, 128), jnp.int16),
            pltpu.VMEM((Z, 16, 128), F32),
            pltpu.VMEM((MATS, 16, 128), F32),
            pltpu.VMEM((MATS, 16, 128), F32),
            dma((Z * Y,)), dma((Z * Y,)),
            dma((7,)), dma((7,)),
            dma((count + 1, 7)), dma((count + 1, 7)),
            dma((count, 7)), dma((count, 7)),
            dma((X * C + Z * Y,)), dma((X * C + Z * Y,)),
            dma((1,)), dma((1,)),
        ] + work_space(),
        compiler_params=pltpu.CompilerParams(
            vmem_limit_bytes=60 * 2**20, collective_id=0, has_side_effects=True
        ),
    )(order, when, images, noises, freq, conv, time, attn, io, norm)


def time_features(time_index):
    times = (time_index.astype(jnp.float32) + 0.5) / NT
    half = CH // 2
    frequency = jnp.exp(-math.log(10000.0) * jnp.arange(half, dtype=jnp.float32) / half)
    angles = 1000.0 * times[:, None] * frequency[None, :]
    return jnp.concatenate([jnp.sin(angles), jnp.cos(angles)], axis=1)


def adam_update(weight, first, second, average, gradient, rate):
    first = BETA_ONE * first + (1 - BETA_ONE) * gradient
    second = BETA_TWO * second + (1 - BETA_TWO) * gradient * gradient
    ratio = first / (1 - BETA_ONE**STEP) / (jnp.sqrt(second / (1 - BETA_TWO**STEP)) + ADAM_EPS)
    weight = weight - rate * (ratio + WEIGHT_DECAY * weight)
    average = EMA_DECAY * average + (1 - EMA_DECAY) * weight
    return (weight, first, second, average)


def adam_kernel(grads_ref, gion_ref, total_ref, *refs):
    old, new = refs[:20], refs[20:40]
    loss_ref, cost_ref, norm_ref = refs[40:]
    norm = jnp.sqrt(jnp.sum(total_ref[0:7], axis=(0, 1), keepdims=True))
    scale = CLIP_NORM / jnp.maximum(norm, CLIP_NORM)

    def update(kind, at, gradient):
        got = adam_update(*[old[5 * part + kind][at] for part in range(4)], gradient * scale, RATES[kind])
        for part in range(4):
            new[5 * part + kind][at] = got[part]

    for layer, start in enumerate(CONV_AT):
        update(1, (layer,), grads_ref[start : start + 9])
    for layer, start in enumerate(TIME_AT):
        update(2, (layer,), grads_ref[start])
    for j in range(4):
        update(3, (slice(None), j), grads_ref[ATTN_AT + j])
    tile = gion_ref[...]
    own = old[0].shape[0] // (2 * SUB)
    for kind, pieces in ((0, (0, 16)), (4, (32,))):
        flat = [tile[r : r + 1, at : at + SUB] for r in range(own) for at in pieces]
        flat = jnp.concatenate(flat, axis=1)
        got = adam_update(
            *[old[5 * part + kind][...].reshape(flat.shape) for part in range(4)], flat * scale, RATES[kind]
        )
        for part in range(4):
            new[5 * part + kind][...] = got[part].reshape(old[kind].shape)
    micro = loss_ref.shape[0]
    for m in range(micro):
        loss_ref[m] = total_ref[7, m]
        cost_ref[m] = total_ref[7, micro + m]
    norm_ref[0] = norm[0, 0]


def adam(micro, grads, gion, total, state):
    whole = pl.BlockSpec(memory_space=pltpu.VMEM)
    scalar = pl.BlockSpec(memory_space=pltpu.SMEM)

    return pl.pallas_call(
        adam_kernel,
        out_shape=tuple(jax.ShapeDtypeStruct(v.shape, F32) for v in state)
        + (jax.ShapeDtypeStruct((micro,), F32),) * 2
        + (jax.ShapeDtypeStruct((1,), F32),),
        in_specs=[whole] * (3 + len(state)),
        out_specs=(whole,) * len(state) + (scalar,) * 3,
        compiler_params=pltpu.CompilerParams(vmem_limit_bytes=60 * 2**20),
    )(grads, gion, total, *state)


def pack_mats(conv, time, attn):
    return jnp.concatenate(
        [time[0:1], conv[0], conv[1], attn.transpose(1, 0, 2), time[1:2], conv[2], conv[3]], axis=0
    )


def unpack_mats(mats):
    conv = jnp.stack([mats[at : at + 9] for at in CONV_AT])
    time = jnp.stack([mats[at] for at in TIME_AT])
    return conv, time, mats[ATTN_AT : ATTN_AT + 4].transpose(1, 0, 2)


def pack_small(io, norm):
    own = norm.shape[0] // SUB
    io = io.reshape(own, 2, SUB)
    norm = norm.reshape(own, SUB)
    gap = jnp.zeros((own, 16 - SUB), io.dtype)
    return jnp.concatenate(
        [io[:, 0], gap, io[:, 1], gap, norm, gap, jnp.zeros((own, 80), io.dtype)], axis=1
    )


def body(
    fused,
    images, noises, order, time_index, io_weight, conv_weight, time_weight, attn_weight, norm_param,
    io_first, conv_first, time_first, attn_first, norm_first,
    io_second, conv_second, time_second, attn_second, norm_second,
    io_average, conv_average, time_average, attn_average, norm_average,
):
    rank = lax.axis_index("mp")
    place = lax.axis_index("dp")
    micro, count, depth = noises.shape
    batch = count * lax.axis_size("dp")
    turn = jnp.minimum(rank, micro - 1)
    weights = (io_weight, conv_weight, time_weight, attn_weight, norm_param)
    firsts = (io_first, conv_first, time_first, attn_first, norm_first)
    seconds = (io_second, conv_second, time_second, attn_second, norm_second)
    averages = (io_average, conv_average, time_average, attn_average, norm_average)
    if fused:
        grads, gion, total = fused_network(
            micro, batch, order, time_index.astype(F32), images, noises, conv_weight, time_weight, attn_weight, io_weight, norm_param
        )
        out = adam(micro, grads, gion, total, weights + firsts + seconds + averages)
        return out[:22] + (out[22].reshape(()),)
    chosen = lax.dynamic_slice_in_dim(order, turn * count, count, 0)
    own_x = jnp.take(images, chosen, axis=0)
    own_z = lax.dynamic_index_in_dim(noises, turn, 0, keepdims=False)
    when = lax.dynamic_index_in_dim(time_index, turn, 0, keepdims=False)
    feat = jnp.pad(time_features(when).astype(BF16).astype(F32), ((0, 8 - count), (0, 0)))
    times = (when.astype(F32) + 0.5) / NT
    times = jnp.pad(jnp.broadcast_to(times[:, None], (count, 128)), ((0, 8 - count), (0, 0)))
    mats = pack_mats(conv_weight, time_weight, attn_weight).astype(BF16)
    mats = lax.all_gather(lax.all_gather(mats, "dp", axis=1, tiled=True), "mp", axis=2, tiled=True)
    ion = pack_small(io_weight, norm_param).astype(BF16)
    ion = lax.all_gather(ion, ("mp", "dp"), axis=0, tiled=True).astype(F32)
    both = lax.all_gather(jnp.stack([own_x, own_z]), "dp", axis=1, tiled=True)
    spot = jnp.arange(8)[:, None]
    mine = ((jnp.arange(batch)[None, :] == place * count + spot) & (spot < count)).astype(F32)
    active = (rank < micro).astype(F32)
    flag = jnp.stack([active, jnp.float32(2.0 / (micro * batch))]).reshape(1, 2)
    dmats, dion, scal = local_network(both[0], both[1], mine, times, feat, flag, mats, ion)
    dmats = lax.psum_scatter(dmats, "dp", scatter_dimension=1, tiled=True)
    dmats = lax.psum_scatter(dmats, "mp", scatter_dimension=2, tiled=True)
    dion = lax.psum_scatter(dion.T, ("mp", "dp"), scatter_dimension=0, tiled=True)
    hot = (jnp.arange(micro) == rank).astype(F32)
    squares = jnp.sum(dmats * dmats) + jnp.sum(dion * dion)
    total_sq, loss_sum, cost_sum = lax.psum(
        (squares, hot * scal[0, 0], jnp.where(place == 0, hot * scal[0, 1], 0.0)), ("dp", "mp")
    )
    grad_norm = jnp.sqrt(total_sq)
    scale = CLIP_NORM / jnp.maximum(grad_norm, CLIP_NORM)
    conv_grad, time_grad, attn_grad = unpack_mats(dmats)
    grads = (
        jnp.concatenate([dion[:, None, 0:SUB], dion[:, None, 16 : 16 + SUB]], axis=1).reshape(-1),
        conv_grad,
        time_grad,
        attn_grad,
        dion[:, 32 : 32 + SUB].reshape(-1),
    )
    results = [
        adam_update(weights[kind], firsts[kind], seconds[kind], averages[kind], grads[kind] * scale, RATES[kind])
        for kind in range(5)
    ]
    return tuple(results[kind][part] for part in range(4) for kind in range(5)) + (loss_sum, cost_sum, grad_norm)


def solution(mesh):
    flat = P(("mp", "dp"))
    state = (flat, P(None, None, "dp", "mp"), P(None, "dp", "mp"), P("dp", None, "mp"), flat)
    fused = mesh.shape["dp"] == Z * Y and mesh.shape["mp"] == X * C
    return jax.shard_map(
        functools.partial(body, fused),
        mesh=mesh,
        in_specs=(P("dp", None), P(None, "dp", None), P("dp"), P(None, "dp")) + state * 4,
        out_specs=state * 4 + (P(), P(), P()),
        check_vma=False,
    )
```
